32 devices in a mesh: groups: 2 (over y), row: 4 (over x, core), col: 4 (over z).
Axes of the slice: x: 2, y: 2, z: 4, core: 2. Of those that a mesh axis runs over, the one named last changes fastest.
Arguments:
- features: bfloat16 [4096, 128], P(('groups', 'row', 'col')), parts along dimension 0, may hold values from -6 to 6
- weight: bfloat16 [128, 256], replicated, may hold values from -0.5 to 0.5
- cotangent: bfloat16 [4096, 256], P(('groups', 'row', 'col')), parts along dimension 0, may hold values from -6 to 6
- tile_values: bfloat16 [8, 4, 8, 128, 128], P(('groups', 'row'), 'col'), parts along dimension 0, may hold values from -0.3125 to 0.3125
- tile_rows: int32 [8, 4, 8], P(('groups', 'row'), 'col'), parts along dimension 0, may hold values from 0 to 3, as said below
- tile_cols: int32 [8, 4, 8], P(('groups', 'row'), 'col'), parts along dimension 0, may hold values from 0 to 3
- tile_count: int32 [8, 4], P(('groups', 'row'), 'col'), parts along dimension 0, may hold values from 2 to 8, as said below
Outputs:
- act: bfloat16 [4096, 256], P(('groups', 'row', 'col')), parts along dimension 0
- grad_features: bfloat16 [4096, 128], P(('groups', 'row', 'col')), parts along dimension 0
- grad_weight: float32 [256, 256], P('groups'), parts along dimension 0
The draws below stay inside these ranges and needn't reach their ends.
There are 2 independent parts, one for each index of `groups`. The reference program is written for one: setup_inputs(seed, part) draws one part's arguments, and reference() takes and returns one part's arrays. A program takes and returns all parts, laid end to end along the dimension named above; an argument that names none is the same for every part. Nothing has to cross between parts.
Inputs may be any that keep to these rules, and one draw needn't show every extreme that they name: Within one grid cell the pairs (tile_rows, tile_cols) of all 8 slots are distinct. `tile_count`: some grid cell has all 8 slots live.
All inputs are finite; a program needn't handle non-finite values.
Results may differ from the reference program's by a relative error of at most 0.009.
Values may be sent and summed in bfloat16 or wider, within the bound.
No kernel may reach another device: no remote copies, remote signals or barrier semaphores. Data moves between devices by JAX's collectives and lax.ppermute only.
A program may use at most 64 MiB of HBM per device.

```python
import jax
import jax.numpy as jnp
from jax import lax

F = 128
H = 256
TILE = 128
PIECE = 1
TILES_DEV = 8
NODES = 2048
N_ROW = 4
N_COL = 4


def tile_positions(key):
    total = N_COL * PIECE * N_ROW * PIECE
    keys = jax.random.split(key, N_ROW * N_COL)

    def one_cell(cell_key):
        return jax.random.permutation(cell_key, total)[:TILES_DEV]
    positions = jax.vmap(one_cell)(keys)
    return positions.reshape(N_ROW, N_COL, TILES_DEV).astype(jnp.int32)


def draw_tile_rows(key, part):
    positions = tile_positions(key)
    return (positions // (N_ROW * PIECE)).astype(jnp.int32)


def draw_tile_cols(key, part):
    positions = tile_positions(key)
    return (positions % (N_ROW * PIECE)).astype(jnp.int32)


def draw_tile_count(key, part):
    key = jax.random.fold_in(key, 3)
    first_key, second_key = jax.random.split(key)
    counts = jax.random.randint(first_key, (N_ROW * N_COL,), TILES_DEV // 4, TILES_DEV // 2 + 1)
    chosen = jax.random.randint(second_key, (), 0, N_ROW * N_COL)
    cells = jnp.arange(N_ROW * N_COL, dtype=jnp.int32)
    counts = jnp.where(cells == chosen, TILES_DEV, counts)
    return counts.reshape(N_ROW, N_COL).astype(jnp.int32)


def levels(rng, shape, shards, smallest, high):
    loudness = 1.0
    for position, shards_of in shards:
        heights = jax.random.uniform(jax.random.fold_in(jax.random.fold_in(rng, 6), position), (shards_of,), jnp.float32, smallest / len(shards), high / len(shards))
        loudness = loudness * jnp.repeat(jnp.exp(heights), shape[position] // shards_of).reshape((-1,) + (1,) * (len(shape) - 1 - position))
    return loudness


def noise(stream_key, dims, spread, limit, cuts=(), held_as=jnp.bfloat16):
    array = spread * jax.random.normal(stream_key, dims, jnp.float32)
    if cuts:
        array = array * levels(stream_key, dims, cuts, -0.22, 0.18)
    return jnp.clip(array, -limit, limit).astype(held_as)


def setup_inputs(seed: int = 0, part: int = 0) -> dict:
    splits = jax.random.split(jax.random.key(seed), 8)
    own_keys = jax.random.split(jax.random.fold_in(splits[7], part), 8)
    features = noise(own_keys[0], (NODES, F), 1.0, 6.0, ((0, 16),))
    weight = noise(splits[1], (F, H), F ** -0.5, 0.5)
    cotangent = noise(own_keys[2], (NODES, H), 1.0, 6.0, ((0, 16),))
    tile_values = noise(own_keys[3], (N_ROW, N_COL, TILES_DEV, TILE, TILE), (3 * N_ROW * N_COL * TILE // 16) ** -0.5, 0.3125, ((0, 4), (1, 4)))
    tile_rows = draw_tile_rows(jax.random.fold_in(jax.random.fold_in(splits[7], part), 71), part)
    tile_cols = draw_tile_cols(jax.random.fold_in(jax.random.fold_in(splits[7], part), 71), part)
    tile_count = draw_tile_count(jax.random.fold_in(jax.random.fold_in(splits[7], part), 71), part)
    return {"features": features, "weight": weight, "cotangent": cotangent, "tile_values": tile_values, "tile_rows": tile_rows, "tile_cols": tile_cols, "tile_count": tile_count}


def reference(features, weight, cotangent, tile_values, tile_rows, tile_cols, tile_count):
    highest = lax.Precision.HIGHEST
    block_tiles = N_COL * PIECE
    set_tiles = N_ROW * PIECE
    cells = N_ROW * N_COL
    values = tile_values.reshape(cells, TILES_DEV, TILE, TILE)
    row_ids = tile_rows.reshape(cells, TILES_DEV)
    col_ids = tile_cols.reshape(cells, TILES_DEV)
    counts = tile_count.reshape(cells)
    slots = jnp.arange(TILES_DEV, dtype=jnp.int32)
    cell_ids = jnp.arange(cells, dtype=jnp.int32)
    grid_features = features.astype(jnp.float32).reshape(N_ROW, N_COL, PIECE, TILE, F)

    def forward(total, item):
        cell, tile_vals, row_take, col_take, count = item
        row_cell = cell // N_COL
        col_cell = cell % N_COL
        operand = lax.dynamic_index_in_dim(grid_features, col_cell, 1, keepdims=False).reshape(set_tiles, TILE, F)
        taken = operand[col_take]
        weights_live = (slots < count).astype(jnp.float32)
        product = jnp.einsum('tab,tbf->taf', tile_vals.astype(jnp.float32), taken, precision=highest)
        product = product * weights_live[:, None, None]
        partial_value = jax.ops.segment_sum(product, row_take, num_segments=block_tiles)
        return total.at[row_cell].add(partial_value), None

    start = jnp.zeros((N_ROW, block_tiles, TILE, F), jnp.float32)
    summed, _ = lax.scan(forward, start, (cell_ids, values, row_ids, col_ids, counts))
    aggregated = summed.reshape(NODES, F)
    weight_wide = weight.astype(jnp.float32)
    pre = jnp.dot(aggregated, weight_wide, precision=highest)
    act = jax.nn.silu(pre).astype(jnp.bfloat16)
    sigma = jax.nn.sigmoid(pre)
    grad_pre = cotangent.astype(jnp.float32) * sigma * (1.0 + pre * (1.0 - sigma))
    back = jnp.dot(grad_pre, weight_wide.T, precision=highest)
    grid_back = back.reshape(N_ROW, block_tiles, TILE, F)

    def backward(total, item):
        cell, tile_vals, row_take, col_take, count = item
        row_cell = cell // N_COL
        col_cell = cell % N_COL
        operand = lax.dynamic_index_in_dim(grid_back, row_cell, 0, keepdims=False)
        taken = operand[row_take]
        weights_live = (slots < count).astype(jnp.float32)
        product = jnp.einsum('tab,taf->tbf', tile_vals.astype(jnp.float32), taken, precision=highest)
        product = product * weights_live[:, None, None]
        partial_value = jax.ops.segment_sum(product, col_take, num_segments=set_tiles)
        return total.at[:, col_cell].add(partial_value.reshape(N_ROW, PIECE, TILE, F)), None

    start_back = jnp.zeros((N_ROW, N_COL, PIECE, TILE, F), jnp.float32)
    summed_back, _ = lax.scan(backward, start_back, (cell_ids, values, row_ids, col_ids, counts))
    grad_features = summed_back.reshape(NODES, F).astype(jnp.bfloat16)
    grad_weight = jnp.dot(aggregated.T, grad_pre, precision=highest) * (float(NODES) ** -0.5)
    return act, grad_features, grad_weight
```

```python
import functools

import jax
import jax.numpy as jnp
from jax import lax
from jax.experimental import pallas as pl
from jax.experimental.pallas import tpu as pltpu
from jax.sharding import PartitionSpec as P

VMEM = pl.BlockSpec(memory_space=pltpu.VMEM)
SMEM = pl.BlockSpec(memory_space=pltpu.SMEM)


def call(kernel, outs, in_specs, flops=0, bytes_accessed=0):
    return pl.pallas_call(
        kernel,
        out_shape=outs,
        in_specs=in_specs,
        out_specs=jax.tree.map(lambda _: VMEM, outs),
        compiler_params=pltpu.CompilerParams(vmem_limit_bytes=48 * 1024 * 1024),
        cost_estimate=pl.CostEstimate(
            flops=flops, bytes_accessed=bytes_accessed, transcendentals=0
        ),
    )


def gather(own, axis):
    n = lax.axis_size(axis)
    return [own] + [
        lax.ppermute(own, axis, [(s, (s - d) % n) for s in range(n)]) for d in range(1, n)
    ]


def exchange(sends, axis):
    n = lax.axis_size(axis)
    return [
        lax.ppermute(sends[d - 1], axis, [(s, (s + d) % n) for s in range(n)])
        for d in range(1, n)
    ]


def split(value):
    high = value.astype(jnp.bfloat16)
    return high, (value - high.astype(jnp.float32)).astype(jnp.bfloat16)


def dot(left, right, dims=((1,), (0,))):
    return lax.dot_general(left, right, (dims, ((), ())), preferred_element_type=jnp.float32)


def dense_kernel(n_row, n_col, piece, vals, rows, cols, count, place, near, far):
    side = vals.shape[1]
    near[...] = jnp.zeros_like(near)
    far[...] = jnp.zeros_like(far)
    my_row, my_col = place[0], place[1]

    def add(t, _):
        row, col = rows[t], cols[t]
        row = lax.rem(row // piece - my_col + n_col, n_col) * piece + lax.rem(row, piece)
        col = lax.rem(col // piece - my_row + n_row, n_row) * piece + lax.rem(col, piece)
        down = pl.ds(pl.multiple_of(row * side, side), side)
        across = pl.ds(pl.multiple_of(col * side, side), side)
        tile = vals[t]
        near[down, across] = tile
        far[across, down] = tile.T
        return 0

    lax.fori_loop(0, count[0], add, 0)


def spread_kernel(n, matrix, *refs):
    operands, own, sends = refs[:n], refs[n], refs[n + 1 :]
    rows = own.shape[0]
    stacked = jnp.concatenate([operand[...] for operand in operands], axis=0)
    product = dot(matrix[...], stacked)
    own[...] = product[:rows]
    for d, send in enumerate(sends, 1):
        send[...] = product[d * rows : (d + 1) * rows].astype(send.dtype)


def layer_kernel(own, *refs):
    *parts, weight, cotangent, act, back, term = refs
    total = own[...]
    for part in parts:
        total = total + part[...].astype(jnp.float32)
    high, low = split(total)
    pre = dot(high, weight[...]) + dot(low, weight[...])
    sigma = jax.nn.sigmoid(pre)
    act[...] = (pre * sigma).astype(act.dtype)
    grad = cotangent[...].astype(jnp.float32) * sigma * (1.0 + pre * (1.0 - sigma))
    grad_high, grad_low = split(grad)
    across = ((1,), (1,))
    back[...] = (dot(grad_high, weight[...], across) + dot(grad_low, weight[...], across)).astype(
        back.dtype
    )
    down = ((0,), (0,))
    term[...] = (
        dot(high, grad_high, down) + dot(low, grad_high, down) + dot(high, grad_low, down)
    ).astype(term.dtype)


def sum_kernel(scale, *refs):
    *parts, out = refs
    total = parts[0][...].astype(jnp.float32)
    for part in parts[1:]:
        total = total + part[...].astype(jnp.float32)
    if scale is not None:
        total = total * scale
    out[...] = total.astype(out.dtype)


def per_device(features, weight, cotangent, tile_values, tile_rows, tile_cols, tile_count):
    narrow = jnp.bfloat16
    vals = tile_values.reshape(tile_values.shape[2:])
    slots, side = vals.shape[:2]
    n_row, n_col = lax.axis_size("row"), lax.axis_size("col")
    nodes, width = features.shape
    hidden = weight.shape[1]
    down, across = n_col * nodes, n_row * nodes
    place = jnp.stack([lax.axis_index("row"), lax.axis_index("col")]).astype(jnp.int32)

    def like(shape, dtype=narrow):
        return jax.ShapeDtypeStruct(shape, dtype)

    gathered = gather(features, "row")
    near, far = call(
        functools.partial(dense_kernel, n_row, n_col, nodes // side),
        (like((down, across)), like((across, down))),
        [VMEM, SMEM, SMEM, SMEM, SMEM],
        bytes_accessed=6 * down * across,
    )(vals, tile_rows.reshape(-1), tile_cols.reshape(-1), tile_count.reshape(-1), place)

    own, *sends = call(
        functools.partial(spread_kernel, n_row),
        (like((nodes, width), jnp.float32),) + (like((nodes, width)),) * (n_col - 1),
        [VMEM] * (1 + n_row),
        flops=2 * down * across * width,
    )(near, *gathered)
    parts = exchange(sends, "col")

    act, back, term = call(
        layer_kernel,
        (like((nodes, hidden)), like((nodes, width)), like((width, hidden))),
        [VMEM] * (n_col + 2),
        flops=14 * nodes * width * hidden,
    )(own, *parts, weight, cotangent)
    spread = gather(back, "col")
    terms = gather(term, "row")

    own, *sends = call(
        functools.partial(spread_kernel, n_col),
        (like((nodes, width), jnp.float32),) + (like((nodes, width)),) * (n_row - 1),
        [VMEM] * (1 + n_col),
        flops=2 * down * across * width,
    )(far, *spread)
    parts = exchange(sends, "row")

    row_sum = call(
        functools.partial(sum_kernel, None), like((width, hidden)), [VMEM] * n_row
    )(*terms)
    terms = gather(row_sum, "col")
    grad_features = call(
        functools.partial(sum_kernel, None), like((nodes, width)), [VMEM] * n_row
    )(own, *parts)
    scale = float(nodes * n_row * n_col) ** -0.5
    grad_weight = call(
        functools.partial(sum_kernel, scale), like((width, hidden), jnp.float32), [VMEM] * n_col
    )(*terms)
    return act, grad_features, grad_weight


def solution(mesh):
    placed = (
        P(("groups", "row", "col"), None),
        P(),
        P(("groups", "row", "col"), None),
        P(("groups", "row"), "col", None, None, None),
        P(("groups", "row"), "col", None),
        P(("groups", "row"), "col", None),
        P(("groups", "row"), "col"),
    )
    return jax.shard_map(
        per_device,
        mesh=mesh,
        in_specs=placed,
        out_specs=(
            P(("groups", "row", "col"), None),
            P(("groups", "row", "col"), None),
            P("groups", None),
        ),
        check_vma=False,
    )
```

```python
import functools

import jax
import jax.numpy as jnp
from jax import lax
from jax.experimental import pallas as pl
from jax.experimental.pallas import tpu as pltpu
from jax.sharding import PartitionSpec as P

VMEM = pl.BlockSpec(memory_space=pltpu.VMEM)
SMEM = pl.BlockSpec(memory_space=pltpu.SMEM)


def call(kernel, outs, in_specs, flops=0, bytes_accessed=0):
    return pl.pallas_call(
        kernel,
        out_shape=outs,
        in_specs=in_specs,
        out_specs=jax.tree.map(lambda _: VMEM, outs),
        compiler_params=pltpu.CompilerParams(vmem_limit_bytes=48 * 1024 * 1024),
        cost_estimate=pl.CostEstimate(
            flops=flops, bytes_accessed=bytes_accessed, transcendentals=0
        ),
    )


def gather(own, axis):
    n = lax.axis_size(axis)
    return [own] + [
        lax.ppermute(own, axis, [(s, (s - d) % n) for s in range(n)]) for d in range(1, n)
    ]


def split(value):
    high = value.astype(jnp.bfloat16)
    return high, (value - high.astype(jnp.float32)).astype(jnp.bfloat16)


def dot(left, right, dims=((1,), (0,))):
    return lax.dot_general(left, right, (dims, ((), ())), preferred_element_type=jnp.float32)


def dense_kernel(vals, rows, cols, count, near, far):
    side = vals.shape[1]
    near[...] = jnp.zeros_like(near)
    far[...] = jnp.zeros_like(far)

    def add(t, _):
        down = pl.ds(pl.multiple_of(rows[t] * side, side), side)
        across = pl.ds(pl.multiple_of(cols[t] * side, side), side)
        tile = vals[t]
        near[down, across] = tile
        far[across, down] = tile.T
        return 0

    lax.fori_loop(0, count[0], add, 0)


def spread_kernel(matrix, operand, out):
    out[...] = dot(matrix[...], operand[...]).astype(out.dtype)


def add_pieces(pieces, rows):
    total = pieces[:rows].astype(jnp.float32)
    for start in range(rows, pieces.shape[0], rows):
        total = total + pieces[start : start + rows].astype(jnp.float32)
    return total


def layer_kernel(pieces, weight, cotangent, act, back, term):
    total = add_pieces(pieces, act.shape[0])
    high, low = split(total)
    pre = dot(high, weight[...]) + dot(low, weight[...])
    sigma = jax.nn.sigmoid(pre)
    act[...] = (pre * sigma).astype(act.dtype)
    grad = cotangent[...].astype(jnp.float32) * sigma * (1.0 + pre * (1.0 - sigma))
    grad_high, grad_low = split(grad)
    across = ((1,), (1,))
    back[...] = (dot(grad_high, weight[...], across) + dot(grad_low, weight[...], across)).astype(
        back.dtype
    )
    down = ((0,), (0,))
    term[...] = (
        dot(high, grad_high, down) + dot(low, grad_high, down) + dot(high, grad_low, down)
    ).astype(term.dtype)


def fold_kernel(pieces, out):
    out[...] = add_pieces(pieces, out.shape[0]).astype(out.dtype)


def sum_kernel(scale, *refs):
    *parts, out = refs
    total = parts[0][...].astype(jnp.float32)
    for part in parts[1:]:
        total = total + part[...].astype(jnp.float32)
    if scale is not None:
        total = total * scale
    out[...] = total.astype(out.dtype)


def per_device(features, weight, cotangent, tile_values, tile_rows, tile_cols, tile_count):
    narrow = jnp.bfloat16
    vals = tile_values.reshape(tile_values.shape[2:])
    slots, side = vals.shape[:2]
    n_row, n_col = lax.axis_size("row"), lax.axis_size("col")
    nodes, width = features.shape
    hidden = weight.shape[1]
    down, across = n_col * nodes, n_row * nodes
    def like(shape, dtype=narrow):
        return jax.ShapeDtypeStruct(shape, dtype)

    gathered = lax.all_gather(features, "row", axis=0, tiled=True)
    near, far = call(
        dense_kernel,
        (like((down, across)), like((across, down))),
        [VMEM, SMEM, SMEM, SMEM],
        bytes_accessed=6 * down * across,
    )(vals, tile_rows.reshape(-1), tile_cols.reshape(-1), tile_count.reshape(-1))

    sends = call(
        spread_kernel,
        like((down, width)),
        [VMEM] * 2,
        flops=2 * down * across * width,
    )(near, gathered)
    parts = lax.all_to_all(sends, "col", 0, 0, tiled=True)

    act, back, term = call(
        layer_kernel,
        (like((nodes, hidden)), like((nodes, width)), like((width, hidden))),
        [VMEM] * 3,
        flops=14 * nodes * width * hidden,
    )(parts, weight, cotangent)
    spread = lax.all_gather(back, "col", axis=0, tiled=True)
    terms = gather(term, "row")

    sends = call(
        spread_kernel,
        like((across, width)),
        [VMEM] * 2,
        flops=2 * down * across * width,
    )(far, spread)
    parts = lax.all_to_all(sends, "row", 0, 0, tiled=True)

    row_sum = call(
        functools.partial(sum_kernel, None), like((width, hidden)), [VMEM] * n_row
    )(*terms)
    terms = gather(row_sum, "col")
    grad_features = call(fold_kernel, like((nodes, width)), [VMEM])(parts)
    scale = float(nodes * n_row * n_col) ** -0.5
    grad_weight = call(
        functools.partial(sum_kernel, scale), like((width, hidden), jnp.float32), [VMEM] * n_col
    )(*terms)
    return act, grad_features, grad_weight


def solution(mesh):
    placed = (
        P(("groups", "row", "col"), None),
        P(),
        P(("groups", "row", "col"), None),
        P(("groups", "row"), "col", None, None, None),
        P(("groups", "row"), "col", None),
        P(("groups", "row"), "col", None),
        P(("groups", "row"), "col"),
    )
    return jax.shard_map(
        per_device,
        mesh=mesh,
        in_specs=placed,
        out_specs=(
            P(("groups", "row", "col"), None),
            P(("groups", "row", "col"), None),
            P("groups", None),
        ),
        check_vma=False,
    )
```

```python
import functools

import jax
import jax.numpy as jnp
from jax import lax
from jax.experimental import pallas as pl
from jax.experimental.pallas import tpu as pltpu
from jax.sharding import PartitionSpec as P

VMEM = pl.BlockSpec(memory_space=pltpu.VMEM)
ANY = pl.BlockSpec(memory_space=pl.ANY)
HBM = pl.BlockSpec(memory_space=pltpu.HBM)
LEAST = 16 * 1024 * 1024
NARROW = jnp.bfloat16


def call(kernel, outs, in_specs, scratch=(), flops=0, need=0, after=()):
    outs = tuple(jax.ShapeDtypeStruct(shape, dtype) for shape, dtype in outs)
    late = len(after)
    run = pl.pallas_call(
        (lambda *refs: kernel(*refs[late:])) if late else kernel,
        out_shape=outs,
        in_specs=[ANY] * late + list(in_specs),
        out_specs=(VMEM,) * len(outs),
        scratch_shapes=scratch,
        compiler_params=pltpu.CompilerParams(vmem_limit_bytes=LEAST + need),
        cost_estimate=pl.CostEstimate(flops=flops, bytes_accessed=need, transcendentals=0),
    )
    return functools.partial(run, *after)


def swap(value, axis, distance):
    n = lax.axis_size(axis)
    return lax.ppermute(value, axis, [(s, s ^ distance) for s in range(n)])


def wide(value):
    return value.astype(jnp.float32)


def split(value):
    high = value.astype(NARROW)
    return high, (value - wide(high)).astype(NARROW)


def dot(left, right, dims=((1,), (0,))):
    return lax.dot_general(left, right, (dims, ((), ())), preferred_element_type=jnp.float32)


def dense_kernel(piece, vals_in, rows_in, cols_in, count_in, near, vals, rows, cols, count, sems):
    copies = [
        pltpu.make_async_copy(source, target, sems.at[k])
        for k, (source, target) in enumerate(
            ((rows_in, rows), (cols_in, cols), (count_in, count), (vals_in, vals))
        )
    ]
    for copy in copies:
        copy.start()
    my_row, my_col = lax.axis_index("row"), lax.axis_index("col")
    side = vals.shape[-1]
    near[...] = jnp.zeros_like(near)
    for copy in copies:
        copy.wait()

    def add(t, _):
        row, col = rows[0, 0, t], cols[0, 0, t]
        row = ((row // piece) ^ my_col) * piece + lax.rem(row, piece)
        col = ((col // piece) ^ my_row) * piece + lax.rem(col, piece)
        down = pl.ds(pl.multiple_of(row * side, side), side)
        across = pl.ds(pl.multiple_of(col * side, side), side)
        near[down, across] = vals[0, 0, t]
        return 0

    lax.fori_loop(0, count[0, 0], add, 0)


def turn_kernel(step, near, far):
    def turn(k, _):
        band = pl.ds(pl.multiple_of(k * step, step), step)
        far[:, band] = near[band, :].T
        return 0

    lax.fori_loop(0, near.shape[0] // step, turn, 0)


def tree(terms):
    while len(terms) > 1:
        terms = [left + right for left, right in zip(terms[::2], terms[1::2])]
    return terms[0]


def forward_kernel(n, matrix, *refs):
    operands, own, sends = refs[:n], refs[n], refs[n + 1 :]
    rows = own.shape[0]
    stacked = jnp.concatenate([operand[...] for operand in operands], axis=0)
    product = dot(matrix[...], stacked)
    own[...] = product[:rows]
    for d, send in enumerate(sends, 1):
        send[...] = product[d * rows : (d + 1) * rows].astype(send.dtype)


def layer_kernel(*refs):
    *parts, weight, cotangent, same, other, pre_out = refs
    nodes, hidden = cotangent.shape
    half = hidden // 2
    total = tree([wide(part[...]) for part in parts])
    high, low = split(total)
    pre = dot(high, weight[...]) + dot(low, weight[...])
    pre_out[...] = pre
    sigma = jax.nn.sigmoid(pre)
    grad = wide(cotangent[...]) * sigma * (1.0 + pre * (1.0 - sigma))
    grad_high, grad_low = split(grad)
    across = ((1,), (1,))
    back = dot(grad_high, weight[...], across) + dot(grad_low, weight[...], across)
    same[:nodes] = back.astype(same.dtype)
    other[:nodes] = back.astype(other.dtype)
    down = ((0,), (0,))
    term = dot(high, grad_high, down) + dot(low, grad_high, down) + dot(high, grad_low, down)
    term = term.astype(same.dtype)
    odd = lax.rem(lax.axis_index("col"), 2) == 1
    left, right = term[:, :half], term[:, half:]
    same[nodes:] = jnp.where(odd, right, left)
    other[nodes:] = jnp.where(odd, left, right)


def act_kernel(pre, act):
    act[...] = (pre[...] * jax.nn.sigmoid(pre[...])).astype(act.dtype)


def backward_kernel(n, matrix, *refs):
    messages, own, kept, sends = refs[:n], refs[n], refs[n + 1], refs[n + 2 :]
    rows = own.shape[0]
    stacked = jnp.concatenate([message[:rows] for message in messages], axis=0)
    product = dot(matrix[...], stacked)
    own[...] = product[:rows]
    term = tree([wide(message[rows:]) for message in messages]).astype(kept.dtype)
    kept[...] = term
    for d, send in enumerate(sends, 1):
        send[:rows] = product[d * rows : (d + 1) * rows].astype(send.dtype)
        send[rows:] = term


def term_kernel(scale, kept, *refs):
    *messages, half = refs
    rows = messages[0].shape[0] - kept.shape[0]
    half[...] = tree([wide(kept[...])] + [wide(message[rows:]) for message in messages]) * scale


def feature_kernel(own, *refs):
    *messages, out = refs
    rows = own.shape[0]
    out[...] = tree([own[...]] + [wide(message[:rows]) for message in messages]).astype(out.dtype)


def join_kernel(mine, other, out):
    half = mine.shape[1]
    odd = lax.rem(lax.axis_index("col"), 2) == 1
    out[:, :half] = jnp.where(odd, other[...], mine[...])
    out[:, half:] = jnp.where(odd, mine[...], other[...])


def per_device(features, weight, cotangent, tile_values, tile_rows, tile_cols, tile_count):
    slots, side = tile_values.shape[2:4]
    n_row, n_col = lax.axis_size("row"), lax.axis_size("col")
    nodes, width = features.shape
    hidden = weight.shape[1]
    half = hidden // 2
    down, across = n_col * nodes, n_row * nodes
    dense_bytes = 2 * down * across

    gathered = [swap(features, "row", d) for d in range(n_row - 1, 0, -1)][::-1]
    (near,) = call(
        functools.partial(dense_kernel, nodes // side),
        [((down, across), NARROW)],
        [HBM] * 4,
        scratch=[
            pltpu.VMEM(tile_values.shape, NARROW),
            pltpu.SMEM(tile_rows.shape, jnp.int32),
            pltpu.SMEM(tile_cols.shape, jnp.int32),
            pltpu.SMEM(tile_count.shape, jnp.int32),
            pltpu.SemaphoreType.DMA((4,)),
        ],
        need=2 * dense_bytes,
    )(tile_values, tile_rows, tile_cols, tile_count)

    own, *sends = call(
        functools.partial(forward_kernel, n_row),
        [((nodes, width), jnp.float32)] + [((nodes, width), NARROW)] * (n_col - 1),
        [VMEM] * (1 + n_row),
        flops=2 * down * across * width,
        need=2 * dense_bytes,
    )(near, features, *gathered)
    parts = [swap(sends[d - 1], "col", d) for d in range(n_col - 1, 0, -1)][::-1]
    (far,) = call(
        functools.partial(turn_kernel, side),
        [((across, down), NARROW)],
        [VMEM],
        need=3 * dense_bytes,
    )(near)

    message = ((nodes + width, width), NARROW)
    same, other, pre = call(
        layer_kernel,
        [message, message, ((nodes, hidden), jnp.float32)],
        [VMEM] * (n_col + 2),
        flops=14 * nodes * width * hidden,
        after=[far],
    )(own, *parts, weight, cotangent)
    spread = [swap((same, other)[d % 2], "col", d) for d in range(n_col - 1, 0, -1)][::-1]
    (act,) = call(act_kernel, [((nodes, hidden), NARROW)], [VMEM])(pre)

    own, kept, *sends = call(
        functools.partial(backward_kernel, n_col),
        [((nodes, width), jnp.float32), ((width, half), NARROW)] + [message] * (n_row - 1),
        [VMEM] * (1 + n_col),
        flops=2 * down * across * width,
        need=2 * dense_bytes,
    )(far, same, *spread)
    parts = [swap(sends[d - 1], "row", d) for d in range(n_row - 1, 0, -1)][::-1]

    scale = float(nodes * n_row * n_col) ** -0.5
    (mine,) = call(
        functools.partial(term_kernel, scale), [((width, half), jnp.float32)], [VMEM] * n_row
    )(kept, *parts)
    (grad_features,) = call(feature_kernel, [((nodes, width), NARROW)], [VMEM] * n_row)(
        own, *parts
    )
    (grad_weight,) = call(join_kernel, [((width, hidden), jnp.float32)], [VMEM] * 2)(
        mine, swap(mine, "col", 1)
    )
    return act, grad_features, grad_weight


def solution(mesh):
    placed = (
        P(("groups", "row", "col"), None),
        P(),
        P(("groups", "row", "col"), None),
        P(("groups", "row"), "col", None, None, None),
        P(("groups", "row"), "col", None),
        P(("groups", "row"), "col", None),
        P(("groups", "row"), "col"),
    )
    return jax.shard_map(
        per_device,
        mesh=mesh,
        in_specs=placed,
        out_specs=(
            P(("groups", "row", "col"), None),
            P(("groups", "row", "col"), None),
            P("groups", None),
        ),
        check_vma=False,
    )
```

```python
import functools

import jax
import jax.numpy as jnp
from jax import lax
from jax.experimental import pallas as pl
from jax.experimental.pallas import tpu as pltpu
from jax.sharding import PartitionSpec as P

VMEM = pl.BlockSpec(memory_space=pltpu.VMEM)
ANY = pl.BlockSpec(memory_space=pl.ANY)
HBM = pl.BlockSpec(memory_space=pltpu.HBM)
LEAST = 16 * 1024 * 1024
NARROW = jnp.bfloat16


def call(kernel, outs, in_specs, scratch=(), flops=0, need=0, after=()):
    outs = tuple(jax.ShapeDtypeStruct(shape, dtype) for shape, dtype in outs)
    late = len(after)
    run = pl.pallas_call(
        (lambda *refs: kernel(*refs[late:])) if late else kernel,
        out_shape=outs,
        in_specs=[ANY] * late + list(in_specs),
        out_specs=(VMEM,) * len(outs),
        scratch_shapes=scratch,
        compiler_params=pltpu.CompilerParams(vmem_limit_bytes=LEAST + need),
        cost_estimate=pl.CostEstimate(flops=flops, bytes_accessed=need, transcendentals=0),
    )
    return functools.partial(run, *after)


def swap(value, axis, distance):
    n = lax.axis_size(axis)
    return lax.ppermute(value, axis, [(s, s ^ distance) for s in range(n)])


def bits(n):
    return [1 << k for k in range(n.bit_length() - 1)]


def gather(own, axis):
    held = {0: own}
    for bit in reversed(bits(lax.axis_size(axis))):
        held.update({d | bit: swap(value, axis, bit) for d, value in held.items()})
    return [held[d] for d in range(len(held))]


def wide(value):
    return value.astype(jnp.float32)


def split(value):
    high = value.astype(NARROW)
    return high, (value - wide(high)).astype(NARROW)


def dot(left, right, dims=((1,), (0,))):
    return lax.dot_general(left, right, (dims, ((), ())), preferred_element_type=jnp.float32)


def dense_kernel(piece, vals_in, rows_in, cols_in, count_in, near, vals, rows, cols, count, sems):
    copies = [
        pltpu.make_async_copy(source, target, sems.at[k])
        for k, (source, target) in enumerate(
            ((rows_in, rows), (cols_in, cols), (count_in, count), (vals_in, vals))
        )
    ]
    for copy in copies:
        copy.start()
    my_row, my_col = lax.axis_index("row"), lax.axis_index("col")
    side = vals.shape[-1]
    near[...] = jnp.zeros_like(near)
    for copy in copies:
        copy.wait()

    def add(t, _):
        row, col = rows[0, 0, t], cols[0, 0, t]
        row = ((row // piece) ^ my_col) * piece + lax.rem(row, piece)
        col = ((col // piece) ^ my_row) * piece + lax.rem(col, piece)
        down = pl.ds(pl.multiple_of(row * side, side), side)
        across = pl.ds(pl.multiple_of(col * side, side), side)
        near[down, across] = vals[0, 0, t]
        return 0

    lax.fori_loop(0, count[0, 0], add, 0)


def turn_kernel(step, near, far):
    def turn(k, _):
        band = pl.ds(pl.multiple_of(k * step, step), step)
        far[:, band] = near[band, :].T
        return 0

    lax.fori_loop(0, near.shape[0] // step, turn, 0)


def tree(terms):
    while len(terms) > 1:
        terms = [left + right for left, right in zip(terms[::2], terms[1::2])]
    return terms[0]


def forward_kernel(n, matrix, *refs):
    operands, own, sends = refs[:n], refs[n], refs[n + 1 :]
    rows = own.shape[0]
    stacked = jnp.concatenate([operand[...] for operand in operands], axis=0)
    product = dot(matrix[...], stacked)
    own[...] = product[:rows]
    for d, send in enumerate(sends, 1):
        send[...] = product[d * rows : (d + 1) * rows].astype(send.dtype)


def layer_kernel(*refs):
    *parts, weight, cotangent, back, pre_out, mine, other = refs
    half = mine.shape[1]
    total = tree([wide(part[...]) for part in parts])
    high, low = split(total)
    pre = dot(high, weight[...]) + dot(low, weight[...])
    pre_out[...] = pre
    sigma = jax.nn.sigmoid(pre)
    grad = wide(cotangent[...]) * sigma * (1.0 + pre * (1.0 - sigma))
    grad_high, grad_low = split(grad)
    across = ((1,), (1,))
    back[...] = (dot(grad_high, weight[...], across) + dot(grad_low, weight[...], across)).astype(
        back.dtype
    )
    down = ((0,), (0,))
    term = dot(high, grad_high, down) + dot(low, grad_high, down) + dot(high, grad_low, down)
    odd = lax.rem(lax.axis_index("row"), 2) == 1
    left, right = term[:, :half], term[:, half:]
    mine[...] = jnp.where(odd, right, left).astype(mine.dtype)
    other[...] = jnp.where(odd, left, right).astype(other.dtype)


def act_kernel(pre, act):
    act[...] = (pre[...] * jax.nn.sigmoid(pre[...])).astype(act.dtype)


def add_kernel(scale, left, right, out):
    out[...] = ((wide(left[...]) + wide(right[...])) * scale).astype(out.dtype)


def add(left, right, dtype=NARROW, scale=1.0, after=()):
    (out,) = call(
        functools.partial(add_kernel, scale), [(left.shape, dtype)], [VMEM] * 2, after=after
    )(left, right)
    return out


def fold(pieces, distance):
    stay = [piece for d, piece in enumerate(pieces) if not d & distance]
    return stay, jnp.concatenate([piece for d, piece in enumerate(pieces) if d & distance], axis=0)


def backward_kernel(n, n_out, matrix, left, right, *refs):
    messages, (stay, send, summed) = refs[:n], refs[n:]
    rows = messages[0].shape[0]
    stacked = jnp.concatenate([message[...] for message in messages], axis=0)
    product = dot(matrix[...], stacked)
    kept, going = fold([product[d * rows : (d + 1) * rows] for d in range(n_out)], 1)
    stay[...] = jnp.concatenate(kept, axis=0)
    send[...] = going.astype(send.dtype)
    summed[...] = (wide(left[...]) + wide(right[...])).astype(summed.dtype)


def fold_kernel(rows, kept, came, stay, send):
    total = kept[...] + wide(came[...])
    pieces = [total[k : k + rows] for k in range(0, total.shape[0], rows)]
    left, going = fold(pieces, 1)
    stay[...] = jnp.concatenate(left, axis=0)
    send[...] = going.astype(send.dtype)


def join_kernel(mine, other, out):
    half = mine.shape[1]
    odd = lax.rem(lax.axis_index("row"), 2) == 1
    out[:, :half] = jnp.where(odd, other[...], mine[...])
    out[:, half:] = jnp.where(odd, mine[...], other[...])


def per_device(features, weight, cotangent, tile_values, tile_rows, tile_cols, tile_count):
    slots, side = tile_values.shape[2:4]
    n_row, n_col = lax.axis_size("row"), lax.axis_size("col")
    nodes, width = features.shape
    hidden = weight.shape[1]
    half = hidden // 2
    down, across = n_col * nodes, n_row * nodes
    dense_bytes = 2 * down * across

    gathered = gather(features, "row")
    (near,) = call(
        functools.partial(dense_kernel, nodes // side),
        [((down, across), NARROW)],
        [HBM] * 4,
        scratch=[
            pltpu.VMEM(tile_values.shape, NARROW),
            pltpu.SMEM(tile_rows.shape, jnp.int32),
            pltpu.SMEM(tile_cols.shape, jnp.int32),
            pltpu.SMEM(tile_count.shape, jnp.int32),
            pltpu.SemaphoreType.DMA((4,)),
        ],
        need=2 * dense_bytes,
    )(tile_values, tile_rows, tile_cols, tile_count)

    own, *sends = call(
        functools.partial(forward_kernel, n_row),
        [((nodes, width), jnp.float32)] + [((nodes, width), NARROW)] * (n_col - 1),
        [VMEM] * (1 + n_row),
        flops=2 * down * across * width,
        need=2 * dense_bytes,
    )(near, *gathered)
    parts = [swap(sends[d - 1], "col", d) for d in range(n_col - 1, 0, -1)][::-1]
    (far,) = call(
        functools.partial(turn_kernel, side),
        [((across, down), NARROW)],
        [VMEM],
        need=3 * dense_bytes,
    )(near)

    square = (width, half)
    back, pre, term, other = call(
        layer_kernel,
        [
            ((nodes, width), NARROW),
            ((nodes, hidden), jnp.float32),
            (square, jnp.float32),
            (square, NARROW),
        ],
        [VMEM] * (n_col + 2),
        flops=14 * nodes * width * hidden,
        after=[far],
    )(own, *parts, weight, cotangent)
    spread = gather(back, "col")
    (act,) = call(act_kernel, [((nodes, hidden), NARROW)], [VMEM])(pre)

    term = add(term, swap(other, "row", 1))
    *early, last = bits(n_row)[1:]
    for bit in early:
        term = add(term, swap(term, "row", bit))

    pieces = n_row // 2
    stay, send, term = call(
        functools.partial(backward_kernel, n_col, n_row),
        [((pieces * nodes, width), jnp.float32), ((pieces * nodes, width), NARROW), (square, NARROW)],
        [VMEM] * (3 + n_col),
        flops=2 * down * across * width,
        need=2 * dense_bytes,
    )(far, term, swap(term, "row", last), *spread)

    for bit in bits(n_row)[1:]:
        pieces //= 2
        shape = (pieces * nodes, width)
        stay, send = call(
            functools.partial(fold_kernel, nodes), [(shape, jnp.float32), (shape, NARROW)], [VMEM] * 2
        )(stay, swap(send, "row", bit // 2))
    grad_features = add(stay, swap(send, "row", n_row // 2))

    *early, last = bits(n_col)
    for bit in early:
        term = add(term, swap(term, "col", bit), after=[stay])
    scale = float(nodes * n_row * n_col) ** -0.5
    mine = add(term, swap(term, "col", last), jnp.float32, scale)
    (grad_weight,) = call(join_kernel, [((width, hidden), jnp.float32)], [VMEM] * 2)(
        mine, swap(mine, "row", 1)
    )
    return act, grad_features, grad_weight


def solution(mesh):
    placed = (
        P(("groups", "row", "col"), None),
        P(),
        P(("groups", "row", "col"), None),
        P(("groups", "row"), "col", None, None, None),
        P(("groups", "row"), "col", None),
        P(("groups", "row"), "col", None),
        P(("groups", "row"), "col"),
    )
    return jax.shard_map(
        per_device,
        mesh=mesh,
        in_specs=placed,
        out_specs=(
            P(("groups", "row", "col"), None),
            P(("groups", "row", "col"), None),
            P("groups", None),
        ),
        check_vma=False,
    )
```

```python
import functools

import jax
import jax.numpy as jnp
from jax import lax
from jax.experimental import pallas as pl
from jax.experimental.pallas import tpu as pltpu
from jax.sharding import PartitionSpec as P

VMEM = pl.BlockSpec(memory_space=pltpu.VMEM)
ANY = pl.BlockSpec(memory_space=pl.ANY)
LEAST = 16 * 1024 * 1024
NARROW = jnp.bfloat16


def call(kernel, outs, in_specs, scratch=(), flops=0, need=0, after=()):
    outs = tuple(jax.ShapeDtypeStruct(shape, dtype) for shape, dtype in outs)
    late = len(after)
    run = pl.pallas_call(
        (lambda *refs: kernel(*refs[late:])) if late else kernel,
        out_shape=outs,
        in_specs=[ANY] * late + list(in_specs),
        out_specs=(VMEM,) * len(outs),
        scratch_shapes=scratch,
        compiler_params=pltpu.CompilerParams(vmem_limit_bytes=LEAST + need),
        cost_estimate=pl.CostEstimate(flops=flops, bytes_accessed=need, transcendentals=0),
    )
    return functools.partial(run, *after)


def exchange(sends, axis, ahead):
    n = lax.axis_size(axis)
    return [
        lax.ppermute(send, axis, [(s, (s + (d if ahead else -d)) % n) for s in range(n)])
        for d, send in enumerate(sends, 1)
    ]


def neighbour(value, axis):
    n = lax.axis_size(axis)
    return lax.ppermute(value, axis, [(s, s ^ 1) for s in range(n)])


def wide(value):
    return value.astype(jnp.float32)


def split(value):
    high = value.astype(NARROW)
    return high, (value - wide(high)).astype(NARROW)


def dot(left, right, dims=((1,), (0,))):
    return lax.dot_general(left, right, (dims, ((), ())), preferred_element_type=jnp.float32)


def dense_kernel(n_row, n_col, piece, vals, rows_in, cols_in, count_in, near, rows, cols, count, sems):
    copies = [
        pltpu.make_async_copy(source, target, sems.at[k])
        for k, (source, target) in enumerate(((rows_in, rows), (cols_in, cols), (count_in, count)))
    ]
    for copy in copies:
        copy.start()
    my_row, my_col = lax.axis_index("row"), lax.axis_index("col")
    side = vals.shape[-1]
    near[...] = jnp.zeros_like(near)
    for copy in copies:
        copy.wait()

    def add(t, _):
        row, col = rows[0, 0, t], cols[0, 0, t]
        row = lax.rem(row // piece - my_col + n_col, n_col) * piece + lax.rem(row, piece)
        col = lax.rem(col // piece - my_row + n_row, n_row) * piece + lax.rem(col, piece)
        down = pl.ds(pl.multiple_of(row * side, side), side)
        across = pl.ds(pl.multiple_of(col * side, side), side)
        near[down, across] = vals[0, 0, t]
        return 0

    lax.fori_loop(0, count[0, 0], add, 0)


def turn_kernel(step, near, far):
    def turn(k, _):
        band = pl.ds(pl.multiple_of(k * step, step), step)
        far[:, band] = near[band, :].T
        return 0

    lax.fori_loop(0, near.shape[0] // step, turn, 0)


def tree(terms):
    while len(terms) > 1:
        middle = len(terms) // 2
        terms = [left + right for left, right in zip(terms[:middle], terms[middle:])]
    return terms[0]


def forward_kernel(n, matrix, *refs):
    operands, own, sends = refs[:n], refs[n], refs[n + 1 :]
    rows = own.shape[0]
    stacked = jnp.concatenate([operand[...] for operand in operands], axis=0)
    product = dot(matrix[...], stacked)
    own[...] = product[:rows]
    for d, send in enumerate(sends, 1):
        send[...] = product[d * rows : (d + 1) * rows].astype(send.dtype)


def layer_kernel(*refs):
    *parts, weight, cotangent, same, other, pre_out = refs
    nodes, hidden = cotangent.shape
    half = hidden // 2
    total = tree([wide(part[...]) for part in parts])
    high, low = split(total)
    pre = dot(high, weight[...]) + dot(low, weight[...])
    pre_out[...] = pre
    sigma = jax.nn.sigmoid(pre)
    grad = wide(cotangent[...]) * sigma * (1.0 + pre * (1.0 - sigma))
    grad_high, grad_low = split(grad)
    across = ((1,), (1,))
    back = dot(grad_high, weight[...], across) + dot(grad_low, weight[...], across)
    same[:nodes] = back.astype(same.dtype)
    other[:nodes] = back.astype(other.dtype)
    down = ((0,), (0,))
    term = dot(high, grad_high, down) + dot(low, grad_high, down) + dot(high, grad_low, down)
    term = term.astype(same.dtype)
    odd = lax.rem(lax.axis_index("col"), 2) == 1
    left, right = term[:, :half], term[:, half:]
    same[nodes:] = jnp.where(odd, right, left)
    other[nodes:] = jnp.where(odd, left, right)


def act_kernel(pre, act):
    act[...] = (pre[...] * jax.nn.sigmoid(pre[...])).astype(act.dtype)


def backward_kernel(n, matrix, *refs):
    messages, own, kept, sends = refs[:n], refs[n], refs[n + 1], refs[n + 2 :]
    rows = own.shape[0]
    stacked = jnp.concatenate([message[:rows] for message in messages], axis=0)
    product = dot(matrix[...], stacked)
    own[...] = product[:rows]
    term = tree([wide(message[rows:]) for message in messages]).astype(kept.dtype)
    kept[...] = term
    for d, send in enumerate(sends, 1):
        send[:rows] = product[d * rows : (d + 1) * rows].astype(send.dtype)
        send[rows:] = term


def term_kernel(scale, kept, *refs):
    *messages, half = refs
    rows = messages[0].shape[0] - kept.shape[0]
    total = tree([wide(kept[...])] + [wide(message[rows:]) for message in messages])
    half[...] = (total * scale).astype(half.dtype)


def feature_kernel(own, *refs):
    *messages, out = refs
    rows = own.shape[0]
    out[...] = tree([own[...]] + [wide(message[:rows]) for message in messages]).astype(out.dtype)


def join_kernel(mine, other, out):
    half = mine.shape[1]
    odd = lax.rem(lax.axis_index("col"), 2) == 1
    out[:, :half] = jnp.where(odd, wide(other[...]), wide(mine[...]))
    out[:, half:] = jnp.where(odd, wide(mine[...]), wide(other[...]))


def per_device(features, weight, cotangent, tile_values, tile_rows, tile_cols, tile_count):
    slots, side = tile_values.shape[2:4]
    n_row, n_col = lax.axis_size("row"), lax.axis_size("col")
    nodes, width = features.shape
    hidden = weight.shape[1]
    half = hidden // 2
    down, across = n_col * nodes, n_row * nodes
    dense_bytes = 2 * down * across

    gathered = exchange([features] * (n_row - 1), "row", False)
    (near,) = call(
        functools.partial(dense_kernel, n_row, n_col, nodes // side),
        [((down, across), NARROW)],
        [VMEM] * 4,
        scratch=[
            pltpu.SMEM(tile_rows.shape, jnp.int32),
            pltpu.SMEM(tile_cols.shape, jnp.int32),
            pltpu.SMEM(tile_count.shape, jnp.int32),
            pltpu.SemaphoreType.DMA((3,)),
        ],
        need=2 * dense_bytes,
    )(tile_values, tile_rows, tile_cols, tile_count)

    own, *sends = call(
        functools.partial(forward_kernel, n_row),
        [((nodes, width), jnp.float32)] + [((nodes, width), NARROW)] * (n_col - 1),
        [VMEM] * (1 + n_row),
        flops=2 * down * across * width,
        need=2 * dense_bytes,
    )(near, features, *gathered)
    parts = exchange(sends, "col", True)
    (far,) = call(
        functools.partial(turn_kernel, side),
        [((across, down), NARROW)],
        [VMEM],
        need=3 * dense_bytes,
    )(near)

    message = ((nodes + width, width), NARROW)
    same, other, pre = call(
        layer_kernel,
        [message, message, ((nodes, hidden), jnp.float32)],
        [VMEM] * (n_col + 2),
        flops=14 * nodes * width * hidden,
        after=[far],
    )(own, *parts, weight, cotangent)
    spread = exchange([(same, other)[d % 2] for d in range(1, n_col)], "col", False)
    (act,) = call(act_kernel, [((nodes, hidden), NARROW)], [VMEM])(pre)

    own, kept, *sends = call(
        functools.partial(backward_kernel, n_col),
        [((nodes, width), jnp.float32), ((width, half), NARROW)] + [message] * (n_row - 1),
        [VMEM] * (1 + n_col),
        flops=2 * down * across * width,
        need=2 * dense_bytes,
    )(far, same, *spread)
    parts = exchange(sends, "row", True)

    scale = float(nodes * n_row * n_col) ** -0.5
    (mine,) = call(
        functools.partial(term_kernel, scale), [((width, half), NARROW)], [VMEM] * n_row
    )(kept, *parts)
    (grad_features,) = call(feature_kernel, [((nodes, width), NARROW)], [VMEM] * n_row)(
        own, *parts
    )
    (grad_weight,) = call(join_kernel, [((width, hidden), jnp.float32)], [VMEM] * 2)(
        mine, neighbour(mine, "col")
    )
    return act, grad_features, grad_weight


def solution(mesh):
    placed = (
        P(("groups", "row", "col"), None),
        P(),
        P(("groups", "row", "col"), None),
        P(("groups", "row"), "col", None, None, None),
        P(("groups", "row"), "col", None),
        P(("groups", "row"), "col", None),
        P(("groups", "row"), "col"),
    )
    return jax.shard_map(
        per_device,
        mesh=mesh,
        in_specs=placed,
        out_specs=(
            P(("groups", "row", "col"), None),
            P(("groups", "row", "col"), None),
            P("groups", None),
        ),
        check_vma=False,
    )
```

```python
import functools

import jax
import jax.numpy as jnp
from jax import lax
from jax.experimental import pallas as pl
from jax.experimental.pallas import tpu as pltpu
from jax.sharding import PartitionSpec as P

VMEM = pl.BlockSpec(memory_space=pltpu.VMEM)
ANY = pl.BlockSpec(memory_space=pl.ANY)
LEAST = 16 * 1024 * 1024
NARROW = jnp.bfloat16


def call(kernel, outs, in_specs, scratch=(), flops=0, need=0, after=()):
    outs = tuple(jax.ShapeDtypeStruct(shape, dtype) for shape, dtype in outs)
    late = len(after)
    run = pl.pallas_call(
        (lambda *refs: kernel(*refs[late:])) if late else kernel,
        out_shape=outs,
        in_specs=[ANY] * late + list(in_specs),
        out_specs=(VMEM,) * len(outs),
        scratch_shapes=scratch,
        compiler_params=pltpu.CompilerParams(vmem_limit_bytes=LEAST + need),
        cost_estimate=pl.CostEstimate(flops=flops, bytes_accessed=need, transcendentals=0),
    )
    return functools.partial(run, *after)


def exchange(sends, axis, ahead):
    n = lax.axis_size(axis)
    return [
        lax.ppermute(send, axis, [(s, (s + (d if ahead else -d)) % n) for s in range(n)])
        for d, send in enumerate(sends, 1)
    ]


def wide(value):
    return value.astype(jnp.float32)


def split(value):
    high = value.astype(NARROW)
    return high, (value - wide(high)).astype(NARROW)


def dot(left, right, dims=((1,), (0,))):
    return lax.dot_general(left, right, (dims, ((), ())), preferred_element_type=jnp.float32)


def dense_kernel(n_row, n_col, piece, vals, rows_in, cols_in, count_in, near, rows, cols, count, sems):
    copies = [
        pltpu.make_async_copy(source, target, sems.at[k])
        for k, (source, target) in enumerate(((rows_in, rows), (cols_in, cols), (count_in, count)))
    ]
    for copy in copies:
        copy.start()
    my_row, my_col = lax.axis_index("row"), lax.axis_index("col")
    side = vals.shape[-1]
    near[...] = jnp.zeros_like(near)
    for copy in copies:
        copy.wait()

    def add(t, _):
        row, col = rows[0, 0, t], cols[0, 0, t]
        row = lax.rem(row // piece - my_col + n_col, n_col) * piece + lax.rem(row, piece)
        col = lax.rem(col // piece - my_row + n_row, n_row) * piece + lax.rem(col, piece)
        down = pl.ds(pl.multiple_of(row * side, side), side)
        across = pl.ds(pl.multiple_of(col * side, side), side)
        near[down, across] = vals[0, 0, t]
        return 0

    lax.fori_loop(0, count[0, 0], add, 0)


def turn_kernel(step, near, far):
    def turn(k, _):
        band = pl.ds(pl.multiple_of(k * step, step), step)
        far[:, band] = near[band, :].T
        return 0

    lax.fori_loop(0, near.shape[0] // step, turn, 0)


def tree(terms):
    while len(terms) > 1:
        middle = len(terms) // 2
        terms = [left + right for left, right in zip(terms[:middle], terms[middle:])]
    return terms[0]


def forward_kernel(n, matrix, *refs):
    operands, own, sends = refs[:n], refs[n], refs[n + 1 :]
    rows = own.shape[0]
    stacked = jnp.concatenate([operand[...] for operand in operands], axis=0)
    product = dot(matrix[...], stacked)
    own[...] = product[:rows]
    for d, send in enumerate(sends, 1):
        send[...] = product[d * rows : (d + 1) * rows].astype(send.dtype)


def layer_kernel(*refs):
    *parts, weight, cotangent, message, pre_out = refs
    nodes = cotangent.shape[0]
    total = tree([wide(part[...]) for part in parts])
    high, low = split(total)
    pre = dot(high, weight[...]) + dot(low, weight[...])
    pre_out[...] = pre
    sigma = jax.nn.sigmoid(pre)
    grad = wide(cotangent[...]) * sigma * (1.0 + pre * (1.0 - sigma))
    grad_high, grad_low = split(grad)
    across = ((1,), (1,))
    back = dot(grad_high, weight[...], across) + dot(grad_low, weight[...], across)
    message[:nodes] = back.astype(message.dtype)
    down = ((0,), (0,))
    term = dot(high, grad_high, down) + dot(low, grad_high, down) + dot(high, grad_low, down)
    half = message.shape[1]
    rows = total.shape[1]
    for k in range(term.shape[1] // half):
        start = nodes + k * rows
        message[start : start + rows] = term[:, k * half : (k + 1) * half].astype(message.dtype)


def act_kernel(pre, act):
    act[...] = (pre[...] * jax.nn.sigmoid(pre[...])).astype(act.dtype)


def backward_kernel(n, matrix, *refs):
    messages, own, kept, sends = refs[:n], refs[n], refs[n + 1], refs[n + 2 :]
    rows = own.shape[0]
    stacked = jnp.concatenate([message[:rows] for message in messages], axis=0)
    product = dot(matrix[...], stacked)
    own[...] = product[:rows]
    term = tree([wide(message[rows:]) for message in messages]).astype(kept.dtype)
    kept[...] = term
    for d, send in enumerate(sends, 1):
        send[:rows] = product[d * rows : (d + 1) * rows].astype(send.dtype)
        send[rows:] = term


def last_kernel(scale, own, kept, *refs):
    *messages, features_out, weight_out = refs
    nodes = own.shape[0]
    rows, half = weight_out.shape[0], kept.shape[1]
    features_out[...] = tree(
        [own[...]] + [wide(message[:nodes]) for message in messages]
    ).astype(features_out.dtype)
    total = tree([wide(kept[...])] + [wide(message[nodes:]) for message in messages]) * scale
    for k in range(weight_out.shape[1] // half):
        weight_out[:, k * half : (k + 1) * half] = total[k * rows : (k + 1) * rows]


def per_device(features, weight, cotangent, tile_values, tile_rows, tile_cols, tile_count):
    slots, side = tile_values.shape[2:4]
    n_row, n_col = lax.axis_size("row"), lax.axis_size("col")
    nodes, width = features.shape
    hidden = weight.shape[1]
    down, across = n_col * nodes, n_row * nodes
    dense_bytes = 2 * down * across

    gathered = exchange([features] * (n_row - 1), "row", False)
    (near,) = call(
        functools.partial(dense_kernel, n_row, n_col, nodes // side),
        [((down, across), NARROW)],
        [VMEM] * 4,
        scratch=[
            pltpu.SMEM(tile_rows.shape, jnp.int32),
            pltpu.SMEM(tile_cols.shape, jnp.int32),
            pltpu.SMEM(tile_count.shape, jnp.int32),
            pltpu.SemaphoreType.DMA((3,)),
        ],
        need=2 * dense_bytes,
    )(tile_values, tile_rows, tile_cols, tile_count)

    own, *sends = call(
        functools.partial(forward_kernel, n_row),
        [((nodes, width), jnp.float32)] + [((nodes, width), NARROW)] * (n_col - 1),
        [VMEM] * (1 + n_row),
        flops=2 * down * across * width,
        need=2 * dense_bytes,
    )(near, features, *gathered)
    parts = exchange(sends, "col", True)
    (far,) = call(
        functools.partial(turn_kernel, side),
        [((across, down), NARROW)],
        [VMEM],
        need=3 * dense_bytes,
    )(near)

    stacked = hidden // width * width
    message = ((nodes + stacked, width), NARROW)
    sent, pre = call(
        layer_kernel,
        [message, ((nodes, hidden), jnp.float32)],
        [VMEM] * (n_col + 2),
        flops=14 * nodes * width * hidden,
        after=[far],
    )(own, *parts, weight, cotangent)
    spread = exchange([sent] * (n_col - 1), "col", False)
    (act,) = call(act_kernel, [((nodes, hidden), NARROW)], [VMEM])(pre)

    own, kept, *sends = call(
        functools.partial(backward_kernel, n_col),
        [((nodes, width), jnp.float32), ((stacked, width), NARROW)] + [message] * (n_row - 1),
        [VMEM] * (1 + n_col),
        flops=2 * down * across * width,
        need=2 * dense_bytes,
    )(far, sent, *spread)
    parts = exchange(sends, "row", True)

    scale = float(nodes * n_row * n_col) ** -0.5
    grad_features, grad_weight = call(
        functools.partial(last_kernel, scale),
        [((nodes, width), NARROW), ((width, hidden), jnp.float32)],
        [VMEM] * (n_row + 1),
    )(own, kept, *parts)
    return act, grad_features, grad_weight


def solution(mesh):
    placed = (
        P(("groups", "row", "col"), None),
        P(),
        P(("groups", "row", "col"), None),
        P(("groups", "row"), "col", None, None, None),
        P(("groups", "row"), "col", None),
        P(("groups", "row"), "col", None),
        P(("groups", "row"), "col"),
    )
    return jax.shard_map(
        per_device,
        mesh=mesh,
        in_specs=placed,
        out_specs=(
            P(("groups", "row", "col"), None),
            P(("groups", "row", "col"), None),
            P("groups", None),
        ),
        check_vma=False,
    )
```

```python
import functools

import jax
import jax.numpy as jnp
from jax import lax
from jax.experimental import pallas as pl
from jax.experimental.pallas import tpu as pltpu
from jax.sharding import PartitionSpec as P

VMEM = pl.BlockSpec(memory_space=pltpu.VMEM)
ANY = pl.BlockSpec(memory_space=pl.ANY)
LEAST = 16 * 1024 * 1024
NARROW = jnp.bfloat16


def call(kernel, outs, in_specs, scratch=(), flops=0, need=0, after=()):
    outs = tuple(jax.ShapeDtypeStruct(shape, dtype) for shape, dtype in outs)
    late = len(after)
    run = pl.pallas_call(
        (lambda *refs: kernel(*refs[late:])) if late else kernel,
        out_shape=outs,
        in_specs=[ANY] * late + list(in_specs),
        out_specs=(VMEM,) * len(outs),
        scratch_shapes=scratch,
        compiler_params=pltpu.CompilerParams(vmem_limit_bytes=LEAST + need),
        cost_estimate=pl.CostEstimate(flops=flops, bytes_accessed=need, transcendentals=0),
    )
    return functools.partial(run, *after)


def exchange(sends, axis, ahead):
    n = lax.axis_size(axis)
    return [
        lax.ppermute(send, axis, [(s, (s + (d if ahead else -d)) % n) for s in range(n)])
        for d, send in enumerate(sends, 1)
    ]


def send(value, axis, pairs):
    return lax.ppermute(value, axis, pairs)


def wide(value):
    return value.astype(jnp.float32)


def split(value):
    high = value.astype(NARROW)
    return high, (value - wide(high)).astype(NARROW)


def dot(left, right, dims=((1,), (0,))):
    return lax.dot_general(left, right, (dims, ((), ())), preferred_element_type=jnp.float32)


def dense_kernel(n_row, n_col, piece, sides, vals, rows_in, cols_in, count_in, near, rows, cols, count, sems):
    copies = [
        pltpu.make_async_copy(source, target, sems.at[k])
        for k, (source, target) in enumerate(((rows_in, rows), (cols_in, cols), (count_in, count)))
    ]
    for copy in copies:
        copy.start()
    my_row, my_col = lax.axis_index("row"), lax.axis_index("col")
    side = vals.shape[-1]
    near[...] = jnp.zeros_like(near)
    for copy in copies:
        copy.wait()

    def add(t, _):
        row, col = rows[0, 0, t], cols[0, 0, t]
        if sides:
            place = (row // piece) ^ (2 * (my_col // 2))
        else:
            place = lax.rem(row // piece - my_col + n_col, n_col)
        row = place * piece + lax.rem(row, piece)
        col = lax.rem(col // piece - my_row + n_row, n_row) * piece + lax.rem(col, piece)
        down = pl.ds(pl.multiple_of(row * side, side), side)
        across = pl.ds(pl.multiple_of(col * side, side), side)
        near[down, across] = vals[0, 0, t]
        return 0

    lax.fori_loop(0, count[0, 0], add, 0)


def turn_kernel(step, near, far):
    def turn(k, _):
        band = pl.ds(pl.multiple_of(k * step, step), step)
        far[:, band] = near[band, :].T
        return 0

    lax.fori_loop(0, near.shape[0] // step, turn, 0)


def tree(terms):
    while len(terms) > 1:
        middle = len(terms) // 2
        terms = [left + right for left, right in zip(terms[:middle], terms[middle:])]
    return terms[0]


def forward_kernel(n, matrix, *refs):
    operands, own, sends = refs[:n], refs[n], refs[n + 1 :]
    rows = own.shape[0]
    stacked = jnp.concatenate([operand[...] for operand in operands], axis=0)
    product = dot(matrix[...], stacked)
    own[...] = product[:rows]
    for d, send in enumerate(sends, 1):
        send[...] = product[d * rows : (d + 1) * rows].astype(send.dtype)


def layer(total, weight, cotangent):
    high, low = split(total)
    pre = dot(high, weight) + dot(low, weight)
    sigma = jax.nn.sigmoid(pre)
    grad = wide(cotangent) * sigma * (1.0 + pre * (1.0 - sigma))
    grad_high, grad_low = split(grad)
    across, down = ((1,), (1,)), ((0,), (0,))
    back = dot(grad_high, weight, across) + dot(grad_low, weight, across)
    term = dot(high, grad_high, down) + dot(low, grad_high, down) + dot(high, grad_low, down)
    return pre, sigma, back, term


def fill_message(message, back, term):
    nodes, width = back.shape
    rows = term.shape[0]
    message[:nodes] = back.astype(message.dtype)
    for k in range(term.shape[1] // width):
        start = nodes + k * rows
        message[start : start + rows] = term[:, k * width : (k + 1) * width].astype(message.dtype)


def layer_kernel(*refs):
    *parts, weight, cotangent, message, pre_out = refs
    total = tree([wide(part[...]) for part in parts])
    pre, _, back, term = layer(total, weight[...], cotangent[...])
    pre_out[...] = pre
    fill_message(message, back, term)


def middle_forward_kernel(n, matrix, *refs):
    operands, (own, near, far) = refs[:n], refs[n:]
    rows = own.shape[0]
    stacked = jnp.concatenate([operand[...] for operand in operands], axis=0)
    product = dot(matrix[...], stacked)
    own[...] = product[:rows]
    near[...] = product[:rows].astype(near.dtype)
    far[...] = product[rows:].astype(far.dtype)


def middle_layer_kernel(own, first, second, third, weight, mine, ends, message, pre_out, act_out):
    nodes = mine.shape[0]
    high_side = lax.axis_index("col") >= 2
    total = (own[...] + wide(first[...])) + (wide(second[...]) + wide(third[...]))
    cotangent = jnp.concatenate(
        [
            jnp.where(high_side, mine[...], ends[...]),
            jnp.where(high_side, ends[...], mine[...]),
        ],
        axis=0,
    )
    pre, sigma, back, term = layer(total, weight[...], cotangent)
    fill_message(message, back, term)
    act = pre * sigma
    pre_out[...] = jnp.where(high_side, pre[:nodes], pre[nodes:])
    act_out[...] = jnp.where(high_side, act[nodes:], act[:nodes]).astype(act_out.dtype)


def middle_backward_kernel(matrix, mine, beside, across, beyond, *refs):
    own, kept, *sends = refs
    rows = own.shape[0]
    my_col = lax.axis_index("col")
    middle = (my_col == 1) | (my_col == 2)
    near = jnp.where(middle, mine[...], beside[...])
    far = jnp.where(middle, across[...], beyond[...])
    backs = 2 * rows
    product = dot(matrix[...], jnp.concatenate([near[:backs], far[:backs]], axis=0))
    own[...] = product[:rows]
    term = (wide(near[backs:]) + wide(far[backs:])).astype(kept.dtype)
    kept[...] = term
    for d, target in enumerate(sends, 1):
        target[:rows] = product[d * rows : (d + 1) * rows].astype(target.dtype)
        target[rows:] = term


def choose_kernel(pre, came, act):
    my_col = lax.axis_index("col")
    middle = (my_col == 1) | (my_col == 2)
    mine = (pre[...] * jax.nn.sigmoid(pre[...])).astype(act.dtype)
    act[...] = jnp.where(middle, mine, came[...])


def act_kernel(pre, act):
    act[...] = (pre[...] * jax.nn.sigmoid(pre[...])).astype(act.dtype)


def backward_kernel(n, matrix, *refs):
    messages, own, kept, sends = refs[:n], refs[n], refs[n + 1], refs[n + 2 :]
    rows = own.shape[0]
    stacked = jnp.concatenate([message[:rows] for message in messages], axis=0)
    product = dot(matrix[...], stacked)
    own[...] = product[:rows]
    term = tree([wide(message[rows:]) for message in messages]).astype(kept.dtype)
    kept[...] = term
    for d, send in enumerate(sends, 1):
        send[:rows] = product[d * rows : (d + 1) * rows].astype(send.dtype)
        send[rows:] = term


def last_kernel(scale, own, kept, *refs):
    *messages, features_out, weight_out = refs
    nodes = own.shape[0]
    rows, half = weight_out.shape[0], kept.shape[1]
    features_out[...] = tree(
        [own[...]] + [wide(message[:nodes]) for message in messages]
    ).astype(features_out.dtype)
    total = tree([wide(kept[...])] + [wide(message[nodes:]) for message in messages]) * scale
    for k in range(weight_out.shape[1] // half):
        weight_out[:, k * half : (k + 1) * half] = total[k * rows : (k + 1) * rows]


def per_device(features, weight, cotangent, tile_values, tile_rows, tile_cols, tile_count):
    slots, side = tile_values.shape[2:4]
    n_row, n_col = lax.axis_size("row"), lax.axis_size("col")
    nodes, width = features.shape
    hidden = weight.shape[1]
    down, across = n_col * nodes, n_row * nodes
    dense_bytes = 2 * down * across

    sides = n_col == 4
    gathered = exchange([features] * (n_row - 1), "row", False)
    if sides:
        inward, outward = [(0, 1), (3, 2)], [(1, 0), (2, 3)]
        swapped = [(1, 2), (2, 1)]
        ends = send(cotangent, "col", inward)
    (near,) = call(
        functools.partial(dense_kernel, n_row, n_col, nodes // side, sides),
        [((down, across), NARROW)],
        [VMEM] * 4,
        scratch=[
            pltpu.SMEM(tile_rows.shape, jnp.int32),
            pltpu.SMEM(tile_cols.shape, jnp.int32),
            pltpu.SMEM(tile_count.shape, jnp.int32),
            pltpu.SemaphoreType.DMA((3,)),
        ],
        need=2 * dense_bytes,
    )(tile_values, tile_rows, tile_cols, tile_count)

    stacked = hidden // width * width
    message = ((nodes + stacked, width), NARROW)
    forward = dict(flops=2 * down * across * width, need=2 * dense_bytes)
    if sides:
        pair = (2 * nodes, width)
        own, mine, other = call(
            functools.partial(middle_forward_kernel, n_row),
            [(pair, jnp.float32), (pair, NARROW), (pair, NARROW)],
            [VMEM] * (1 + n_row),
            **forward,
        )(near, features, *gathered)
        beyond = send(other, "col", [(0, 2), (3, 1)])
        parts = [send(mine, "col", inward), send(other, "col", swapped), beyond]
    else:
        own, *sends = call(
            functools.partial(forward_kernel, n_row),
            [((nodes, width), jnp.float32)] + [((nodes, width), NARROW)] * (n_col - 1),
            [VMEM] * (1 + n_row),
            **forward,
        )(near, features, *gathered)
        parts = exchange(sends, "col", True)
    (far,) = call(
        functools.partial(turn_kernel, side),
        [((across, down), NARROW)],
        [VMEM],
        need=3 * dense_bytes,
    )(near)

    results = [((nodes, width), jnp.float32), ((stacked, width), NARROW)] + [message] * (n_row - 1)
    if sides:
        sent, pre, act = call(
            middle_layer_kernel,
            [
                ((2 * nodes + stacked, width), NARROW),
                ((nodes, hidden), jnp.float32),
                ((nodes, hidden), NARROW),
            ],
            [VMEM] * 7,
            flops=28 * nodes * width * hidden,
            after=[far],
        )(own, *parts, weight, cotangent, ends)
        beyond = send(sent, "col", [(2, 0), (1, 3)])
        spread = [send(sent, "col", outward), send(sent, "col", swapped), beyond]
        (act,) = call(choose_kernel, [((nodes, hidden), NARROW)], [VMEM] * 2)(
            pre, send(act, "col", outward)
        )
        own, kept, *sends = call(
            middle_backward_kernel, results, [VMEM] * 5, **forward
        )(far, sent, *spread)
    else:
        sent, pre = call(
            layer_kernel,
            [message, ((nodes, hidden), jnp.float32)],
            [VMEM] * (n_col + 2),
            flops=14 * nodes * width * hidden,
            after=[far],
        )(own, *parts, weight, cotangent)
        spread = exchange([sent] * (n_col - 1), "col", False)
        (act,) = call(act_kernel, [((nodes, hidden), NARROW)], [VMEM])(pre)
        own, kept, *sends = call(
            functools.partial(backward_kernel, n_col), results, [VMEM] * (1 + n_col), **forward
        )(far, sent, *spread)
    parts = exchange(sends, "row", True)

    scale = float(nodes * n_row * n_col) ** -0.5
    grad_features, grad_weight = call(
        functools.partial(last_kernel, scale),
        [((nodes, width), NARROW), ((width, hidden), jnp.float32)],
        [VMEM] * (n_row + 1),
    )(own, kept, *parts)
    return act, grad_features, grad_weight


def solution(mesh):
    placed = (
        P(("groups", "row", "col"), None),
        P(),
        P(("groups", "row", "col"), None),
        P(("groups", "row"), "col", None, None, None),
        P(("groups", "row"), "col", None),
        P(("groups", "row"), "col", None),
        P(("groups", "row"), "col"),
    )
    return jax.shard_map(
        per_device,
        mesh=mesh,
        in_specs=placed,
        out_specs=(
            P(("groups", "row", "col"), None),
            P(("groups", "row", "col"), None),
            P("groups", None),
        ),
        check_vma=False,
    )
```

```python
import functools

import jax
import jax.numpy as jnp
from jax import lax
from jax.experimental import pallas as pl
from jax.experimental.pallas import tpu as pltpu
from jax.sharding import PartitionSpec as P

VMEM = pl.BlockSpec(memory_space=pltpu.VMEM)
ANY = pl.BlockSpec(memory_space=pl.ANY)
LEAST = 16 * 1024 * 1024
NARROW = jnp.bfloat16


def call(kernel, outs, in_specs, scratch=(), flops=0, need=0, after=()):
    outs = tuple(jax.ShapeDtypeStruct(shape, dtype) for shape, dtype in outs)
    late = len(after)
    run = pl.pallas_call(
        (lambda *refs: kernel(*refs[late:])) if late else kernel,
        out_shape=outs,
        in_specs=[ANY] * late + list(in_specs),
        out_specs=(VMEM,) * len(outs),
        scratch_shapes=scratch,
        compiler_params=pltpu.CompilerParams(vmem_limit_bytes=LEAST + need),
        cost_estimate=pl.CostEstimate(flops=flops, bytes_accessed=need, transcendentals=0),
    )
    return functools.partial(run, *after)


def exchange(sends, axis, ahead):
    n = lax.axis_size(axis)
    return [
        lax.ppermute(send, axis, [(s, (s + (d if ahead else -d)) % n) for s in range(n)])
        for d, send in enumerate(sends, 1)
    ]


def meet(own, axis):
    n = lax.axis_size(axis)
    return [own] + [
        lax.ppermute(own, axis, [(s, s ^ d) for s in range(n)]) for d in range(n - 1, 0, -1)
    ]


def wide(value):
    return value.astype(jnp.float32)


def split(value):
    high = value.astype(NARROW)
    return high, (value - wide(high)).astype(NARROW)


def dot(left, right, dims=((1,), (0,))):
    return lax.dot_general(left, right, (dims, ((), ())), preferred_element_type=jnp.float32)


def dense_kernel(n_row, n_col, piece, vals, rows_in, cols_in, count_in, near, rows, cols, count, sems):
    copies = [
        pltpu.make_async_copy(source, target, sems.at[k])
        for k, (source, target) in enumerate(((rows_in, rows), (cols_in, cols), (count_in, count)))
    ]
    for copy in copies:
        copy.start()
    my_row, my_col = lax.axis_index("row"), lax.axis_index("col")
    side = vals.shape[-1]
    near[...] = jnp.zeros_like(near)
    for copy in copies:
        copy.wait()

    def add(t, _):
        row, col = rows[0, 0, t], cols[0, 0, t]
        row = lax.rem(row // piece - my_col + n_col, n_col) * piece + lax.rem(row, piece)
        place = lax.rem(n_row - ((col // piece) ^ my_row), n_row)
        col = place * piece + lax.rem(col, piece)
        down = pl.ds(pl.multiple_of(row * side, side), side)
        across = pl.ds(pl.multiple_of(col * side, side), side)
        near[down, across] = vals[0, 0, t]
        return 0

    lax.fori_loop(0, count[0, 0], add, 0)


def turn_kernel(step, near, far):
    def turn(k, _):
        band = pl.ds(pl.multiple_of(k * step, step), step)
        far[:, band] = near[band, :].T
        return 0

    lax.fori_loop(0, near.shape[0] // step, turn, 0)


def tree(terms):
    while len(terms) > 1:
        middle = len(terms) // 2
        terms = [left + right for left, right in zip(terms[:middle], terms[middle:])]
    return terms[0]


def forward_kernel(n, matrix, *refs):
    operands, own, sends = refs[:n], refs[n], refs[n + 1 :]
    rows = own.shape[0]
    stacked = jnp.concatenate([operand[...] for operand in operands], axis=0)
    product = dot(matrix[...], stacked)
    own[...] = product[:rows]
    for d, send in enumerate(sends, 1):
        send[...] = product[d * rows : (d + 1) * rows].astype(send.dtype)


def layer_kernel(*refs):
    *parts, weight, cotangent, message, pre_out = refs
    nodes = cotangent.shape[0]
    total = tree([wide(part[...]) for part in parts])
    high, low = split(total)
    pre = dot(high, weight[...]) + dot(low, weight[...])
    pre_out[...] = pre
    sigma = jax.nn.sigmoid(pre)
    grad = wide(cotangent[...]) * sigma * (1.0 + pre * (1.0 - sigma))
    grad_high, grad_low = split(grad)
    across = ((1,), (1,))
    back = dot(grad_high, weight[...], across) + dot(grad_low, weight[...], across)
    message[:nodes] = back.astype(message.dtype)
    down = ((0,), (0,))
    term = dot(high, grad_high, down) + dot(low, grad_high, down) + dot(high, grad_low, down)
    half = message.shape[1]
    rows = total.shape[1]
    for k in range(term.shape[1] // half):
        start = nodes + k * rows
        message[start : start + rows] = term[:, k * half : (k + 1) * half].astype(message.dtype)


def act_kernel(pre, act):
    act[...] = (pre[...] * jax.nn.sigmoid(pre[...])).astype(act.dtype)


def backward_kernel(n, n_out, matrix, *refs):
    messages, out = refs[:n], refs[n]
    rows = matrix.shape[0] // n_out
    size = messages[0].shape[0]
    stacked = jnp.concatenate([message[:rows] for message in messages], axis=0)
    product = dot(matrix[...], stacked)
    term = tree([wide(message[rows:]) for message in messages]).astype(out.dtype)
    my_row = lax.axis_index("row")
    for d in range(n_out):
        start = pl.multiple_of((my_row ^ ((n_out - d) % n_out)) * size, size)
        out[pl.ds(start, rows)] = product[d * rows : (d + 1) * rows].astype(out.dtype)
        out[pl.ds(pl.multiple_of(start + rows, rows), size - rows)] = term


def last_kernel(n, scale, messages, features_out, weight_out):
    size = messages.shape[0] // n
    nodes, rows = features_out.shape[0], weight_out.shape[0]
    half = messages.shape[1]
    total = tree([wide(messages[k * size : (k + 1) * size]) for k in range(n)])
    features_out[...] = total[:nodes].astype(features_out.dtype)
    for k in range(weight_out.shape[1] // half):
        start = nodes + k * rows
        weight_out[:, k * half : (k + 1) * half] = total[start : start + rows] * scale


def per_device(features, weight, cotangent, tile_values, tile_rows, tile_cols, tile_count):
    slots, side = tile_values.shape[2:4]
    n_row, n_col = lax.axis_size("row"), lax.axis_size("col")
    nodes, width = features.shape
    hidden = weight.shape[1]
    down, across = n_col * nodes, n_row * nodes
    dense_bytes = 2 * down * across

    gathered = meet(features, "row")
    (near,) = call(
        functools.partial(dense_kernel, n_row, n_col, nodes // side),
        [((down, across), NARROW)],
        [VMEM] * 4,
        scratch=[
            pltpu.SMEM(tile_rows.shape, jnp.int32),
            pltpu.SMEM(tile_cols.shape, jnp.int32),
            pltpu.SMEM(tile_count.shape, jnp.int32),
            pltpu.SemaphoreType.DMA((3,)),
        ],
        need=2 * dense_bytes,
    )(tile_values, tile_rows, tile_cols, tile_count)

    own, *sends = call(
        functools.partial(forward_kernel, n_row),
        [((nodes, width), jnp.float32)] + [((nodes, width), NARROW)] * (n_col - 1),
        [VMEM] * (1 + n_row),
        flops=2 * down * across * width,
        need=2 * dense_bytes,
    )(near, *gathered)
    parts = exchange(sends, "col", True)
    (far,) = call(
        functools.partial(turn_kernel, side),
        [((across, down), NARROW)],
        [VMEM],
        need=3 * dense_bytes,
    )(near)

    stacked = hidden // width * width
    message = ((nodes + stacked, width), NARROW)
    sent, pre = call(
        layer_kernel,
        [message, ((nodes, hidden), jnp.float32)],
        [VMEM] * (n_col + 2),
        flops=14 * nodes * width * hidden,
        after=[far],
    )(own, *parts, weight, cotangent)
    spread = exchange([sent] * (n_col - 1), "col", False)
    (act,) = call(act_kernel, [((nodes, hidden), NARROW)], [VMEM])(pre)

    (sends,) = call(
        functools.partial(backward_kernel, n_col, n_row),
        [((n_row * message[0][0], width), NARROW)],
        [VMEM] * (1 + n_col),
        flops=2 * down * across * width,
        need=2 * dense_bytes,
    )(far, sent, *spread)
    parts = lax.all_to_all(sends, "row", 0, 0, tiled=True)

    scale = float(nodes * n_row * n_col) ** -0.5
    grad_features, grad_weight = call(
        functools.partial(last_kernel, n_row, scale),
        [((nodes, width), NARROW), ((width, hidden), jnp.float32)],
        [VMEM],
    )(parts)
    return act, grad_features, grad_weight


def solution(mesh):
    placed = (
        P(("groups", "row", "col"), None),
        P(),
        P(("groups", "row", "col"), None),
        P(("groups", "row"), "col", None, None, None),
        P(("groups", "row"), "col", None),
        P(("groups", "row"), "col", None),
        P(("groups", "row"), "col"),
    )
    return jax.shard_map(
        per_device,
        mesh=mesh,
        in_specs=placed,
        out_specs=(
            P(("groups", "row", "col"), None),
            P(("groups", "row", "col"), None),
            P("groups", None),
        ),
        check_vma=False,
    )
```

```python
import functools

import jax
import jax.numpy as jnp
from jax import lax
from jax.experimental import pallas as pl
from jax.experimental.pallas import tpu as pltpu
from jax.sharding import PartitionSpec as P

VMEM = pl.BlockSpec(memory_space=pltpu.VMEM)
ANY = pl.BlockSpec(memory_space=pl.ANY)
LEAST = 16 * 1024 * 1024
NARROW = jnp.bfloat16


def call(kernel, outs, in_specs, scratch=(), flops=0, need=0, after=()):
    outs = tuple(jax.ShapeDtypeStruct(shape, dtype) for shape, dtype in outs)
    late = len(after)
    run = pl.pallas_call(
        (lambda *refs: kernel(*refs[late:])) if late else kernel,
        out_shape=outs,
        in_specs=[ANY] * late + list(in_specs),
        out_specs=(VMEM,) * len(outs),
        scratch_shapes=scratch,
        compiler_params=pltpu.CompilerParams(vmem_limit_bytes=LEAST + need),
        cost_estimate=pl.CostEstimate(flops=flops, bytes_accessed=need, transcendentals=0),
    )
    return functools.partial(run, *after)


def exchange(sends, axis, ahead):
    n = lax.axis_size(axis)
    return [
        lax.ppermute(send, axis, [(s, (s + (d if ahead else -d)) % n) for s in range(n)])
        for d, send in enumerate(sends, 1)
    ]


def neighbour(value, axis):
    n = lax.axis_size(axis)
    return lax.ppermute(value, axis, [(s, s ^ 1) for s in range(n)])


def wide(value):
    return value.astype(jnp.float32)


def split(value):
    high = value.astype(NARROW)
    return high, (value - wide(high)).astype(NARROW)


def dot(left, right, dims=((1,), (0,))):
    return lax.dot_general(left, right, (dims, ((), ())), preferred_element_type=jnp.float32)


def dense_kernel(n_row, n_col, piece, vals, rows_in, cols_in, count_in, near, rows, cols, count, sems):
    copies = [
        pltpu.make_async_copy(source, target, sems.at[k])
        for k, (source, target) in enumerate(((rows_in, rows), (cols_in, cols), (count_in, count)))
    ]
    for copy in copies:
        copy.start()
    my_row, my_col = lax.axis_index("row"), lax.axis_index("col")
    side = vals.shape[-1]
    near[...] = jnp.zeros_like(near)
    for copy in copies:
        copy.wait()

    def add(t, _):
        row, col = rows[0, 0, t], cols[0, 0, t]
        row = lax.rem(row // piece - my_col + n_col, n_col) * piece + lax.rem(row, piece)
        col = lax.rem(col // piece - my_row + n_row, n_row) * piece + lax.rem(col, piece)
        down = pl.ds(pl.multiple_of(row * side, side), side)
        across = pl.ds(pl.multiple_of(col * side, side), side)
        near[down, across] = vals[0, 0, t]
        return 0

    lax.fori_loop(0, count[0, 0], add, 0)


def turn_kernel(step, near, far):
    def turn(k, _):
        band = pl.ds(pl.multiple_of(k * step, step), step)
        far[:, band] = near[band, :].T
        return 0

    lax.fori_loop(0, near.shape[0] // step, turn, 0)


def tree(terms):
    while len(terms) > 1:
        middle = len(terms) // 2
        terms = [left + right for left, right in zip(terms[:middle], terms[middle:])]
    return terms[0]


def forward_kernel(n, matrix, *refs):
    operands, own, sends = refs[:n], refs[n], refs[n + 1 :]
    rows = own.shape[0]
    stacked = jnp.concatenate([operand[...] for operand in operands], axis=0)
    product = dot(matrix[...], stacked)
    own[...] = product[:rows]
    for d, send in enumerate(sends, 1):
        send[...] = product[d * rows : (d + 1) * rows].astype(send.dtype)


def layer_kernel(*refs):
    *parts, weight, cotangent, back, mine, other, pre_out = refs
    half = mine.shape[1]
    total = tree([wide(part[...]) for part in parts])
    high, low = split(total)
    pre = dot(high, weight[...]) + dot(low, weight[...])
    pre_out[...] = pre
    sigma = jax.nn.sigmoid(pre)
    grad = wide(cotangent[...]) * sigma * (1.0 + pre * (1.0 - sigma))
    grad_high, grad_low = split(grad)
    down = ((0,), (0,))
    term = dot(high, grad_high, down) + dot(low, grad_high, down) + dot(high, grad_low, down)
    odd = lax.rem(lax.axis_index("row"), 2) == 1
    left, right = term[:, :half], term[:, half:]
    mine[...] = jnp.where(odd, right, left)
    other[...] = jnp.where(odd, left, right).astype(other.dtype)
    across = ((1,), (1,))
    back[...] = (dot(grad_high, weight[...], across) + dot(grad_low, weight[...], across)).astype(
        back.dtype
    )


def message_kernel(back, mine, came, message):
    nodes = back.shape[0]
    message[:nodes] = back[...]
    message[nodes:] = (mine[...] + wide(came[...])).astype(message.dtype)


def act_kernel(pre, act):
    act[...] = (pre[...] * jax.nn.sigmoid(pre[...])).astype(act.dtype)


def backward_kernel(n, matrix, *refs):
    messages, own, kept, sends = refs[:n], refs[n], refs[n + 1], refs[n + 2 :]
    rows = own.shape[0]
    stacked = jnp.concatenate([message[:rows] for message in messages], axis=0)
    product = dot(matrix[...], stacked)
    own[...] = product[:rows]
    term = tree([wide(message[rows:]) for message in messages]).astype(kept.dtype)
    kept[...] = term
    for d, send in enumerate(sends, 1):
        send[:rows] = product[d * rows : (d + 1) * rows].astype(send.dtype)
        send[rows:] = term


def last_kernel(scale, own, kept, *refs):
    *messages, features_out, weight_out = refs
    nodes, half = own.shape[0], kept.shape[1]
    features_out[...] = tree(
        [own[...]] + [wide(message[:nodes]) for message in messages]
    ).astype(features_out.dtype)
    terms = [wide(kept[...])] + [wide(message[nodes:]) for message in messages]
    mine, other = tree(terms[::2]) * scale, tree(terms[1::2]) * scale
    odd = lax.rem(lax.axis_index("row"), 2) == 1
    weight_out[:, :half] = jnp.where(odd, other, mine)
    weight_out[:, half:] = jnp.where(odd, mine, other)


def per_device(features, weight, cotangent, tile_values, tile_rows, tile_cols, tile_count):
    slots, side = tile_values.shape[2:4]
    n_row, n_col = lax.axis_size("row"), lax.axis_size("col")
    nodes, width = features.shape
    hidden = weight.shape[1]
    down, across = n_col * nodes, n_row * nodes
    dense_bytes = 2 * down * across

    gathered = exchange([features] * (n_row - 1), "row", False)
    (near,) = call(
        functools.partial(dense_kernel, n_row, n_col, nodes // side),
        [((down, across), NARROW)],
        [VMEM] * 4,
        scratch=[
            pltpu.SMEM(tile_rows.shape, jnp.int32),
            pltpu.SMEM(tile_cols.shape, jnp.int32),
            pltpu.SMEM(tile_count.shape, jnp.int32),
            pltpu.SemaphoreType.DMA((3,)),
        ],
        need=2 * dense_bytes,
    )(tile_values, tile_rows, tile_cols, tile_count)

    own, *sends = call(
        functools.partial(forward_kernel, n_row),
        [((nodes, width), jnp.float32)] + [((nodes, width), NARROW)] * (n_col - 1),
        [VMEM] * (1 + n_row),
        flops=2 * down * across * width,
        need=2 * dense_bytes,
    )(near, features, *gathered)
    parts = exchange(sends, "col", True)
    (far,) = call(
        functools.partial(turn_kernel, side),
        [((across, down), NARROW)],
        [VMEM],
        need=3 * dense_bytes,
    )(near)

    half = hidden // 2
    square = (width, half)
    message = ((nodes + width, width), NARROW)
    back, mine, other, pre = call(
        layer_kernel,
        [
            ((nodes, width), NARROW),
            (square, jnp.float32),
            (square, NARROW),
            ((nodes, hidden), jnp.float32),
        ],
        [VMEM] * (n_col + 2),
        flops=14 * nodes * width * hidden,
        after=[far],
    )(own, *parts, weight, cotangent)
    (sent,) = call(message_kernel, [message], [VMEM] * 3)(back, mine, neighbour(other, "row"))
    spread = exchange([sent] * (n_col - 1), "col", False)
    (act,) = call(act_kernel, [((nodes, hidden), NARROW)], [VMEM])(pre)

    own, kept, *sends = call(
        functools.partial(backward_kernel, n_col),
        [((nodes, width), jnp.float32), (square, NARROW)] + [message] * (n_row - 1),
        [VMEM] * (1 + n_col),
        flops=2 * down * across * width,
        need=2 * dense_bytes,
    )(far, sent, *spread)
    parts = exchange(sends, "row", True)

    scale = float(nodes * n_row * n_col) ** -0.5
    grad_features, grad_weight = call(
        functools.partial(last_kernel, scale),
        [((nodes, width), NARROW), ((width, hidden), jnp.float32)],
        [VMEM] * (n_row + 1),
    )(own, kept, *parts)
    return act, grad_features, grad_weight


def solution(mesh):
    placed = (
        P(("groups", "row", "col"), None),
        P(),
        P(("groups", "row", "col"), None),
        P(("groups", "row"), "col", None, None, None),
        P(("groups", "row"), "col", None),
        P(("groups", "row"), "col", None),
        P(("groups", "row"), "col"),
    )
    return jax.shard_map(
        per_device,
        mesh=mesh,
        in_specs=placed,
        out_specs=(
            P(("groups", "row", "col"), None),
            P(("groups", "row", "col"), None),
            P("groups", None),
        ),
        check_vma=False,
    )
```

```python
import functools

import jax
import jax.numpy as jnp
from jax import lax
from jax.experimental import pallas as pl
from jax.experimental.pallas import tpu as pltpu
from jax.sharding import PartitionSpec as P

VMEM = pl.BlockSpec(memory_space=pltpu.VMEM)
ANY = pl.BlockSpec(memory_space=pl.ANY)
LEAST = 16 * 1024 * 1024
NARROW = jnp.bfloat16


def call(kernel, outs, in_specs, scratch=(), flops=0, need=0, after=()):
    outs = tuple(jax.ShapeDtypeStruct(shape, dtype) for shape, dtype in outs)
    late = len(after)
    run = pl.pallas_call(
        (lambda *refs: kernel(*refs[late:])) if late else kernel,
        out_shape=outs,
        in_specs=[ANY] * late + list(in_specs),
        out_specs=(VMEM,) * len(outs),
        scratch_shapes=scratch,
        compiler_params=pltpu.CompilerParams(vmem_limit_bytes=LEAST + need),
        cost_estimate=pl.CostEstimate(flops=flops, bytes_accessed=need, transcendentals=0),
    )
    return functools.partial(run, *after)


def exchange(sends, axis, ahead):
    n = lax.axis_size(axis)
    return [
        lax.ppermute(send, axis, [(s, (s + (d if ahead else -d)) % n) for s in range(n)])
        for d, send in enumerate(sends, 1)
    ]


def far_first(n, ahead):
    return sorted(range(1, n), key=lambda d: (-min(d, n - d), d if ahead else -d))


def in_order(arrays, offsets):
    return [array for _, array in sorted(zip(offsets, arrays), key=lambda pair: pair[0])]


def neighbour(value, axis):
    n = lax.axis_size(axis)
    return lax.ppermute(value, axis, [(s, s ^ 1) for s in range(n)])


def wide(value):
    return value.astype(jnp.float32)


def split(value):
    high = value.astype(NARROW)
    return high, (value - wide(high)).astype(NARROW)


def dot(left, right, dims=((1,), (0,))):
    return lax.dot_general(left, right, (dims, ((), ())), preferred_element_type=jnp.float32)


def dense_kernel(n_row, n_col, piece, vals, rows_in, cols_in, count_in, near, rows, cols, count, sems):
    copies = [
        pltpu.make_async_copy(source, target, sems.at[k])
        for k, (source, target) in enumerate(((rows_in, rows), (cols_in, cols), (count_in, count)))
    ]
    for copy in copies:
        copy.start()
    my_row, my_col = lax.axis_index("row"), lax.axis_index("col")
    side = vals.shape[-1]
    near[...] = jnp.zeros_like(near)
    for copy in copies:
        copy.wait()

    def add(t, _):
        row, col = rows[0, 0, t], cols[0, 0, t]
        row = lax.rem(row // piece - my_col + n_col, n_col) * piece + lax.rem(row, piece)
        col = lax.rem(col // piece - my_row + n_row, n_row) * piece + lax.rem(col, piece)
        down = pl.ds(pl.multiple_of(row * side, side), side)
        across = pl.ds(pl.multiple_of(col * side, side), side)
        near[down, across] = vals[0, 0, t]
        return 0

    lax.fori_loop(0, count[0, 0], add, 0)


def turn_kernel(step, near, far):
    def turn(k, _):
        band = pl.ds(pl.multiple_of(k * step, step), step)
        far[:, band] = near[band, :].T
        return 0

    lax.fori_loop(0, near.shape[0] // step, turn, 0)


def tree(terms):
    while len(terms) > 1:
        middle = len(terms) // 2
        terms = [left + right for left, right in zip(terms[:middle], terms[middle:])]
    return terms[0]


def forward_kernel(n, matrix, *refs):
    operands, own, sends = refs[:n], refs[n], refs[n + 1 :]
    rows = own.shape[0]
    stacked = jnp.concatenate([operand[...] for operand in operands], axis=0)
    product = dot(matrix[...], stacked)
    own[...] = product[:rows]
    for d, send in enumerate(sends, 1):
        send[...] = product[d * rows : (d + 1) * rows].astype(send.dtype)


def layer_kernel(*refs):
    own, *parts, weight, cotangent, back, mine, other, pre_out = refs
    parts = [own] + in_order(parts, far_first(len(parts) + 1, True))
    half = mine.shape[1]
    total = tree([wide(part[...]) for part in parts])
    high, low = split(total)
    pre = dot(high, weight[...]) + dot(low, weight[...])
    pre_out[...] = pre
    sigma = jax.nn.sigmoid(pre)
    grad = wide(cotangent[...]) * sigma * (1.0 + pre * (1.0 - sigma))
    grad_high, grad_low = split(grad)
    down = ((0,), (0,))
    term = dot(high, grad_high, down) + dot(low, grad_high, down) + dot(high, grad_low, down)
    odd = lax.rem(lax.axis_index("row"), 2) == 1
    left, right = term[:, :half], term[:, half:]
    mine[...] = jnp.where(odd, right, left)
    other[...] = jnp.where(odd, left, right).astype(other.dtype)
    across = ((1,), (1,))
    back[...] = (dot(grad_high, weight[...], across) + dot(grad_low, weight[...], across)).astype(
        back.dtype
    )


def message_kernel(back, mine, came, message):
    nodes = back.shape[0]
    message[:nodes] = back[...]
    message[nodes:] = (mine[...] + wide(came[...])).astype(message.dtype)


def act_kernel(pre, act):
    act[...] = (pre[...] * jax.nn.sigmoid(pre[...])).astype(act.dtype)


def backward_kernel(n, matrix, *refs):
    messages, own, kept, sends = refs[:n], refs[n], refs[n + 1], refs[n + 2 :]
    messages = messages[:1] + tuple(in_order(messages[1:], far_first(n, False)[::-1]))
    rows = own.shape[0]
    stacked = jnp.concatenate([message[:rows] for message in messages], axis=0)
    product = dot(matrix[...], stacked)
    own[...] = product[:rows]
    term = tree([wide(message[rows:]) for message in messages]).astype(kept.dtype)
    kept[...] = term
    for d, send in enumerate(sends, 1):
        send[:rows] = product[d * rows : (d + 1) * rows].astype(send.dtype)
        send[rows:] = term


def last_kernel(scale, own, kept, *refs):
    *messages, features_out, weight_out = refs
    nodes, half = own.shape[0], kept.shape[1]
    features_out[...] = tree(
        [own[...]] + [wide(message[:nodes]) for message in messages]
    ).astype(features_out.dtype)
    terms = [wide(kept[...])] + [wide(message[nodes:]) for message in messages]
    mine, other = tree(terms[::2]) * scale, tree(terms[1::2]) * scale
    odd = lax.rem(lax.axis_index("row"), 2) == 1
    weight_out[:, :half] = jnp.where(odd, other, mine)
    weight_out[:, half:] = jnp.where(odd, mine, other)


def per_device(features, weight, cotangent, tile_values, tile_rows, tile_cols, tile_count):
    slots, side = tile_values.shape[2:4]
    n_row, n_col = lax.axis_size("row"), lax.axis_size("col")
    nodes, width = features.shape
    hidden = weight.shape[1]
    down, across = n_col * nodes, n_row * nodes
    dense_bytes = 2 * down * across

    gathered = exchange([features] * (n_row - 1), "row", False)
    (near,) = call(
        functools.partial(dense_kernel, n_row, n_col, nodes // side),
        [((down, across), NARROW)],
        [VMEM] * 4,
        scratch=[
            pltpu.SMEM(tile_rows.shape, jnp.int32),
            pltpu.SMEM(tile_cols.shape, jnp.int32),
            pltpu.SMEM(tile_count.shape, jnp.int32),
            pltpu.SemaphoreType.DMA((3,)),
        ],
        need=2 * dense_bytes,
    )(tile_values, tile_rows, tile_cols, tile_count)

    own, *sends = call(
        functools.partial(forward_kernel, n_row),
        [((nodes, width), jnp.float32)] + [((nodes, width), NARROW)] * (n_col - 1),
        [VMEM] * (1 + n_row),
        flops=2 * down * across * width,
        need=2 * dense_bytes,
    )(near, features, *gathered)
    parts = exchange(sends, "col", True)
    (far,) = call(
        functools.partial(turn_kernel, side),
        [((across, down), NARROW)],
        [VMEM],
        need=3 * dense_bytes,
    )(near)

    half = hidden // 2
    square = (width, half)
    message = ((nodes + width, width), NARROW)
    back, mine, other, pre = call(
        layer_kernel,
        [
            ((nodes, width), NARROW),
            (square, jnp.float32),
            (square, NARROW),
            ((nodes, hidden), jnp.float32),
        ],
        [VMEM] * (n_col + 2),
        flops=14 * nodes * width * hidden,
        after=[far],
    )(own, *[parts[d - 1] for d in far_first(n_col, True)], weight, cotangent)
    (sent,) = call(message_kernel, [message], [VMEM] * 3)(back, mine, neighbour(other, "row"))
    spread = exchange([sent] * (n_col - 1), "col", False)
    (act,) = call(act_kernel, [((nodes, hidden), NARROW)], [VMEM])(pre)

    own, kept, *sends = call(
        functools.partial(backward_kernel, n_col),
        [((nodes, width), jnp.float32), (square, NARROW)] + [message] * (n_row - 1),
        [VMEM] * (1 + n_col),
        flops=2 * down * across * width,
        need=2 * dense_bytes,
    )(far, sent, *[spread[d - 1] for d in far_first(n_col, False)[::-1]])
    parts = exchange(sends, "row", True)

    scale = float(nodes * n_row * n_col) ** -0.5
    grad_features, grad_weight = call(
        functools.partial(last_kernel, scale),
        [((nodes, width), NARROW), ((width, hidden), jnp.float32)],
        [VMEM] * (n_row + 1),
    )(own, kept, *parts)
    return act, grad_features, grad_weight


def solution(mesh):
    placed = (
        P(("groups", "row", "col"), None),
        P(),
        P(("groups", "row", "col"), None),
        P(("groups", "row"), "col", None, None, None),
        P(("groups", "row"), "col", None),
        P(("groups", "row"), "col", None),
        P(("groups", "row"), "col"),
    )
    return jax.shard_map(
        per_device,
        mesh=mesh,
        in_specs=placed,
        out_specs=(
            P(("groups", "row", "col"), None),
            P(("groups", "row", "col"), None),
            P("groups", None),
        ),
        check_vma=False,
    )
```

```python
import functools

import jax
import jax.numpy as jnp
from jax import lax
from jax.experimental import pallas as pl
from jax.experimental.pallas import tpu as pltpu
from jax.sharding import PartitionSpec as P

VMEM = pl.BlockSpec(memory_space=pltpu.VMEM)
ANY = pl.BlockSpec(memory_space=pl.ANY)
LEAST = 16 * 1024 * 1024
NARROW = jnp.bfloat16


def call(kernel, outs, in_specs, scratch=(), flops=0, need=0, after=()):
    outs = tuple(jax.ShapeDtypeStruct(shape, dtype) for shape, dtype in outs)
    late = len(after)
    run = pl.pallas_call(
        (lambda *refs: kernel(*refs[late:])) if late else kernel,
        out_shape=outs,
        in_specs=[ANY] * late + list(in_specs),
        out_specs=(VMEM,) * len(outs),
        scratch_shapes=scratch,
        compiler_params=pltpu.CompilerParams(vmem_limit_bytes=LEAST + need),
        cost_estimate=pl.CostEstimate(flops=flops, bytes_accessed=need, transcendentals=0),
    )
    return functools.partial(run, *after)


def ring_place(k, n):
    return k ^ (k >> 1) if n == 4 else k


def exchange(sends, axis, ahead):
    n = lax.axis_size(axis)

    def target(s, d):
        return ring_place((ring_place(s, n) + (d if ahead else -d)) % n, n)

    return [
        lax.ppermute(send, axis, [(s, target(s, d)) for s in range(n)])
        for d, send in enumerate(sends, 1)
    ]


def odd_row():
    return lax.rem(ring_place(lax.axis_index("row"), lax.axis_size("row")), 2) == 1


def neighbour(value, axis):
    n = lax.axis_size(axis)
    return lax.ppermute(value, axis, [(s, s ^ 1) for s in range(n)])


def wide(value):
    return value.astype(jnp.float32)


def split(value):
    high = value.astype(NARROW)
    return high, (value - wide(high)).astype(NARROW)


def dot(left, right, dims=((1,), (0,))):
    return lax.dot_general(left, right, (dims, ((), ())), preferred_element_type=jnp.float32)


def dense_kernel(n_row, n_col, piece, vals, rows_in, cols_in, count_in, near, rows, cols, count, sems):
    copies = [
        pltpu.make_async_copy(source, target, sems.at[k])
        for k, (source, target) in enumerate(((rows_in, rows), (cols_in, cols), (count_in, count)))
    ]
    for copy in copies:
        copy.start()
    my_row, my_col = lax.axis_index("row"), lax.axis_index("col")
    side = vals.shape[-1]
    near[...] = jnp.zeros_like(near)
    for copy in copies:
        copy.wait()

    def ahead(there, here, n):
        return lax.rem(ring_place(there, n) - ring_place(here, n) + n, n)

    def add(t, _):
        row, col = rows[0, 0, t], cols[0, 0, t]
        row = ahead(row // piece, my_col, n_col) * piece + lax.rem(row, piece)
        col = ahead(col // piece, my_row, n_row) * piece + lax.rem(col, piece)
        down = pl.ds(pl.multiple_of(row * side, side), side)
        across = pl.ds(pl.multiple_of(col * side, side), side)
        near[down, across] = vals[0, 0, t]
        return 0

    lax.fori_loop(0, count[0, 0], add, 0)


def turn_kernel(step, near, far):
    def turn(k, _):
        band = pl.ds(pl.multiple_of(k * step, step), step)
        far[:, band] = near[band, :].T
        return 0

    lax.fori_loop(0, near.shape[0] // step, turn, 0)


def tree(terms):
    while len(terms) > 1:
        middle = len(terms) // 2
        terms = [left + right for left, right in zip(terms[:middle], terms[middle:])]
    return terms[0]


def forward_kernel(n, matrix, *refs):
    operands, own, sends = refs[:n], refs[n], refs[n + 1 :]
    rows = own.shape[0]
    stacked = jnp.concatenate([operand[...] for operand in operands], axis=0)
    product = dot(matrix[...], stacked)
    own[...] = product[:rows]
    for d, send in enumerate(sends, 1):
        send[...] = product[d * rows : (d + 1) * rows].astype(send.dtype)


def layer_kernel(*refs):
    *parts, weight, cotangent, back, mine, other, pre_out = refs
    half = mine.shape[1]
    total = tree([wide(part[...]) for part in parts])
    high, low = split(total)
    pre = dot(high, weight[...]) + dot(low, weight[...])
    pre_out[...] = pre
    sigma = jax.nn.sigmoid(pre)
    grad = wide(cotangent[...]) * sigma * (1.0 + pre * (1.0 - sigma))
    grad_high, grad_low = split(grad)
    down = ((0,), (0,))
    term = dot(high, grad_high, down) + dot(low, grad_high, down) + dot(high, grad_low, down)
    odd = odd_row()
    left, right = term[:, :half], term[:, half:]
    mine[...] = jnp.where(odd, right, left)
    other[...] = jnp.where(odd, left, right).astype(other.dtype)
    across = ((1,), (1,))
    back[...] = (dot(grad_high, weight[...], across) + dot(grad_low, weight[...], across)).astype(
        back.dtype
    )


def message_kernel(back, mine, came, message):
    nodes = back.shape[0]
    message[:nodes] = back[...]
    message[nodes:] = (mine[...] + wide(came[...])).astype(message.dtype)


def act_kernel(pre, act):
    act[...] = (pre[...] * jax.nn.sigmoid(pre[...])).astype(act.dtype)


def backward_kernel(n, matrix, *refs):
    messages, own, kept, sends = refs[:n], refs[n], refs[n + 1], refs[n + 2 :]
    rows = own.shape[0]
    stacked = jnp.concatenate([message[:rows] for message in messages], axis=0)
    product = dot(matrix[...], stacked)
    own[...] = product[:rows]
    term = tree([wide(message[rows:]) for message in messages]).astype(kept.dtype)
    kept[...] = term
    for d, send in enumerate(sends, 1):
        send[:rows] = product[d * rows : (d + 1) * rows].astype(send.dtype)
        send[rows:] = term


def last_kernel(scale, own, kept, *refs):
    *messages, features_out, weight_out = refs
    nodes, half = own.shape[0], kept.shape[1]
    features_out[...] = tree(
        [own[...]] + [wide(message[:nodes]) for message in messages]
    ).astype(features_out.dtype)
    terms = [wide(kept[...])] + [wide(message[nodes:]) for message in messages]
    mine, other = tree(terms[::2]) * scale, tree(terms[1::2]) * scale
    odd = odd_row()
    weight_out[:, :half] = jnp.where(odd, other, mine)
    weight_out[:, half:] = jnp.where(odd, mine, other)


def per_device(features, weight, cotangent, tile_values, tile_rows, tile_cols, tile_count):
    slots, side = tile_values.shape[2:4]
    n_row, n_col = lax.axis_size("row"), lax.axis_size("col")
    nodes, width = features.shape
    hidden = weight.shape[1]
    down, across = n_col * nodes, n_row * nodes
    dense_bytes = 2 * down * across

    gathered = exchange([features] * (n_row - 1), "row", False)
    (near,) = call(
        functools.partial(dense_kernel, n_row, n_col, nodes // side),
        [((down, across), NARROW)],
        [VMEM] * 4,
        scratch=[
            pltpu.SMEM(tile_rows.shape, jnp.int32),
            pltpu.SMEM(tile_cols.shape, jnp.int32),
            pltpu.SMEM(tile_count.shape, jnp.int32),
            pltpu.SemaphoreType.DMA((3,)),
        ],
        need=2 * dense_bytes,
    )(tile_values, tile_rows, tile_cols, tile_count)

    own, *sends = call(
        functools.partial(forward_kernel, n_row),
        [((nodes, width), jnp.float32)] + [((nodes, width), NARROW)] * (n_col - 1),
        [VMEM] * (1 + n_row),
        flops=2 * down * across * width,
        need=2 * dense_bytes,
    )(near, features, *gathered)
    parts = exchange(sends, "col", True)
    (far,) = call(
        functools.partial(turn_kernel, side),
        [((across, down), NARROW)],
        [VMEM],
        need=3 * dense_bytes,
    )(near)

    half = hidden // 2
    square = (width, half)
    message = ((nodes + width, width), NARROW)
    back, mine, other, pre = call(
        layer_kernel,
        [
            ((nodes, width), NARROW),
            (square, jnp.float32),
            (square, NARROW),
            ((nodes, hidden), jnp.float32),
        ],
        [VMEM] * (n_col + 2),
        flops=14 * nodes * width * hidden,
        after=[far],
    )(own, *parts, weight, cotangent)
    (sent,) = call(message_kernel, [message], [VMEM] * 3)(back, mine, neighbour(other, "row"))
    spread = exchange([sent] * (n_col - 1), "col", False)
    (act,) = call(act_kernel, [((nodes, hidden), NARROW)], [VMEM])(pre)

    own, kept, *sends = call(
        functools.partial(backward_kernel, n_col),
        [((nodes, width), jnp.float32), (square, NARROW)] + [message] * (n_row - 1),
        [VMEM] * (1 + n_col),
        flops=2 * down * across * width,
        need=2 * dense_bytes,
    )(far, sent, *spread)
    parts = exchange(sends, "row", True)

    scale = float(nodes * n_row * n_col) ** -0.5
    grad_features, grad_weight = call(
        functools.partial(last_kernel, scale),
        [((nodes, width), NARROW), ((width, hidden), jnp.float32)],
        [VMEM] * (n_row + 1),
    )(own, kept, *parts)
    return act, grad_features, grad_weight


def solution(mesh):
    placed = (
        P(("groups", "row", "col"), None),
        P(),
        P(("groups", "row", "col"), None),
        P(("groups", "row"), "col", None, None, None),
        P(("groups", "row"), "col", None),
        P(("groups", "row"), "col", None),
        P(("groups", "row"), "col"),
    )
    return jax.shard_map(
        per_device,
        mesh=mesh,
        in_specs=placed,
        out_specs=(
            P(("groups", "row", "col"), None),
            P(("groups", "row", "col"), None),
            P("groups", None),
        ),
        check_vma=False,
    )
```

```python
import functools

import jax
import jax.numpy as jnp
from jax import lax
from jax.experimental import pallas as pl
from jax.experimental.pallas import tpu as pltpu
from jax.sharding import PartitionSpec as P

VMEM = pl.BlockSpec(memory_space=pltpu.VMEM)
ANY = pl.BlockSpec(memory_space=pl.ANY)
LEAST = 16 * 1024 * 1024
NARROW = jnp.bfloat16


def call(kernel, outs, in_specs, scratch=(), flops=0, need=0, after=()):
    outs = tuple(jax.ShapeDtypeStruct(shape, dtype) for shape, dtype in outs)
    late = len(after)
    run = pl.pallas_call(
        (lambda *refs: kernel(*refs[late:])) if late else kernel,
        out_shape=outs,
        in_specs=[ANY] * late + list(in_specs),
        out_specs=(VMEM,) * len(outs),
        scratch_shapes=scratch,
        compiler_params=pltpu.CompilerParams(vmem_limit_bytes=LEAST + need),
        cost_estimate=pl.CostEstimate(flops=flops, bytes_accessed=need, transcendentals=0),
    )
    return functools.partial(run, *after)


def ring_place(k, axis):
    return k ^ (k >> 1) if axis == "col" and lax.axis_size(axis) == 4 else k


def exchange(sends, axis, ahead):
    n = lax.axis_size(axis)

    def target(s, d):
        return ring_place((ring_place(s, axis) + (d if ahead else -d)) % n, axis)

    return [
        lax.ppermute(send, axis, [(s, target(s, d)) for s in range(n)])
        for d, send in enumerate(sends, 1)
    ]


def odd_row():
    return lax.rem(lax.axis_index("row"), 2) == 1


def neighbour(value, axis):
    n = lax.axis_size(axis)
    return lax.ppermute(value, axis, [(s, s ^ 1) for s in range(n)])


def wide(value):
    return value.astype(jnp.float32)


def split(value):
    high = value.astype(NARROW)
    return high, (value - wide(high)).astype(NARROW)


def dot(left, right, dims=((1,), (0,))):
    return lax.dot_general(left, right, (dims, ((), ())), preferred_element_type=jnp.float32)


def dense_kernel(piece, vals, rows_in, cols_in, count_in, near, rows, cols, count, sems):
    copies = [
        pltpu.make_async_copy(source, target, sems.at[k])
        for k, (source, target) in enumerate(((rows_in, rows), (cols_in, cols), (count_in, count)))
    ]
    for copy in copies:
        copy.start()
    side = vals.shape[-1]
    near[...] = jnp.zeros_like(near)
    for copy in copies:
        copy.wait()

    def ahead(there, axis):
        n = lax.axis_size(axis)
        return lax.rem(ring_place(there, axis) - ring_place(lax.axis_index(axis), axis) + n, n)

    def add(t, _):
        row, col = rows[0, 0, t], cols[0, 0, t]
        row = ahead(row // piece, "col") * piece + lax.rem(row, piece)
        col = ahead(col // piece, "row") * piece + lax.rem(col, piece)
        down = pl.ds(pl.multiple_of(row * side, side), side)
        across = pl.ds(pl.multiple_of(col * side, side), side)
        near[down, across] = vals[0, 0, t]
        return 0

    lax.fori_loop(0, count[0, 0], add, 0)


def turn_kernel(step, near, far):
    def turn(k, _):
        band = pl.ds(pl.multiple_of(k * step, step), step)
        far[:, band] = near[band, :].T
        return 0

    lax.fori_loop(0, near.shape[0] // step, turn, 0)


def tree(terms):
    while len(terms) > 1:
        middle = len(terms) // 2
        terms = [left + right for left, right in zip(terms[:middle], terms[middle:])]
    return terms[0]


def forward_kernel(n, matrix, *refs):
    operands, own, sends = refs[:n], refs[n], refs[n + 1 :]
    rows = own.shape[0]
    stacked = jnp.concatenate([operand[...] for operand in operands], axis=0)
    product = dot(matrix[...], stacked)
    own[...] = product[:rows]
    for d, send in enumerate(sends, 1):
        send[...] = product[d * rows : (d + 1) * rows].astype(send.dtype)


def layer_kernel(*refs):
    *parts, weight, cotangent, back, mine, other, pre_out = refs
    half = mine.shape[1]
    total = tree([wide(part[...]) for part in parts])
    high, low = split(total)
    pre = dot(high, weight[...]) + dot(low, weight[...])
    pre_out[...] = pre
    sigma = jax.nn.sigmoid(pre)
    grad = wide(cotangent[...]) * sigma * (1.0 + pre * (1.0 - sigma))
    grad_high, grad_low = split(grad)
    down = ((0,), (0,))
    term = dot(high, grad_high, down) + dot(low, grad_high, down) + dot(high, grad_low, down)
    odd = odd_row()
    left, right = term[:, :half], term[:, half:]
    mine[...] = jnp.where(odd, right, left)
    other[...] = jnp.where(odd, left, right).astype(other.dtype)
    across = ((1,), (1,))
    back[...] = (dot(grad_high, weight[...], across) + dot(grad_low, weight[...], across)).astype(
        back.dtype
    )


def message_kernel(back, mine, came, message):
    nodes = back.shape[0]
    message[:nodes] = back[...]
    message[nodes:] = (mine[...] + wide(came[...])).astype(message.dtype)


def act_kernel(pre, act):
    act[...] = (pre[...] * jax.nn.sigmoid(pre[...])).astype(act.dtype)


def backward_kernel(n, matrix, *refs):
    messages, own, kept, sends = refs[:n], refs[n], refs[n + 1], refs[n + 2 :]
    rows = own.shape[0]
    stacked = jnp.concatenate([message[:rows] for message in messages], axis=0)
    product = dot(matrix[...], stacked)
    own[...] = product[:rows]
    term = tree([wide(message[rows:]) for message in messages]).astype(kept.dtype)
    kept[...] = term
    for d, send in enumerate(sends, 1):
        send[:rows] = product[d * rows : (d + 1) * rows].astype(send.dtype)
        send[rows:] = term


def last_kernel(scale, own, kept, *refs):
    *messages, features_out, weight_out = refs
    nodes, half = own.shape[0], kept.shape[1]
    features_out[...] = tree(
        [own[...]] + [wide(message[:nodes]) for message in messages]
    ).astype(features_out.dtype)
    terms = [wide(kept[...])] + [wide(message[nodes:]) for message in messages]
    mine, other = tree(terms[::2]) * scale, tree(terms[1::2]) * scale
    odd = odd_row()
    weight_out[:, :half] = jnp.where(odd, other, mine)
    weight_out[:, half:] = jnp.where(odd, mine, other)


def per_device(features, weight, cotangent, tile_values, tile_rows, tile_cols, tile_count):
    slots, side = tile_values.shape[2:4]
    n_row, n_col = lax.axis_size("row"), lax.axis_size("col")
    nodes, width = features.shape
    hidden = weight.shape[1]
    down, across = n_col * nodes, n_row * nodes
    dense_bytes = 2 * down * across

    gathered = exchange([features] * (n_row - 1), "row", False)
    (near,) = call(
        functools.partial(dense_kernel, nodes // side),
        [((down, across), NARROW)],
        [VMEM] * 4,
        scratch=[
            pltpu.SMEM(tile_rows.shape, jnp.int32),
            pltpu.SMEM(tile_cols.shape, jnp.int32),
            pltpu.SMEM(tile_count.shape, jnp.int32),
            pltpu.SemaphoreType.DMA((3,)),
        ],
        need=2 * dense_bytes,
    )(tile_values, tile_rows, tile_cols, tile_count)

    own, *sends = call(
        functools.partial(forward_kernel, n_row),
        [((nodes, width), jnp.float32)] + [((nodes, width), NARROW)] * (n_col - 1),
        [VMEM] * (1 + n_row),
        flops=2 * down * across * width,
        need=2 * dense_bytes,
    )(near, features, *gathered)
    parts = exchange(sends, "col", True)
    (far,) = call(
        functools.partial(turn_kernel, side),
        [((across, down), NARROW)],
        [VMEM],
        need=3 * dense_bytes,
    )(near)

    half = hidden // 2
    square = (width, half)
    message = ((nodes + width, width), NARROW)
    back, mine, other, pre = call(
        layer_kernel,
        [
            ((nodes, width), NARROW),
            (square, jnp.float32),
            (square, NARROW),
            ((nodes, hidden), jnp.float32),
        ],
        [VMEM] * (n_col + 2),
        flops=14 * nodes * width * hidden,
        after=[far],
    )(own, *parts, weight, cotangent)
    (sent,) = call(message_kernel, [message], [VMEM] * 3)(back, mine, neighbour(other, "row"))
    spread = exchange([sent] * (n_col - 1), "col", False)
    (act,) = call(act_kernel, [((nodes, hidden), NARROW)], [VMEM])(pre)

    own, kept, *sends = call(
        functools.partial(backward_kernel, n_col),
        [((nodes, width), jnp.float32), (square, NARROW)] + [message] * (n_row - 1),
        [VMEM] * (1 + n_col),
        flops=2 * down * across * width,
        need=2 * dense_bytes,
    )(far, sent, *spread)
    parts = exchange(sends, "row", True)

    scale = float(nodes * n_row * n_col) ** -0.5
    grad_features, grad_weight = call(
        functools.partial(last_kernel, scale),
        [((nodes, width), NARROW), ((width, hidden), jnp.float32)],
        [VMEM] * (n_row + 1),
    )(own, kept, *parts)
    return act, grad_features, grad_weight


def solution(mesh):
    placed = (
        P(("groups", "row", "col"), None),
        P(),
        P(("groups", "row", "col"), None),
        P(("groups", "row"), "col", None, None, None),
        P(("groups", "row"), "col", None),
        P(("groups", "row"), "col", None),
        P(("groups", "row"), "col"),
    )
    return jax.shard_map(
        per_device,
        mesh=mesh,
        in_specs=placed,
        out_specs=(
            P(("groups", "row", "col"), None),
            P(("groups", "row", "col"), None),
            P("groups", None),
        ),
        check_vma=False,
    )
```

```python
import functools

import jax
import jax.numpy as jnp
from jax import lax
from jax.experimental import pallas as pl
from jax.experimental.pallas import tpu as pltpu
from jax.sharding import PartitionSpec as P

VMEM = pl.BlockSpec(memory_space=pltpu.VMEM)
ANY = pl.BlockSpec(memory_space=pl.ANY)
LEAST = 16 * 1024 * 1024
NARROW = jnp.bfloat16


def call(kernel, outs, in_specs, scratch=(), flops=0, need=0, after=()):
    outs = tuple(jax.ShapeDtypeStruct(shape, dtype) for shape, dtype in outs)
    late = len(after)
    run = pl.pallas_call(
        (lambda *refs: kernel(*refs[late:])) if late else kernel,
        out_shape=outs,
        in_specs=[ANY] * late + list(in_specs),
        out_specs=(VMEM,) * len(outs),
        scratch_shapes=scratch,
        compiler_params=pltpu.CompilerParams(vmem_limit_bytes=LEAST + need),
        cost_estimate=pl.CostEstimate(flops=flops, bytes_accessed=need, transcendentals=0),
    )
    return functools.partial(run, *after)


def ring_place(k, axis):
    return k ^ (k >> 1) if axis == "col" and lax.axis_size(axis) == 4 else k


def exchange(sends, axis, ahead):
    n = lax.axis_size(axis)

    def target(s, d):
        return ring_place((ring_place(s, axis) + (d if ahead else -d)) % n, axis)

    return [
        lax.ppermute(send, axis, [(s, target(s, d)) for s in range(n)])
        for d, send in enumerate(sends, 1)
    ]


def odd_row():
    return lax.rem(lax.axis_index("row"), 2) == 1


def swap(value, axis, distance):
    n = lax.axis_size(axis)
    return lax.ppermute(value, axis, [(s, s ^ distance) for s in range(n)])


def wide(value):
    return value.astype(jnp.float32)


def split(value):
    high = value.astype(NARROW)
    return high, (value - wide(high)).astype(NARROW)


def dot(left, right, dims=((1,), (0,))):
    return lax.dot_general(left, right, (dims, ((), ())), preferred_element_type=jnp.float32)


def dense_kernel(piece, paired, vals, rows_in, cols_in, count_in, near, rows, cols, count, sems):
    copies = [
        pltpu.make_async_copy(source, target, sems.at[k])
        for k, (source, target) in enumerate(((rows_in, rows), (cols_in, cols), (count_in, count)))
    ]
    for copy in copies:
        copy.start()
    side = vals.shape[-1]
    near[...] = jnp.zeros_like(near)
    for copy in copies:
        copy.wait()

    def ahead(there, axis):
        n = lax.axis_size(axis)
        return lax.rem(ring_place(there, axis) - ring_place(lax.axis_index(axis), axis) + n, n)

    def add(t, _):
        row, col = rows[0, 0, t], cols[0, 0, t]
        if paired:
            place = lax.rem((row // piece) ^ lax.axis_index("col"), 2) * 2 + row // piece // 2
        else:
            place = ahead(row // piece, "col")
        row = place * piece + lax.rem(row, piece)
        col = ahead(col // piece, "row") * piece + lax.rem(col, piece)
        down = pl.ds(pl.multiple_of(row * side, side), side)
        across = pl.ds(pl.multiple_of(col * side, side), side)
        near[down, across] = vals[0, 0, t]
        return 0

    lax.fori_loop(0, count[0, 0], add, 0)


def turn_kernel(step, near, far):
    def turn(k, _):
        band = pl.ds(pl.multiple_of(k * step, step), step)
        far[:, band] = near[band, :].T
        return 0

    lax.fori_loop(0, near.shape[0] // step, turn, 0)


def tree(terms):
    while len(terms) > 1:
        middle = len(terms) // 2
        terms = [left + right for left, right in zip(terms[:middle], terms[middle:])]
    return terms[0]


def forward_kernel(n, matrix, *refs):
    operands, own, sends = refs[:n], refs[n], refs[n + 1 :]
    rows = own.shape[0]
    stacked = jnp.concatenate([operand[...] for operand in operands], axis=0)
    product = dot(matrix[...], stacked)
    own[...] = product[:rows]
    for d, send in enumerate(sends, 1):
        send[...] = product[d * rows : (d + 1) * rows].astype(send.dtype)


def layer(total, weight, cotangent):
    high, low = split(total)
    pre = dot(high, weight) + dot(low, weight)
    sigma = jax.nn.sigmoid(pre)
    grad = wide(cotangent) * sigma * (1.0 + pre * (1.0 - sigma))
    grad_high, grad_low = split(grad)
    across, down = ((1,), (1,)), ((0,), (0,))
    back = dot(grad_high, weight, across) + dot(grad_low, weight, across)
    term = dot(high, grad_high, down) + dot(low, grad_high, down) + dot(high, grad_low, down)
    return pre, back, term


def halve(term, mine, other):
    half = mine.shape[1]
    odd = odd_row()
    left, right = term[:, :half], term[:, half:]
    mine[...] = jnp.where(odd, right, left)
    other[...] = jnp.where(odd, left, right).astype(other.dtype)


def layer_kernel(*refs):
    *parts, weight, cotangent, back_out, mine, other, pre_out = refs
    total = tree([wide(part[...]) for part in parts])
    pre, back, term = layer(total, weight[...], cotangent[...])
    pre_out[...] = pre
    back_out[...] = back.astype(back_out.dtype)
    halve(term, mine, other)


def in_middle():
    my_col = lax.axis_index("col")
    return (my_col == 1) | (my_col == 2)


def paired_forward_kernel(n, matrix, *refs):
    operands, (own, first, second, third) = refs[:n], refs[n:]
    stacked = jnp.concatenate([operand[...] for operand in operands], axis=0)
    product = dot(matrix[...], stacked).astype(own.dtype)
    rows = own.shape[0]
    same, other = product[:rows], product[rows:]
    middle = in_middle()
    own[...] = same
    first[...] = jnp.where(middle, same, other)
    second[...] = other
    third[...] = jnp.where(middle, other, same)


def paired_layer_kernel(own, first, second, third, weight, cotangent, beyond, *refs):
    back_out, mine, other, pre_out = refs
    nodes = cotangent.shape[0]
    middle = in_middle()
    partner = jnp.where(middle, third[...], first[...])
    side = jnp.where(middle, first[...], third[...])
    total = (wide(own[...]) + wide(partner)) + (wide(second[...]) + wide(side))
    high_col = lax.axis_index("col") >= 2
    here, there = cotangent[...], beyond[...]
    both = jnp.concatenate(
        [jnp.where(high_col, there, here), jnp.where(high_col, here, there)], axis=0
    )
    pre, back, term = layer(total, weight[...], both)
    pre_out[...] = jnp.where(high_col, pre[nodes:], pre[:nodes])
    back_out[...] = back.astype(back_out.dtype)
    halve(term, mine, other)


def message_kernel(back, mine, came, message):
    nodes = back.shape[0]
    message[:nodes] = back[...]
    message[nodes:] = (mine[...] + wide(came[...])).astype(message.dtype)


def act_kernel(pre, act):
    act[...] = (pre[...] * jax.nn.sigmoid(pre[...])).astype(act.dtype)


def backward_kernel(n, matrix, *refs):
    messages, own, kept, sends = refs[:n], refs[n], refs[n + 1], refs[n + 2 :]
    rows, backs = own.shape[0], messages[0].shape[0] - kept.shape[0]
    stacked = jnp.concatenate([message[:backs] for message in messages], axis=0)
    product = dot(matrix[...], stacked)
    own[...] = product[:rows]
    term = tree([wide(message[backs:]) for message in messages]).astype(kept.dtype)
    kept[...] = term
    for d, send in enumerate(sends, 1):
        send[:rows] = product[d * rows : (d + 1) * rows].astype(send.dtype)
        send[rows:] = term


def last_kernel(scale, own, kept, *refs):
    *messages, features_out, weight_out = refs
    nodes, half = own.shape[0], kept.shape[1]
    features_out[...] = tree(
        [own[...]] + [wide(message[:nodes]) for message in messages]
    ).astype(features_out.dtype)
    terms = [wide(kept[...])] + [wide(message[nodes:]) for message in messages]
    mine, other = tree(terms[::2]) * scale, tree(terms[1::2]) * scale
    odd = odd_row()
    weight_out[:, :half] = jnp.where(odd, other, mine)
    weight_out[:, half:] = jnp.where(odd, mine, other)


def per_device(features, weight, cotangent, tile_values, tile_rows, tile_cols, tile_count):
    slots, side = tile_values.shape[2:4]
    n_row, n_col = lax.axis_size("row"), lax.axis_size("col")
    nodes, width = features.shape
    hidden = weight.shape[1]
    down, across = n_col * nodes, n_row * nodes
    dense_bytes = 2 * down * across

    paired = n_col == 4
    gathered = exchange([features] * (n_row - 1), "row", False)
    (near,) = call(
        functools.partial(dense_kernel, nodes // side, paired),
        [((down, across), NARROW)],
        [VMEM] * 4,
        scratch=[
            pltpu.SMEM(tile_rows.shape, jnp.int32),
            pltpu.SMEM(tile_cols.shape, jnp.int32),
            pltpu.SMEM(tile_count.shape, jnp.int32),
            pltpu.SemaphoreType.DMA((3,)),
        ],
        need=2 * dense_bytes,
    )(tile_values, tile_rows, tile_cols, tile_count)

    forward = dict(flops=2 * down * across * width, need=2 * dense_bytes)
    if paired:
        layers = 2
        own, *sends = call(
            functools.partial(paired_forward_kernel, n_row),
            [((2 * nodes, width), NARROW)] * 4,
            [VMEM] * (1 + n_row),
            **forward,
        )(near, features, *gathered)
        layer_call, cotangents = paired_layer_kernel, [cotangent, swap(cotangent, "col", 2)]
    else:
        layers = 1
        own, *sends = call(
            functools.partial(forward_kernel, n_row),
            [((nodes, width), jnp.float32)] + [((nodes, width), NARROW)] * (n_col - 1),
            [VMEM] * (1 + n_row),
            **forward,
        )(near, features, *gathered)
        layer_call, cotangents = layer_kernel, [cotangent]
    parts = exchange(sends, "col", True)
    (far,) = call(
        functools.partial(turn_kernel, side),
        [((across, down), NARROW)],
        [VMEM],
        need=3 * dense_bytes,
    )(near)

    half = hidden // 2
    square = (width, half)
    back, mine, other, pre = call(
        layer_call,
        [
            ((layers * nodes, width), NARROW),
            (square, jnp.float32),
            (square, NARROW),
            ((nodes, hidden), jnp.float32),
        ],
        [VMEM] * (n_col + 1 + len(cotangents)),
        flops=14 * layers * nodes * width * hidden,
        after=[far],
    )(own, *parts, weight, *cotangents)
    (sent,) = call(message_kernel, [((layers * nodes + width, width), NARROW)], [VMEM] * 3)(
        back, mine, swap(other, "row", 1)
    )
    if paired:
        spread = [swap(sent, "col", 1)]
    else:
        spread = exchange([sent] * (n_col - 1), "col", False)
    (act,) = call(act_kernel, [((nodes, hidden), NARROW)], [VMEM])(pre)

    message = ((nodes + width, width), NARROW)
    own, kept, *sends = call(
        functools.partial(backward_kernel, 1 + len(spread)),
        [((nodes, width), jnp.float32), (square, NARROW)] + [message] * (n_row - 1),
        [VMEM] * (2 + len(spread)),
        **forward,
    )(far, sent, *spread)
    parts = exchange(sends, "row", True)

    scale = float(nodes * n_row * n_col) ** -0.5
    grad_features, grad_weight = call(
        functools.partial(last_kernel, scale),
        [((nodes, width), NARROW), ((width, hidden), jnp.float32)],
        [VMEM] * (n_row + 1),
    )(own, kept, *parts)
    return act, grad_features, grad_weight


def solution(mesh):
    placed = (
        P(("groups", "row", "col"), None),
        P(),
        P(("groups", "row", "col"), None),
        P(("groups", "row"), "col", None, None, None),
        P(("groups", "row"), "col", None),
        P(("groups", "row"), "col", None),
        P(("groups", "row"), "col"),
    )
    return jax.shard_map(
        per_device,
        mesh=mesh,
        in_specs=placed,
        out_specs=(
            P(("groups", "row", "col"), None),
            P(("groups", "row", "col"), None),
            P("groups", None),
        ),
        check_vma=False,
    )
```

```python
import functools

import jax
import jax.numpy as jnp
from jax import lax
from jax.experimental import pallas as pl
from jax.experimental.pallas import tpu as pltpu
from jax.sharding import PartitionSpec as P

VMEM = pl.BlockSpec(memory_space=pltpu.VMEM)
ANY = pl.BlockSpec(memory_space=pl.ANY)
LEAST = 16 * 1024 * 1024
NARROW = jnp.bfloat16


def call(kernel, outs, in_specs, scratch=(), flops=0, need=0, after=()):
    outs = tuple(jax.ShapeDtypeStruct(shape, dtype) for shape, dtype in outs)
    late = len(after)
    run = pl.pallas_call(
        (lambda *refs: kernel(*refs[late:])) if late else kernel,
        out_shape=outs,
        in_specs=[ANY] * late + list(in_specs),
        out_specs=(VMEM,) * len(outs),
        scratch_shapes=scratch,
        compiler_params=pltpu.CompilerParams(vmem_limit_bytes=LEAST + need),
        cost_estimate=pl.CostEstimate(flops=flops, bytes_accessed=need, transcendentals=0),
    )
    return functools.partial(run, *after)


def ring_place(k, axis):
    return k ^ (k >> 1) if axis == "col" and lax.axis_size(axis) == 4 else k


def exchange(sends, axis, ahead):
    n = lax.axis_size(axis)

    def target(s, d):
        return ring_place((ring_place(s, axis) + (d if ahead else -d)) % n, axis)

    return [
        lax.ppermute(send, axis, [(s, target(s, d)) for s in range(n)])
        for d, send in enumerate(sends, 1)
    ]


def odd_row():
    return lax.rem(lax.axis_index("row"), 2) == 1


def swap(value, axis, distance):
    n = lax.axis_size(axis)
    return lax.ppermute(value, axis, [(s, s ^ distance) for s in range(n)])


def wide(value):
    return value.astype(jnp.float32)


def split(value):
    high = value.astype(NARROW)
    return high, (value - wide(high)).astype(NARROW)


def dot(left, right, dims=((1,), (0,))):
    return lax.dot_general(left, right, (dims, ((), ())), preferred_element_type=jnp.float32)


def dense_kernel(piece, paired, vals, rows_in, cols_in, count_in, near, rows, cols, count, sems):
    copies = [
        pltpu.make_async_copy(source, target, sems.at[k])
        for k, (source, target) in enumerate(((rows_in, rows), (cols_in, cols), (count_in, count)))
    ]
    for copy in copies:
        copy.start()
    side = vals.shape[-1]
    near[...] = jnp.zeros_like(near)
    for copy in copies:
        copy.wait()

    def ahead(there, axis):
        n = lax.axis_size(axis)
        return lax.rem(ring_place(there, axis) - ring_place(lax.axis_index(axis), axis) + n, n)

    def add(t, _):
        row, col = rows[0, 0, t], cols[0, 0, t]
        if paired:
            there, here = row // piece, lax.axis_index("col")
            apart = lax.rem(ring_place(there, "col") ^ ring_place(here, "col"), 2)
            place = apart * 2 + there // 2
        else:
            place = ahead(row // piece, "col")
        row = place * piece + lax.rem(row, piece)
        col = ahead(col // piece, "row") * piece + lax.rem(col, piece)
        down = pl.ds(pl.multiple_of(row * side, side), side)
        across = pl.ds(pl.multiple_of(col * side, side), side)
        near[down, across] = vals[0, 0, t]
        return 0

    lax.fori_loop(0, count[0, 0], add, 0)


def turn_kernel(step, near, far):
    def turn(k, _):
        band = pl.ds(pl.multiple_of(k * step, step), step)
        far[:, band] = near[band, :].T
        return 0

    lax.fori_loop(0, near.shape[0] // step, turn, 0)


def tree(terms):
    while len(terms) > 1:
        middle = len(terms) // 2
        terms = [left + right for left, right in zip(terms[:middle], terms[middle:])]
    return terms[0]


def forward_kernel(n, matrix, *refs):
    operands, own, sends = refs[:n], refs[n], refs[n + 1 :]
    rows = own.shape[0]
    stacked = jnp.concatenate([operand[...] for operand in operands], axis=0)
    product = dot(matrix[...], stacked)
    own[...] = product[:rows]
    for d, send in enumerate(sends, 1):
        send[...] = product[d * rows : (d + 1) * rows].astype(send.dtype)


def layer(total, weight, cotangent):
    high, low = split(total)
    pre = dot(high, weight) + dot(low, weight)
    sigma = jax.nn.sigmoid(pre)
    grad = wide(cotangent) * sigma * (1.0 + pre * (1.0 - sigma))
    grad_high, grad_low = split(grad)
    across, down = ((1,), (1,)), ((0,), (0,))
    back = dot(grad_high, weight, across) + dot(grad_low, weight, across)
    term = dot(high, grad_high, down) + dot(low, grad_high, down) + dot(high, grad_low, down)
    return pre, back, term


def halve(term, mine, other):
    half = mine.shape[1]
    odd = odd_row()
    left, right = term[:, :half], term[:, half:]
    mine[...] = jnp.where(odd, right, left)
    other[...] = jnp.where(odd, left, right).astype(other.dtype)


def layer_kernel(*refs):
    *parts, weight, cotangent, back_out, mine, other, pre_out = refs
    total = tree([wide(part[...]) for part in parts])
    pre, back, term = layer(total, weight[...], cotangent[...])
    pre_out[...] = pre
    back_out[...] = back.astype(back_out.dtype)
    halve(term, mine, other)


def paired_forward_kernel(n, matrix, *refs):
    operands, (same, other) = refs[:n], refs[n:]
    stacked = jnp.concatenate([operand[...] for operand in operands], axis=0)
    product = dot(matrix[...], stacked).astype(same.dtype)
    rows = same.shape[0]
    same[...] = product[:rows]
    other[...] = product[rows:]


def paired_layer_kernel(own, first, second, third, weight, cotangent, beyond, *refs):
    back_out, mine, other, pre_out = refs
    nodes = cotangent.shape[0]
    total = (wide(own[...]) + wide(second[...])) + (wide(first[...]) + wide(third[...]))
    high_col = lax.axis_index("col") >= 2
    here, there = cotangent[...], beyond[...]
    both = jnp.concatenate(
        [jnp.where(high_col, there, here), jnp.where(high_col, here, there)], axis=0
    )
    pre, back, term = layer(total, weight[...], both)
    pre_out[...] = jnp.where(high_col, pre[nodes:], pre[:nodes])
    back_out[...] = back.astype(back_out.dtype)
    halve(term, mine, other)


def message_kernel(back, mine, came, message):
    nodes = back.shape[0]
    message[:nodes] = back[...]
    message[nodes:] = (mine[...] + wide(came[...])).astype(message.dtype)


def act_kernel(pre, act):
    act[...] = (pre[...] * jax.nn.sigmoid(pre[...])).astype(act.dtype)


def backward_kernel(n, matrix, *refs):
    messages, own, kept, sends = refs[:n], refs[n], refs[n + 1], refs[n + 2 :]
    rows, backs = own.shape[0], messages[0].shape[0] - kept.shape[0]
    stacked = jnp.concatenate([message[:backs] for message in messages], axis=0)
    product = dot(matrix[...], stacked)
    own[...] = product[:rows]
    term = tree([wide(message[backs:]) for message in messages]).astype(kept.dtype)
    kept[...] = term
    for d, send in enumerate(sends, 1):
        send[:rows] = product[d * rows : (d + 1) * rows].astype(send.dtype)
        send[rows:] = term


def last_kernel(scale, own, kept, *refs):
    *messages, features_out, weight_out = refs
    nodes, half = own.shape[0], kept.shape[1]
    features_out[...] = tree(
        [own[...]] + [wide(message[:nodes]) for message in messages]
    ).astype(features_out.dtype)
    terms = [wide(kept[...])] + [wide(message[nodes:]) for message in messages]
    mine, other = tree(terms[::2]) * scale, tree(terms[1::2]) * scale
    odd = odd_row()
    weight_out[:, :half] = jnp.where(odd, other, mine)
    weight_out[:, half:] = jnp.where(odd, mine, other)


def per_device(features, weight, cotangent, tile_values, tile_rows, tile_cols, tile_count):
    slots, side = tile_values.shape[2:4]
    n_row, n_col = lax.axis_size("row"), lax.axis_size("col")
    nodes, width = features.shape
    hidden = weight.shape[1]
    down, across = n_col * nodes, n_row * nodes
    dense_bytes = 2 * down * across

    paired = n_col == 4
    gathered = exchange([features] * (n_row - 1), "row", False)
    (near,) = call(
        functools.partial(dense_kernel, nodes // side, paired),
        [((down, across), NARROW)],
        [VMEM] * 4,
        scratch=[
            pltpu.SMEM(tile_rows.shape, jnp.int32),
            pltpu.SMEM(tile_cols.shape, jnp.int32),
            pltpu.SMEM(tile_count.shape, jnp.int32),
            pltpu.SemaphoreType.DMA((3,)),
        ],
        need=2 * dense_bytes,
    )(tile_values, tile_rows, tile_cols, tile_count)

    forward = dict(flops=2 * down * across * width, need=2 * dense_bytes)
    if paired:
        layers = 2
        own, other = call(
            functools.partial(paired_forward_kernel, n_row),
            [((2 * nodes, width), NARROW)] * 2,
            [VMEM] * (1 + n_row),
            **forward,
        )(near, features, *gathered)
        sends = [other, own, other]
        layer_call, cotangents = paired_layer_kernel, [cotangent, swap(cotangent, "col", 3)]
    else:
        layers = 1
        own, *sends = call(
            functools.partial(forward_kernel, n_row),
            [((nodes, width), jnp.float32)] + [((nodes, width), NARROW)] * (n_col - 1),
            [VMEM] * (1 + n_row),
            **forward,
        )(near, features, *gathered)
        layer_call, cotangents = layer_kernel, [cotangent]
    parts = exchange(sends, "col", True)
    (far,) = call(
        functools.partial(turn_kernel, side),
        [((across, down), NARROW)],
        [VMEM],
        need=3 * dense_bytes,
    )(near)

    half = hidden // 2
    square = (width, half)
    back, mine, other, pre = call(
        layer_call,
        [
            ((layers * nodes, width), NARROW),
            (square, jnp.float32),
            (square, NARROW),
            ((nodes, hidden), jnp.float32),
        ],
        [VMEM] * (n_col + 1 + len(cotangents)),
        flops=14 * layers * nodes * width * hidden,
        after=[far],
    )(own, *parts, weight, *cotangents)
    (sent,) = call(message_kernel, [((layers * nodes + width, width), NARROW)], [VMEM] * 3)(
        back, mine, swap(other, "row", 1)
    )
    if paired:
        spread = [swap(sent, "col", 1)]
    else:
        spread = exchange([sent] * (n_col - 1), "col", False)
    (act,) = call(act_kernel, [((nodes, hidden), NARROW)], [VMEM])(pre)

    message = ((nodes + width, width), NARROW)
    own, kept, *sends = call(
        functools.partial(backward_kernel, 1 + len(spread)),
        [((nodes, width), jnp.float32), (square, NARROW)] + [message] * (n_row - 1),
        [VMEM] * (2 + len(spread)),
        **forward,
    )(far, sent, *spread)
    parts = exchange(sends, "row", True)

    scale = float(nodes * n_row * n_col) ** -0.5
    grad_features, grad_weight = call(
        functools.partial(last_kernel, scale),
        [((nodes, width), NARROW), ((width, hidden), jnp.float32)],
        [VMEM] * (n_row + 1),
    )(own, kept, *parts)
    return act, grad_features, grad_weight


def solution(mesh):
    placed = (
        P(("groups", "row", "col"), None),
        P(),
        P(("groups", "row", "col"), None),
        P(("groups", "row"), "col", None, None, None),
        P(("groups", "row"), "col", None),
        P(("groups", "row"), "col", None),
        P(("groups", "row"), "col"),
    )
    return jax.shard_map(
        per_device,
        mesh=mesh,
        in_specs=placed,
        out_specs=(
            P(("groups", "row", "col"), None),
            P(("groups", "row", "col"), None),
            P("groups", None),
        ),
        check_vma=False,
    )
```

```python
import functools

import jax
import jax.numpy as jnp
from jax import lax
from jax.experimental import pallas as pl
from jax.experimental.pallas import tpu as pltpu
from jax.sharding import PartitionSpec as P

VMEM = pl.BlockSpec(memory_space=pltpu.VMEM)
ANY = pl.BlockSpec(memory_space=pl.ANY)
LEAST = 16 * 1024 * 1024
NARROW = jnp.bfloat16


def call(kernel, outs, in_specs, scratch=(), flops=0, need=0, after=()):
    outs = tuple(jax.ShapeDtypeStruct(shape, dtype) for shape, dtype in outs)
    late = len(after)
    run = pl.pallas_call(
        (lambda *refs: kernel(*refs[late:])) if late else kernel,
        out_shape=outs,
        in_specs=[ANY] * late + list(in_specs),
        out_specs=(VMEM,) * len(outs),
        scratch_shapes=scratch,
        compiler_params=pltpu.CompilerParams(vmem_limit_bytes=LEAST + need),
        cost_estimate=pl.CostEstimate(flops=flops, bytes_accessed=need, transcendentals=0),
    )
    return functools.partial(run, *after)


def ring_place(k, axis):
    return k ^ (k >> 1) if axis == "col" and lax.axis_size(axis) == 4 else k


def exchange(sends, axis, ahead):
    n = lax.axis_size(axis)

    def target(s, d):
        return ring_place((ring_place(s, axis) + (d if ahead else -d)) % n, axis)

    return [
        lax.ppermute(send, axis, [(s, target(s, d)) for s in range(n)])
        for d, send in enumerate(sends, 1)
    ]


def odd_row():
    return lax.rem(lax.axis_index("row"), 2) == 1


def swap(value, axis, distance):
    n = lax.axis_size(axis)
    return lax.ppermute(value, axis, [(s, s ^ distance) for s in range(n)])


def wide(value):
    return value.astype(jnp.float32)


def split(value):
    high = value.astype(NARROW)
    return high, (value - wide(high)).astype(NARROW)


def dot(left, right, dims=((1,), (0,))):
    return lax.dot_general(left, right, (dims, ((), ())), preferred_element_type=jnp.float32)


def dense_kernel(piece, paired, vals, rows_in, cols_in, count_in, near, rows, cols, count, sems):
    copies = [
        pltpu.make_async_copy(source, target, sems.at[k])
        for k, (source, target) in enumerate(((rows_in, rows), (cols_in, cols), (count_in, count)))
    ]
    for copy in copies:
        copy.start()
    side = vals.shape[-1]
    near[...] = jnp.zeros_like(near)
    for copy in copies:
        copy.wait()

    def ahead(there, axis):
        n = lax.axis_size(axis)
        return lax.rem(ring_place(there, axis) - ring_place(lax.axis_index(axis), axis) + n, n)

    def add(t, _):
        row, col = rows[0, 0, t], cols[0, 0, t]
        if paired:
            place = lax.rem((row // piece) ^ lax.axis_index("col"), 2) * 2 + row // piece // 2
        else:
            place = ahead(row // piece, "col")
        row = place * piece + lax.rem(row, piece)
        col = ahead(col // piece, "row") * piece + lax.rem(col, piece)
        down = pl.ds(pl.multiple_of(row * side, side), side)
        across = pl.ds(pl.multiple_of(col * side, side), side)
        near[down, across] = vals[0, 0, t]
        return 0

    lax.fori_loop(0, count[0, 0], add, 0)


def turn_kernel(step, near, far):
    def turn(k, _):
        band = pl.ds(pl.multiple_of(k * step, step), step)
        far[:, band] = near[band, :].T
        return 0

    lax.fori_loop(0, near.shape[0] // step, turn, 0)


def tree(terms):
    while len(terms) > 1:
        middle = len(terms) // 2
        terms = [left + right for left, right in zip(terms[:middle], terms[middle:])]
    return terms[0]


def forward_kernel(n, matrix, *refs):
    operands, own, sends = refs[:n], refs[n], refs[n + 1 :]
    rows = own.shape[0]
    stacked = jnp.concatenate([operand[...] for operand in operands], axis=0)
    product = dot(matrix[...], stacked)
    own[...] = product[:rows]
    for d, send in enumerate(sends, 1):
        send[...] = product[d * rows : (d + 1) * rows].astype(send.dtype)


def layer(total, weight, cotangent):
    high, low = split(total)
    pre = dot(high, weight) + dot(low, weight)
    sigma = jax.nn.sigmoid(pre)
    grad = wide(cotangent) * sigma * (1.0 + pre * (1.0 - sigma))
    grad_high, grad_low = split(grad)
    across, down = ((1,), (1,)), ((0,), (0,))
    back = dot(grad_high, weight, across) + dot(grad_low, weight, across)
    term = dot(high, grad_high, down) + dot(low, grad_high, down) + dot(high, grad_low, down)
    return pre, back, term


def halve(term, mine, other):
    half = mine.shape[1]
    odd = odd_row()
    left, right = term[:, :half], term[:, half:]
    mine[...] = jnp.where(odd, right, left)
    other[...] = jnp.where(odd, left, right).astype(other.dtype)


def layer_kernel(*refs):
    *parts, weight, cotangent, back_out, mine, other, pre_out = refs
    total = tree([wide(part[...]) for part in parts])
    pre, back, term = layer(total, weight[...], cotangent[...])
    pre_out[...] = pre
    back_out[...] = back.astype(back_out.dtype)
    halve(term, mine, other)


def in_middle():
    my_col = lax.axis_index("col")
    return (my_col == 1) | (my_col == 2)


def paired_forward_kernel(n, matrix, *refs):
    operands, cotangent, (own, first, second, third, passed) = refs[:n], refs[n], refs[n + 1 :]
    passed[...] = cotangent[...]
    stacked = jnp.concatenate([operand[...] for operand in operands], axis=0)
    product = dot(matrix[...], stacked).astype(own.dtype)
    rows = own.shape[0]
    same, other = product[:rows], product[rows:]
    middle = in_middle()
    own[...] = same
    first[...] = jnp.where(middle, same, other)
    second[...] = other
    third[...] = jnp.where(middle, other, same)


def paired_layer_kernel(own, first, second, third, weight, cotangent, beyond, *refs):
    back_out, mine, other, pre_out = refs
    nodes = cotangent.shape[0]
    middle = in_middle()
    partner = jnp.where(middle, third[...], first[...])
    side = jnp.where(middle, first[...], third[...])
    total = (wide(own[...]) + wide(partner)) + (wide(second[...]) + wide(side))
    high_col = lax.axis_index("col") >= 2
    here, there = cotangent[...], beyond[...]
    both = jnp.concatenate(
        [jnp.where(high_col, there, here), jnp.where(high_col, here, there)], axis=0
    )
    pre, back, term = layer(total, weight[...], both)
    pre_out[...] = jnp.where(high_col, pre[nodes:], pre[:nodes])
    back_out[...] = back.astype(back_out.dtype)
    halve(term, mine, other)


def message_kernel(back, mine, came, message):
    nodes = back.shape[0]
    message[:nodes] = back[...]
    message[nodes:] = (mine[...] + wide(came[...])).astype(message.dtype)


def act_kernel(pre, act):
    act[...] = (pre[...] * jax.nn.sigmoid(pre[...])).astype(act.dtype)


def backward_kernel(n, matrix, *refs):
    messages, own, kept, sends = refs[:n], refs[n], refs[n + 1], refs[n + 2 :]
    rows, backs = own.shape[0], messages[0].shape[0] - kept.shape[0]
    stacked = jnp.concatenate([message[:backs] for message in messages], axis=0)
    product = dot(matrix[...], stacked)
    own[...] = product[:rows]
    term = tree([wide(message[backs:]) for message in messages]).astype(kept.dtype)
    kept[...] = term
    for d, send in enumerate(sends, 1):
        send[:rows] = product[d * rows : (d + 1) * rows].astype(send.dtype)
        send[rows:] = term


def last_kernel(scale, own, kept, *refs):
    *messages, features_out, weight_out = refs
    nodes, half = own.shape[0], kept.shape[1]
    features_out[...] = tree(
        [own[...]] + [wide(message[:nodes]) for message in messages]
    ).astype(features_out.dtype)
    terms = [wide(kept[...])] + [wide(message[nodes:]) for message in messages]
    mine, other = tree(terms[::2]) * scale, tree(terms[1::2]) * scale
    odd = odd_row()
    weight_out[:, :half] = jnp.where(odd, other, mine)
    weight_out[:, half:] = jnp.where(odd, mine, other)


def per_device(features, weight, cotangent, tile_values, tile_rows, tile_cols, tile_count):
    slots, side = tile_values.shape[2:4]
    n_row, n_col = lax.axis_size("row"), lax.axis_size("col")
    nodes, width = features.shape
    hidden = weight.shape[1]
    down, across = n_col * nodes, n_row * nodes
    dense_bytes = 2 * down * across

    paired = n_col == 4
    gathered = exchange([features] * (n_row - 1), "row", False)
    (near,) = call(
        functools.partial(dense_kernel, nodes // side, paired),
        [((down, across), NARROW)],
        [VMEM] * 4,
        scratch=[
            pltpu.SMEM(tile_rows.shape, jnp.int32),
            pltpu.SMEM(tile_cols.shape, jnp.int32),
            pltpu.SMEM(tile_count.shape, jnp.int32),
            pltpu.SemaphoreType.DMA((3,)),
        ],
        need=2 * dense_bytes,
    )(tile_values, tile_rows, tile_cols, tile_count)

    forward = dict(flops=2 * down * across * width, need=2 * dense_bytes)
    if paired:
        layers = 2
        own, *sends, passed = call(
            functools.partial(paired_forward_kernel, n_row),
            [((2 * nodes, width), NARROW)] * 4 + [((nodes, hidden), NARROW)],
            [VMEM] * (2 + n_row),
            **forward,
        )(near, features, *gathered, cotangent)
        layer_call, cotangents = paired_layer_kernel, [cotangent, swap(passed, "col", 2)]
    else:
        layers = 1
        own, *sends = call(
            functools.partial(forward_kernel, n_row),
            [((nodes, width), jnp.float32)] + [((nodes, width), NARROW)] * (n_col - 1),
            [VMEM] * (1 + n_row),
            **forward,
        )(near, features, *gathered)
        layer_call, cotangents = layer_kernel, [cotangent]
    parts = exchange(sends, "col", True)
    (far,) = call(
        functools.partial(turn_kernel, side),
        [((across, down), NARROW)],
        [VMEM],
        need=3 * dense_bytes,
    )(near)

    half = hidden // 2
    square = (width, half)
    back, mine, other, pre = call(
        layer_call,
        [
            ((layers * nodes, width), NARROW),
            (square, jnp.float32),
            (square, NARROW),
            ((nodes, hidden), jnp.float32),
        ],
        [VMEM] * (n_col + 1 + len(cotangents)),
        flops=14 * layers * nodes * width * hidden,
        after=[far],
    )(own, *parts, weight, *cotangents)
    (sent,) = call(message_kernel, [((layers * nodes + width, width), NARROW)], [VMEM] * 3)(
        back, mine, swap(other, "row", 1)
    )
    if paired:
        spread = [swap(sent, "col", 1)]
    else:
        spread = exchange([sent] * (n_col - 1), "col", False)
    (act,) = call(act_kernel, [((nodes, hidden), NARROW)], [VMEM])(pre)

    message = ((nodes + width, width), NARROW)
    own, kept, *sends = call(
        functools.partial(backward_kernel, 1 + len(spread)),
        [((nodes, width), jnp.float32), (square, NARROW)] + [message] * (n_row - 1),
        [VMEM] * (2 + len(spread)),
        **forward,
    )(far, sent, *spread)
    parts = exchange(sends, "row", True)

    scale = float(nodes * n_row * n_col) ** -0.5
    grad_features, grad_weight = call(
        functools.partial(last_kernel, scale),
        [((nodes, width), NARROW), ((width, hidden), jnp.float32)],
        [VMEM] * (n_row + 1),
    )(own, kept, *parts)
    return act, grad_features, grad_weight


def solution(mesh):
    placed = (
        P(("groups", "row", "col"), None),
        P(),
        P(("groups", "row", "col"), None),
        P(("groups", "row"), "col", None, None, None),
        P(("groups", "row"), "col", None),
        P(("groups", "row"), "col", None),
        P(("groups", "row"), "col"),
    )
    return jax.shard_map(
        per_device,
        mesh=mesh,
        in_specs=placed,
        out_specs=(
            P(("groups", "row", "col"), None),
            P(("groups", "row", "col"), None),
            P("groups", None),
        ),
        check_vma=False,
    )
```

```python
import functools

import jax
import jax.numpy as jnp
from jax import lax
from jax.experimental import pallas as pl
from jax.experimental.pallas import tpu as pltpu
from jax.sharding import PartitionSpec as P

VMEM = pl.BlockSpec(memory_space=pltpu.VMEM)
ANY = pl.BlockSpec(memory_space=pl.ANY)
LEAST = 16 * 1024 * 1024
NARROW = jnp.bfloat16


def call(kernel, outs, in_specs, scratch=(), flops=0, need=0, after=(), aliases=None):
    outs = tuple(jax.ShapeDtypeStruct(shape, dtype) for shape, dtype in outs)
    late = len(after)
    run = pl.pallas_call(
        (lambda *refs: kernel(*refs[late:])) if late else kernel,
        out_shape=outs,
        in_specs=[ANY] * late + list(in_specs),
        out_specs=(VMEM,) * len(outs),
        input_output_aliases=aliases or {},
        scratch_shapes=scratch,
        compiler_params=pltpu.CompilerParams(vmem_limit_bytes=LEAST + need),
        cost_estimate=pl.CostEstimate(flops=flops, bytes_accessed=need, transcendentals=0),
    )
    return functools.partial(run, *after)


def ring_place(k, axis):
    return k ^ (k >> 1) if axis == "col" and lax.axis_size(axis) == 4 else k


def exchange(sends, axis, ahead):
    n = lax.axis_size(axis)

    def target(s, d):
        return ring_place((ring_place(s, axis) + (d if ahead else -d)) % n, axis)

    return [
        lax.ppermute(send, axis, [(s, target(s, d)) for s in range(n)])
        for d, send in enumerate(sends, 1)
    ]


def odd_row():
    return lax.rem(lax.axis_index("row"), 2) == 1


def swap(value, axis, distance):
    n = lax.axis_size(axis)
    return lax.ppermute(value, axis, [(s, s ^ distance) for s in range(n)])


def wide(value):
    return value.astype(jnp.float32)


def split(value):
    high = value.astype(NARROW)
    return high, (value - wide(high)).astype(NARROW)


def dot(left, right, dims=((1,), (0,))):
    return lax.dot_general(left, right, (dims, ((), ())), preferred_element_type=jnp.float32)


def zero_kernel(out):
    out[...] = jnp.zeros_like(out)


def dense_kernel(piece, paired, blank, vals, rows_in, cols_in, count_in, near, rows, cols, count, sems):
    copies = [
        pltpu.make_async_copy(source, target, sems.at[k])
        for k, (source, target) in enumerate(((rows_in, rows), (cols_in, cols), (count_in, count)))
    ]
    for copy in copies:
        copy.start()
    side = vals.shape[-1]
    for copy in copies:
        copy.wait()

    def ahead(there, axis):
        n = lax.axis_size(axis)
        return lax.rem(ring_place(there, axis) - ring_place(lax.axis_index(axis), axis) + n, n)

    def add(t, _):
        row, col = rows[0, 0, t], cols[0, 0, t]
        if paired:
            place = lax.rem((row // piece) ^ lax.axis_index("col"), 2) * 2 + row // piece // 2
        else:
            place = ahead(row // piece, "col")
        row = place * piece + lax.rem(row, piece)
        col = ahead(col // piece, "row") * piece + lax.rem(col, piece)
        down = pl.ds(pl.multiple_of(row * side, side), side)
        across = pl.ds(pl.multiple_of(col * side, side), side)
        near[down, across] = vals[0, 0, t]
        return 0

    lax.fori_loop(0, count[0, 0], add, 0)


def turn_kernel(step, near, far):
    def turn(k, _):
        band = pl.ds(pl.multiple_of(k * step, step), step)
        far[:, band] = near[band, :].T
        return 0

    lax.fori_loop(0, near.shape[0] // step, turn, 0)


def tree(terms):
    while len(terms) > 1:
        middle = len(terms) // 2
        terms = [left + right for left, right in zip(terms[:middle], terms[middle:])]
    return terms[0]


def forward_kernel(n, matrix, *refs):
    operands, own, sends = refs[:n], refs[n], refs[n + 1 :]
    rows = own.shape[0]
    stacked = jnp.concatenate([operand[...] for operand in operands], axis=0)
    product = dot(matrix[...], stacked)
    own[...] = product[:rows]
    for d, send in enumerate(sends, 1):
        send[...] = product[d * rows : (d + 1) * rows].astype(send.dtype)


def layer(total, weight, cotangent):
    high, low = split(total)
    pre = dot(high, weight) + dot(low, weight)
    sigma = jax.nn.sigmoid(pre)
    grad = wide(cotangent) * sigma * (1.0 + pre * (1.0 - sigma))
    grad_high, grad_low = split(grad)
    across, down = ((1,), (1,)), ((0,), (0,))
    back = dot(grad_high, weight, across) + dot(grad_low, weight, across)
    term = dot(high, grad_high, down) + dot(low, grad_high, down) + dot(high, grad_low, down)
    return pre, back, term


def halve(term, mine, other):
    half = mine.shape[1]
    odd = odd_row()
    left, right = term[:, :half], term[:, half:]
    mine[...] = jnp.where(odd, right, left)
    other[...] = jnp.where(odd, left, right).astype(other.dtype)


def layer_kernel(*refs):
    *parts, weight, cotangent, back_out, mine, other, pre_out = refs
    total = tree([wide(part[...]) for part in parts])
    pre, back, term = layer(total, weight[...], cotangent[...])
    pre_out[...] = pre
    back_out[...] = back.astype(back_out.dtype)
    halve(term, mine, other)


def in_middle():
    my_col = lax.axis_index("col")
    return (my_col == 1) | (my_col == 2)


def paired_forward_kernel(n, matrix, *refs):
    operands, (own, first, second, third) = refs[:n], refs[n:]
    stacked = jnp.concatenate([operand[...] for operand in operands], axis=0)
    product = dot(matrix[...], stacked).astype(own.dtype)
    rows = own.shape[0]
    same, other = product[:rows], product[rows:]
    middle = in_middle()
    own[...] = same
    first[...] = jnp.where(middle, same, other)
    second[...] = other
    third[...] = jnp.where(middle, other, same)


def paired_layer_kernel(own, first, second, third, weight, cotangent, beyond, *refs):
    back_out, mine, other, pre_out = refs
    nodes = cotangent.shape[0]
    middle = in_middle()
    partner = jnp.where(middle, third[...], first[...])
    side = jnp.where(middle, first[...], third[...])
    total = (wide(own[...]) + wide(partner)) + (wide(second[...]) + wide(side))
    high_col = lax.axis_index("col") >= 2
    here, there = cotangent[...], beyond[...]
    both = jnp.concatenate(
        [jnp.where(high_col, there, here), jnp.where(high_col, here, there)], axis=0
    )
    pre, back, term = layer(total, weight[...], both)
    pre_out[...] = jnp.where(high_col, pre[nodes:], pre[:nodes])
    back_out[...] = back.astype(back_out.dtype)
    halve(term, mine, other)


def message_kernel(back, mine, came, message):
    nodes = back.shape[0]
    message[:nodes] = back[...]
    message[nodes:] = (mine[...] + wide(came[...])).astype(message.dtype)


def act_kernel(pre, act):
    act[...] = (pre[...] * jax.nn.sigmoid(pre[...])).astype(act.dtype)


def backward_kernel(n, matrix, *refs):
    messages, own, kept, sends = refs[:n], refs[n], refs[n + 1], refs[n + 2 :]
    rows, backs = own.shape[0], messages[0].shape[0] - kept.shape[0]
    stacked = jnp.concatenate([message[:backs] for message in messages], axis=0)
    product = dot(matrix[...], stacked)
    own[...] = product[:rows]
    term = tree([wide(message[backs:]) for message in messages]).astype(kept.dtype)
    kept[...] = term
    for d, send in enumerate(sends, 1):
        send[:rows] = product[d * rows : (d + 1) * rows].astype(send.dtype)
        send[rows:] = term


def last_kernel(scale, own, kept, *refs):
    *messages, features_out, weight_out = refs
    nodes, half = own.shape[0], kept.shape[1]
    features_out[...] = tree(
        [own[...]] + [wide(message[:nodes]) for message in messages]
    ).astype(features_out.dtype)
    terms = [wide(kept[...])] + [wide(message[nodes:]) for message in messages]
    mine, other = tree(terms[::2]) * scale, tree(terms[1::2]) * scale
    odd = odd_row()
    weight_out[:, :half] = jnp.where(odd, other, mine)
    weight_out[:, half:] = jnp.where(odd, mine, other)


def per_device(features, weight, cotangent, tile_values, tile_rows, tile_cols, tile_count):
    slots, side = tile_values.shape[2:4]
    n_row, n_col = lax.axis_size("row"), lax.axis_size("col")
    nodes, width = features.shape
    hidden = weight.shape[1]
    down, across = n_col * nodes, n_row * nodes
    dense_bytes = 2 * down * across

    paired = n_col == 4
    gathered = exchange([features] * (n_row - 1), "row", False)
    (blank,) = call(zero_kernel, [((down, across), NARROW)], [], need=dense_bytes)()
    (near,) = call(
        functools.partial(dense_kernel, nodes // side, paired),
        [((down, across), NARROW)],
        [VMEM] * 5,
        aliases={0: 0},
        scratch=[
            pltpu.SMEM(tile_rows.shape, jnp.int32),
            pltpu.SMEM(tile_cols.shape, jnp.int32),
            pltpu.SMEM(tile_count.shape, jnp.int32),
            pltpu.SemaphoreType.DMA((3,)),
        ],
        need=2 * dense_bytes,
    )(blank, tile_values, tile_rows, tile_cols, tile_count)

    forward = dict(flops=2 * down * across * width, need=2 * dense_bytes)
    if paired:
        layers = 2
        own, *sends = call(
            functools.partial(paired_forward_kernel, n_row),
            [((2 * nodes, width), NARROW)] * 4,
            [VMEM] * (1 + n_row),
            **forward,
        )(near, features, *gathered)
        layer_call, cotangents = paired_layer_kernel, [cotangent, swap(cotangent, "col", 2)]
    else:
        layers = 1
        own, *sends = call(
            functools.partial(forward_kernel, n_row),
            [((nodes, width), jnp.float32)] + [((nodes, width), NARROW)] * (n_col - 1),
            [VMEM] * (1 + n_row),
            **forward,
        )(near, features, *gathered)
        layer_call, cotangents = layer_kernel, [cotangent]
    parts = exchange(sends, "col", True)
    (far,) = call(
        functools.partial(turn_kernel, side),
        [((across, down), NARROW)],
        [VMEM],
        need=3 * dense_bytes,
    )(near)

    half = hidden // 2
    square = (width, half)
    back, mine, other, pre = call(
        layer_call,
        [
            ((layers * nodes, width), NARROW),
            (square, jnp.float32),
            (square, NARROW),
            ((nodes, hidden), jnp.float32),
        ],
        [VMEM] * (n_col + 1 + len(cotangents)),
        flops=14 * layers * nodes * width * hidden,
        after=[far],
    )(own, *parts, weight, *cotangents)
    (sent,) = call(message_kernel, [((layers * nodes + width, width), NARROW)], [VMEM] * 3)(
        back, mine, swap(other, "row", 1)
    )
    if paired:
        spread = [swap(sent, "col", 1)]
    else:
        spread = exchange([sent] * (n_col - 1), "col", False)
    (act,) = call(act_kernel, [((nodes, hidden), NARROW)], [VMEM])(pre)

    message = ((nodes + width, width), NARROW)
    own, kept, *sends = call(
        functools.partial(backward_kernel, 1 + len(spread)),
        [((nodes, width), jnp.float32), (square, NARROW)] + [message] * (n_row - 1),
        [VMEM] * (2 + len(spread)),
        **forward,
    )(far, sent, *spread)
    parts = exchange(sends, "row", True)

    scale = float(nodes * n_row * n_col) ** -0.5
    grad_features, grad_weight = call(
        functools.partial(last_kernel, scale),
        [((nodes, width), NARROW), ((width, hidden), jnp.float32)],
        [VMEM] * (n_row + 1),
    )(own, kept, *parts)
    return act, grad_features, grad_weight


def solution(mesh):
    placed = (
        P(("groups", "row", "col"), None),
        P(),
        P(("groups", "row", "col"), None),
        P(("groups", "row"), "col", None, None, None),
        P(("groups", "row"), "col", None),
        P(("groups", "row"), "col", None),
        P(("groups", "row"), "col"),
    )
    return jax.shard_map(
        per_device,
        mesh=mesh,
        in_specs=placed,
        out_specs=(
            P(("groups", "row", "col"), None),
            P(("groups", "row", "col"), None),
            P("groups", None),
        ),
        check_vma=False,
    )
```

```python
import functools

import jax
import jax.numpy as jnp
from jax import lax
from jax.experimental import pallas as pl
from jax.experimental.pallas import tpu as pltpu
from jax.sharding import PartitionSpec as P

VMEM = pl.BlockSpec(memory_space=pltpu.VMEM)
ANY = pl.BlockSpec(memory_space=pl.ANY)
LEAST = 16 * 1024 * 1024
NARROW = jnp.bfloat16


def call(kernel, outs, in_specs, scratch=(), flops=0, need=0, after=(), aliases=None):
    outs = tuple(jax.ShapeDtypeStruct(shape, dtype) for shape, dtype in outs)
    late = len(after)
    run = pl.pallas_call(
        (lambda *refs: kernel(*refs[late:])) if late else kernel,
        out_shape=outs,
        in_specs=[ANY] * late + list(in_specs),
        out_specs=(VMEM,) * len(outs),
        input_output_aliases=aliases or {},
        scratch_shapes=scratch,
        compiler_params=pltpu.CompilerParams(vmem_limit_bytes=LEAST + need),
        cost_estimate=pl.CostEstimate(flops=flops, bytes_accessed=need, transcendentals=0),
    )
    return functools.partial(run, *after)


def ring_place(k, axis):
    return k ^ (k >> 1) if axis == "col" and lax.axis_size(axis) == 4 else k


def exchange(sends, axis, ahead):
    n = lax.axis_size(axis)

    def target(s, d):
        return ring_place((ring_place(s, axis) + (d if ahead else -d)) % n, axis)

    return [
        lax.ppermute(send, axis, [(s, target(s, d)) for s in range(n)])
        for d, send in enumerate(sends, 1)
    ]


def odd_row():
    return lax.rem(lax.axis_index("row"), 2) == 1


def start_order(n):
    return [*range(2, n), 1]


def swap(value, axis, distance):
    n = lax.axis_size(axis)
    return lax.ppermute(value, axis, [(s, s ^ distance) for s in range(n)])


def wide(value):
    return value.astype(jnp.float32)


def split(value):
    high = value.astype(NARROW)
    return high, (value - wide(high)).astype(NARROW)


def dot(left, right, dims=((1,), (0,))):
    return lax.dot_general(left, right, (dims, ((), ())), preferred_element_type=jnp.float32)


def zero_kernel(out):
    out[...] = jnp.zeros_like(out)


def dense_kernel(piece, paired, blank, vals, rows_in, cols_in, count_in, near, rows, cols, count, sems):
    copies = [
        pltpu.make_async_copy(source, target, sems.at[k])
        for k, (source, target) in enumerate(((rows_in, rows), (cols_in, cols), (count_in, count)))
    ]
    for copy in copies:
        copy.start()
    side = vals.shape[-1]
    for copy in copies:
        copy.wait()

    def ahead(there):
        n, here = lax.axis_size("col"), lax.axis_index("col")
        return lax.rem(ring_place(there, "col") - ring_place(here, "col") + n, n)

    def add(t, _):
        row, col = rows[0, 0, t], cols[0, 0, t]
        if paired:
            place = lax.rem((row // piece) ^ lax.axis_index("col"), 2) * 2 + row // piece // 2
        else:
            place = ahead(row // piece)
        row = place * piece + lax.rem(row, piece)
        col = ((col // piece) ^ lax.axis_index("row")) * piece + lax.rem(col, piece)
        down = pl.ds(pl.multiple_of(row * side, side), side)
        across = pl.ds(pl.multiple_of(col * side, side), side)
        near[down, across] = vals[0, 0, t]
        return 0

    lax.fori_loop(0, count[0, 0], add, 0)


def turn_kernel(step, near, far):
    def turn(k, _):
        band = pl.ds(pl.multiple_of(k * step, step), step)
        far[:, band] = near[band, :].T
        return 0

    lax.fori_loop(0, near.shape[0] // step, turn, 0)


def tree(terms):
    while len(terms) > 1:
        middle = len(terms) // 2
        terms = [left + right for left, right in zip(terms[:middle], terms[middle:])]
    return terms[0]


def stack(operands):
    own, *others = [operand[...] for operand in operands]
    order = start_order(len(operands))
    return jnp.concatenate([own] + [others[order.index(d)] for d in range(1, len(operands))], axis=0)


def forward_kernel(n, matrix, *refs):
    operands, own, sends = refs[:n], refs[n], refs[n + 1 :]
    rows = own.shape[0]
    product = dot(matrix[...], stack(operands))
    own[...] = product[:rows]
    for d, send in enumerate(sends, 1):
        send[...] = product[d * rows : (d + 1) * rows].astype(send.dtype)


def layer(total, weight, cotangent):
    high, low = split(total)
    pre = dot(high, weight) + dot(low, weight)
    sigma = jax.nn.sigmoid(pre)
    grad = wide(cotangent) * sigma * (1.0 + pre * (1.0 - sigma))
    grad_high, grad_low = split(grad)
    across, down = ((1,), (1,)), ((0,), (0,))
    back = dot(grad_high, weight, across) + dot(grad_low, weight, across)
    term = dot(high, grad_high, down) + dot(low, grad_high, down) + dot(high, grad_low, down)
    return pre, back, term


def halve(term, mine, other):
    half = mine.shape[1]
    odd = odd_row()
    left, right = term[:, :half], term[:, half:]
    mine[...] = jnp.where(odd, right, left)
    other[...] = jnp.where(odd, left, right).astype(other.dtype)


def layer_kernel(*refs):
    *parts, weight, cotangent, back_out, mine, other, pre_out = refs
    total = tree([wide(part[...]) for part in parts])
    pre, back, term = layer(total, weight[...], cotangent[...])
    pre_out[...] = pre
    back_out[...] = back.astype(back_out.dtype)
    halve(term, mine, other)


def in_middle():
    my_col = lax.axis_index("col")
    return (my_col == 1) | (my_col == 2)


def paired_forward_kernel(n, matrix, *refs):
    operands, (own, first, second, third) = refs[:n], refs[n:]
    product = dot(matrix[...], stack(operands)).astype(own.dtype)
    rows = own.shape[0]
    same, other = product[:rows], product[rows:]
    middle = in_middle()
    own[...] = same
    first[...] = jnp.where(middle, same, other)
    second[...] = other
    third[...] = jnp.where(middle, other, same)


def paired_layer_kernel(own, first, second, third, weight, cotangent, beyond, *refs):
    back_out, mine, other, pre_out = refs
    nodes = cotangent.shape[0]
    middle = in_middle()
    partner = jnp.where(middle, third[...], first[...])
    side = jnp.where(middle, first[...], third[...])
    total = (wide(own[...]) + wide(partner)) + (wide(second[...]) + wide(side))
    high_col = lax.axis_index("col") >= 2
    here, there = cotangent[...], beyond[...]
    both = jnp.concatenate(
        [jnp.where(high_col, there, here), jnp.where(high_col, here, there)], axis=0
    )
    pre, back, term = layer(total, weight[...], both)
    pre_out[...] = jnp.where(high_col, pre[nodes:], pre[:nodes])
    back_out[...] = back.astype(back_out.dtype)
    halve(term, mine, other)


def message_kernel(back, mine, came, message):
    nodes = back.shape[0]
    message[:nodes] = back[...]
    message[nodes:] = (mine[...] + wide(came[...])).astype(message.dtype)


def act_kernel(pre, act):
    act[...] = (pre[...] * jax.nn.sigmoid(pre[...])).astype(act.dtype)


def backward_kernel(n, matrix, *refs):
    messages, own, kept, sends = refs[:n], refs[n], refs[n + 1], refs[n + 2 :]
    rows, backs = own.shape[0], messages[0].shape[0] - kept.shape[0]
    stacked = jnp.concatenate([message[:backs] for message in messages], axis=0)
    product = dot(matrix[...], stacked)
    own[...] = product[:rows]
    term = tree([wide(message[backs:]) for message in messages]).astype(kept.dtype)
    kept[...] = term
    for d, send in enumerate(sends, 1):
        send[:rows] = product[d * rows : (d + 1) * rows].astype(send.dtype)
        send[rows:] = term


def last_kernel(scale, own, kept, *refs):
    *messages, features_out, weight_out = refs
    nodes, half = own.shape[0], kept.shape[1]
    features_out[...] = tree(
        [own[...]] + [wide(message[:nodes]) for message in messages]
    ).astype(features_out.dtype)
    terms = [wide(kept[...])] + [wide(message[nodes:]) for message in messages]
    mine, other = tree(terms[::2]) * scale, tree(terms[1::2]) * scale
    odd = odd_row()
    weight_out[:, :half] = jnp.where(odd, other, mine)
    weight_out[:, half:] = jnp.where(odd, mine, other)


def per_device(features, weight, cotangent, tile_values, tile_rows, tile_cols, tile_count):
    slots, side = tile_values.shape[2:4]
    n_row, n_col = lax.axis_size("row"), lax.axis_size("col")
    nodes, width = features.shape
    hidden = weight.shape[1]
    down, across = n_col * nodes, n_row * nodes
    dense_bytes = 2 * down * across

    paired = n_col == 4
    gathered = [swap(features, "row", d) for d in start_order(n_row)]
    (blank,) = call(zero_kernel, [((down, across), NARROW)], [], need=dense_bytes)()
    (near,) = call(
        functools.partial(dense_kernel, nodes // side, paired),
        [((down, across), NARROW)],
        [VMEM] * 5,
        aliases={0: 0},
        scratch=[
            pltpu.SMEM(tile_rows.shape, jnp.int32),
            pltpu.SMEM(tile_cols.shape, jnp.int32),
            pltpu.SMEM(tile_count.shape, jnp.int32),
            pltpu.SemaphoreType.DMA((3,)),
        ],
        need=2 * dense_bytes,
    )(blank, tile_values, tile_rows, tile_cols, tile_count)

    forward = dict(flops=2 * down * across * width, need=2 * dense_bytes)
    if paired:
        layers = 2
        own, *sends = call(
            functools.partial(paired_forward_kernel, n_row),
            [((2 * nodes, width), NARROW)] * 4,
            [VMEM] * (1 + n_row),
            **forward,
        )(near, features, *gathered)
        layer_call, cotangents = paired_layer_kernel, [cotangent, swap(cotangent, "col", 2)]
    else:
        layers = 1
        own, *sends = call(
            functools.partial(forward_kernel, n_row),
            [((nodes, width), jnp.float32)] + [((nodes, width), NARROW)] * (n_col - 1),
            [VMEM] * (1 + n_row),
            **forward,
        )(near, features, *gathered)
        layer_call, cotangents = layer_kernel, [cotangent]
    parts = exchange(sends, "col", True)
    (far,) = call(
        functools.partial(turn_kernel, side),
        [((across, down), NARROW)],
        [VMEM],
        need=3 * dense_bytes,
    )(near)

    half = hidden // 2
    square = (width, half)
    back, mine, other, pre = call(
        layer_call,
        [
            ((layers * nodes, width), NARROW),
            (square, jnp.float32),
            (square, NARROW),
            ((nodes, hidden), jnp.float32),
        ],
        [VMEM] * (n_col + 1 + len(cotangents)),
        flops=14 * layers * nodes * width * hidden,
        after=[far],
    )(own, *parts, weight, *cotangents)
    (sent,) = call(message_kernel, [((layers * nodes + width, width), NARROW)], [VMEM] * 3)(
        back, mine, swap(other, "row", 1)
    )
    if paired:
        spread = [swap(sent, "col", 1)]
    else:
        spread = exchange([sent] * (n_col - 1), "col", False)
    (act,) = call(act_kernel, [((nodes, hidden), NARROW)], [VMEM])(pre)

    message = ((nodes + width, width), NARROW)
    own, kept, *sends = call(
        functools.partial(backward_kernel, 1 + len(spread)),
        [((nodes, width), jnp.float32), (square, NARROW)] + [message] * (n_row - 1),
        [VMEM] * (2 + len(spread)),
        **forward,
    )(far, sent, *spread)
    parts = [swap(send, "row", d) for d, send in enumerate(sends, 1)]

    scale = float(nodes * n_row * n_col) ** -0.5
    grad_features, grad_weight = call(
        functools.partial(last_kernel, scale),
        [((nodes, width), NARROW), ((width, hidden), jnp.float32)],
        [VMEM] * (n_row + 1),
    )(own, kept, *parts)
    return act, grad_features, grad_weight


def solution(mesh):
    placed = (
        P(("groups", "row", "col"), None),
        P(),
        P(("groups", "row", "col"), None),
        P(("groups", "row"), "col", None, None, None),
        P(("groups", "row"), "col", None),
        P(("groups", "row"), "col", None),
        P(("groups", "row"), "col"),
    )
    return jax.shard_map(
        per_device,
        mesh=mesh,
        in_specs=placed,
        out_specs=(
            P(("groups", "row", "col"), None),
            P(("groups", "row", "col"), None),
            P("groups", None),
        ),
        check_vma=False,
    )
```

```python
import functools

import jax
import jax.numpy as jnp
from jax import lax
from jax.experimental import pallas as pl
from jax.experimental.pallas import tpu as pltpu
from jax.sharding import PartitionSpec as P

VMEM = pl.BlockSpec(memory_space=pltpu.VMEM)
ANY = pl.BlockSpec(memory_space=pl.ANY)
LEAST = 16 * 1024 * 1024
NARROW = jnp.bfloat16


def call(kernel, outs, in_specs, scratch=(), flops=0, need=0, after=(), aliases=None):
    outs = tuple(jax.ShapeDtypeStruct(shape, dtype) for shape, dtype in outs)
    late = len(after)
    run = pl.pallas_call(
        (lambda *refs: kernel(*refs[late:])) if late else kernel,
        out_shape=outs,
        in_specs=[ANY] * late + list(in_specs),
        out_specs=(VMEM,) * len(outs),
        input_output_aliases=aliases or {},
        scratch_shapes=scratch,
        compiler_params=pltpu.CompilerParams(vmem_limit_bytes=LEAST + need),
        cost_estimate=pl.CostEstimate(flops=flops, bytes_accessed=need, transcendentals=0),
    )
    return functools.partial(run, *after)


def ring_place(k, axis):
    return k ^ (k >> 1) if axis == "col" and lax.axis_size(axis) == 4 else k


def exchange(sends, axis, ahead):
    n = lax.axis_size(axis)

    def target(s, d):
        return ring_place((ring_place(s, axis) + (d if ahead else -d)) % n, axis)

    return [
        lax.ppermute(send, axis, [(s, target(s, d)) for s in range(n)])
        for d, send in enumerate(sends, 1)
    ]


def odd_row():
    return lax.rem(lax.axis_index("row"), 2) == 1


def start_order(n):
    return [*range(2, n), 1]


def swap(value, axis, distance):
    n = lax.axis_size(axis)
    return lax.ppermute(value, axis, [(s, s ^ distance) for s in range(n)])


def wide(value):
    return value.astype(jnp.float32)


def split(value):
    high = value.astype(NARROW)
    return high, (value - wide(high)).astype(NARROW)


def dot(left, right, dims=((1,), (0,))):
    return lax.dot_general(left, right, (dims, ((), ())), preferred_element_type=jnp.float32)


def zero_kernel(out):
    out[...] = jnp.zeros_like(out)


def dense_kernel(piece, paired, blank, vals, rows_in, cols_in, count_in, near, rows, cols, count, sems):
    copies = [
        pltpu.make_async_copy(source, target, sems.at[k])
        for k, (source, target) in enumerate(((rows_in, rows), (cols_in, cols), (count_in, count)))
    ]
    for copy in copies:
        copy.start()
    side = vals.shape[-1]
    for copy in copies:
        copy.wait()

    def ahead(there):
        n, here = lax.axis_size("col"), lax.axis_index("col")
        return lax.rem(ring_place(there, "col") - ring_place(here, "col") + n, n)

    def add(t, _):
        row, col = rows[0, 0, t], cols[0, 0, t]
        if paired:
            place = lax.rem((row // piece) ^ lax.axis_index("col"), 2) * 2 + row // piece // 2
        else:
            place = ahead(row // piece)
        row = place * piece + lax.rem(row, piece)
        col = ((col // piece) ^ lax.axis_index("row")) * piece + lax.rem(col, piece)
        down = pl.ds(pl.multiple_of(row * side, side), side)
        across = pl.ds(pl.multiple_of(col * side, side), side)
        near[down, across] = vals[0, 0, t]
        return 0

    lax.fori_loop(0, count[0, 0], add, 0)


def turn_kernel(step, near, far):
    def turn(k, _):
        band = pl.ds(pl.multiple_of(k * step, step), step)
        far[:, band] = near[band, :].T
        return 0

    lax.fori_loop(0, near.shape[0] // step, turn, 0)


def tree(terms):
    while len(terms) > 1:
        middle = len(terms) // 2
        terms = [left + right for left, right in zip(terms[:middle], terms[middle:])]
    return terms[0]


def stack(operands):
    own, *others = [operand[...] for operand in operands]
    order = start_order(len(operands))
    return jnp.concatenate([own] + [others[order.index(d)] for d in range(1, len(operands))], axis=0)


def forward_kernel(n, matrix, *refs):
    operands, own, sends = refs[:n], refs[n], refs[n + 1 :]
    rows = own.shape[0]
    product = dot(matrix[...], stack(operands))
    own[...] = product[:rows]
    for d, send in enumerate(sends, 1):
        send[...] = product[d * rows : (d + 1) * rows].astype(send.dtype)


def layer(total, weight, cotangent):
    high, low = split(total)
    pre = dot(high, weight) + dot(low, weight)
    sigma = jax.nn.sigmoid(pre)
    grad = wide(cotangent) * sigma * (1.0 + pre * (1.0 - sigma))
    grad_high, grad_low = split(grad)
    across, down = ((1,), (1,)), ((0,), (0,))
    back = dot(grad_high, weight, across) + dot(grad_low, weight, across)
    term = dot(high, grad_high, down) + dot(low, grad_high, down) + dot(high, grad_low, down)
    return pre, back, term


def halve(term, mine, other):
    half = mine.shape[1]
    odd = odd_row()
    left, right = term[:, :half], term[:, half:]
    mine[...] = jnp.where(odd, right, left)
    other[...] = jnp.where(odd, left, right).astype(other.dtype)


def layer_kernel(*refs):
    *parts, weight, cotangent, back_out, mine, other, pre_out = refs
    total = tree([wide(part[...]) for part in parts])
    pre, back, term = layer(total, weight[...], cotangent[...])
    pre_out[...] = pre
    back_out[...] = back.astype(back_out.dtype)
    halve(term, mine, other)


def in_middle():
    my_col = lax.axis_index("col")
    return (my_col == 1) | (my_col == 2)


def paired_forward_kernel(n, matrix, *refs):
    operands, (own, first, second, third) = refs[:n], refs[n:]
    product = dot(matrix[...], stack(operands)).astype(own.dtype)
    rows = own.shape[0]
    same, other = product[:rows], product[rows:]
    middle = in_middle()
    own[...] = same
    first[...] = jnp.where(middle, same, other)
    second[...] = other
    third[...] = jnp.where(middle, other, same)


def paired_layer_kernel(own, first, second, third, weight, cotangent, beyond, *refs):
    back_out, mine, other, pre_out = refs
    nodes = cotangent.shape[0]
    middle = in_middle()
    partner = jnp.where(middle, third[...], first[...])
    side = jnp.where(middle, first[...], third[...])
    total = (wide(own[...]) + wide(partner)) + (wide(second[...]) + wide(side))
    high_col = lax.axis_index("col") >= 2
    here, there = cotangent[...], beyond[...]
    both = jnp.concatenate(
        [jnp.where(high_col, there, here), jnp.where(high_col, here, there)], axis=0
    )
    pre, back, term = layer(total, weight[...], both)
    pre_out[...] = jnp.where(high_col, pre[nodes:], pre[:nodes])
    back_out[...] = back.astype(back_out.dtype)
    halve(term, mine, other)


def message_kernel(back, mine, came, message):
    nodes = back.shape[0]
    message[:nodes] = back[...]
    message[nodes:] = (mine[...] + wide(came[...])).astype(message.dtype)


def act_kernel(pre, act):
    act[...] = (pre[...] * jax.nn.sigmoid(pre[...])).astype(act.dtype)


def backward_kernel(n, matrix, *refs):
    messages, own, kept, sends, product = refs[:n], refs[n], refs[n + 1], refs[n + 2 : -1], refs[-1]
    rows, backs = own.shape[0], messages[0].shape[0] - kept.shape[0]
    stacked = jnp.concatenate([message[:backs] for message in messages], axis=0)
    product[...] = dot(matrix[...], stacked)
    own[...] = product[:rows]
    term = tree([wide(message[backs:]) for message in messages]).astype(kept.dtype)
    kept[...] = term
    here, size = lax.axis_index("row"), lax.axis_size("row")
    for d, send in enumerate(sends, 1):
        start = pl.multiple_of((lax.rem(here + d, size) ^ here) * rows, rows)
        send[:rows] = product[pl.ds(start, rows)].astype(send.dtype)
        send[rows:] = term


def last_kernel(scale, own, kept, *refs):
    *messages, features_out, weight_out = refs
    nodes, half = own.shape[0], kept.shape[1]
    features_out[...] = tree(
        [own[...]] + [wide(message[:nodes]) for message in messages]
    ).astype(features_out.dtype)
    terms = [wide(kept[...])] + [wide(message[nodes:]) for message in messages]
    mine, other = tree(terms[::2]) * scale, tree(terms[1::2]) * scale
    odd = odd_row()
    weight_out[:, :half] = jnp.where(odd, other, mine)
    weight_out[:, half:] = jnp.where(odd, mine, other)


def per_device(features, weight, cotangent, tile_values, tile_rows, tile_cols, tile_count):
    slots, side = tile_values.shape[2:4]
    n_row, n_col = lax.axis_size("row"), lax.axis_size("col")
    nodes, width = features.shape
    hidden = weight.shape[1]
    down, across = n_col * nodes, n_row * nodes
    dense_bytes = 2 * down * across

    paired = n_col == 4
    gathered = [swap(features, "row", d) for d in start_order(n_row)]
    (blank,) = call(zero_kernel, [((down, across), NARROW)], [], need=dense_bytes)()
    (near,) = call(
        functools.partial(dense_kernel, nodes // side, paired),
        [((down, across), NARROW)],
        [VMEM] * 5,
        aliases={0: 0},
        scratch=[
            pltpu.SMEM(tile_rows.shape, jnp.int32),
            pltpu.SMEM(tile_cols.shape, jnp.int32),
            pltpu.SMEM(tile_count.shape, jnp.int32),
            pltpu.SemaphoreType.DMA((3,)),
        ],
        need=2 * dense_bytes,
    )(blank, tile_values, tile_rows, tile_cols, tile_count)

    forward = dict(flops=2 * down * across * width, need=2 * dense_bytes)
    if paired:
        layers = 2
        own, *sends = call(
            functools.partial(paired_forward_kernel, n_row),
            [((2 * nodes, width), NARROW)] * 4,
            [VMEM] * (1 + n_row),
            **forward,
        )(near, features, *gathered)
        layer_call, cotangents = paired_layer_kernel, [cotangent, swap(cotangent, "col", 2)]
    else:
        layers = 1
        own, *sends = call(
            functools.partial(forward_kernel, n_row),
            [((nodes, width), jnp.float32)] + [((nodes, width), NARROW)] * (n_col - 1),
            [VMEM] * (1 + n_row),
            **forward,
        )(near, features, *gathered)
        layer_call, cotangents = layer_kernel, [cotangent]
    parts = exchange(sends, "col", True)
    (far,) = call(
        functools.partial(turn_kernel, side),
        [((across, down), NARROW)],
        [VMEM],
        need=3 * dense_bytes,
    )(near)

    half = hidden // 2
    square = (width, half)
    back, mine, other, pre = call(
        layer_call,
        [
            ((layers * nodes, width), NARROW),
            (square, jnp.float32),
            (square, NARROW),
            ((nodes, hidden), jnp.float32),
        ],
        [VMEM] * (n_col + 1 + len(cotangents)),
        flops=14 * layers * nodes * width * hidden,
        after=[far],
    )(own, *parts, weight, *cotangents)
    (sent,) = call(message_kernel, [((layers * nodes + width, width), NARROW)], [VMEM] * 3)(
        back, mine, swap(other, "row", 1)
    )
    if paired:
        spread = [swap(sent, "col", 1)]
    else:
        spread = exchange([sent] * (n_col - 1), "col", False)
    (act,) = call(act_kernel, [((nodes, hidden), NARROW)], [VMEM])(pre)

    message = ((nodes + width, width), NARROW)
    own, kept, *sends = call(
        functools.partial(backward_kernel, 1 + len(spread)),
        [((nodes, width), jnp.float32), (square, NARROW)] + [message] * (n_row - 1),
        [VMEM] * (2 + len(spread)),
        scratch=[pltpu.VMEM((across, width), jnp.float32)],
        **forward,
    )(far, sent, *spread)
    parts = exchange(sends, "row", True)

    scale = float(nodes * n_row * n_col) ** -0.5
    grad_features, grad_weight = call(
        functools.partial(last_kernel, scale),
        [((nodes, width), NARROW), ((width, hidden), jnp.float32)],
        [VMEM] * (n_row + 1),
    )(own, kept, *parts)
    return act, grad_features, grad_weight


def solution(mesh):
    placed = (
        P(("groups", "row", "col"), None),
        P(),
        P(("groups", "row", "col"), None),
        P(("groups", "row"), "col", None, None, None),
        P(("groups", "row"), "col", None),
        P(("groups", "row"), "col", None),
        P(("groups", "row"), "col"),
    )
    return jax.shard_map(
        per_device,
        mesh=mesh,
        in_specs=placed,
        out_specs=(
            P(("groups", "row", "col"), None),
            P(("groups", "row", "col"), None),
            P("groups", None),
        ),
        check_vma=False,
    )
```

```python
import functools

import jax
import jax.numpy as jnp
from jax import lax
from jax.experimental import pallas as pl
from jax.experimental.pallas import tpu as pltpu
from jax.sharding import PartitionSpec as P

VMEM = pl.BlockSpec(memory_space=pltpu.VMEM)
ANY = pl.BlockSpec(memory_space=pl.ANY)
LEAST = 16 * 1024 * 1024
NARROW = jnp.bfloat16


def call(kernel, outs, in_specs, scratch=(), flops=0, need=0, after=(), aliases=None):
    outs = tuple(jax.ShapeDtypeStruct(shape, dtype) for shape, dtype in outs)
    late = len(after)
    run = pl.pallas_call(
        (lambda *refs: kernel(*refs[late:])) if late else kernel,
        out_shape=outs,
        in_specs=[ANY] * late + list(in_specs),
        out_specs=(VMEM,) * len(outs),
        input_output_aliases=aliases or {},
        scratch_shapes=scratch,
        compiler_params=pltpu.CompilerParams(vmem_limit_bytes=LEAST + need),
        cost_estimate=pl.CostEstimate(flops=flops, bytes_accessed=need, transcendentals=0),
    )
    return functools.partial(run, *after)


def ring_place(k, axis):
    return k ^ (k >> 1) if axis == "col" and lax.axis_size(axis) == 4 else k


def exchange(sends, axis, ahead):
    n = lax.axis_size(axis)

    def target(s, d):
        return ring_place((ring_place(s, axis) + (d if ahead else -d)) % n, axis)

    return [
        lax.ppermute(send, axis, [(s, target(s, d)) for s in range(n)])
        for d, send in enumerate(sends, 1)
    ]


def odd_row():
    return lax.rem(lax.axis_index("row"), 2) == 1


def start_order(n):
    return [*range(2, n), 1]


def swap(value, axis, distance):
    n = lax.axis_size(axis)
    return lax.ppermute(value, axis, [(s, s ^ distance) for s in range(n)])


def wide(value):
    return value.astype(jnp.float32)


def split(value):
    high = value.astype(NARROW)
    return high, (value - wide(high)).astype(NARROW)


def dot(left, right, dims=((1,), (0,))):
    return lax.dot_general(left, right, (dims, ((), ())), preferred_element_type=jnp.float32)


def zero_kernel(out):
    out[...] = jnp.zeros_like(out)


def dense_kernel(piece, paired, blank, vals, rows_in, cols_in, count_in, near, rows, cols, count, sems):
    copies = [
        pltpu.make_async_copy(source, target, sems.at[k])
        for k, (source, target) in enumerate(((rows_in, rows), (cols_in, cols), (count_in, count)))
    ]
    for copy in copies:
        copy.start()
    side = vals.shape[-1]
    for copy in copies:
        copy.wait()

    def ahead(there):
        n, here = lax.axis_size("col"), lax.axis_index("col")
        return lax.rem(ring_place(there, "col") - ring_place(here, "col") + n, n)

    def add(t, _):
        row, col = rows[0, 0, t], cols[0, 0, t]
        if paired:
            place = lax.rem((row // piece) ^ lax.axis_index("col"), 2) * 2 + row // piece // 2
        else:
            place = ahead(row // piece)
        row = place * piece + lax.rem(row, piece)
        col = ((col // piece) ^ lax.axis_index("row")) * piece + lax.rem(col, piece)
        down = pl.ds(pl.multiple_of(row * side, side), side)
        across = pl.ds(pl.multiple_of(col * side, side), side)
        near[down, across] = vals[0, 0, t]
        return 0

    lax.fori_loop(0, count[0, 0], add, 0)


def turn_kernel(step, near, far):
    def turn(k, _):
        band = pl.ds(pl.multiple_of(k * step, step), step)
        far[:, band] = near[band, :].T
        return 0

    lax.fori_loop(0, near.shape[0] // step, turn, 0)


def tree(terms):
    while len(terms) > 1:
        middle = len(terms) // 2
        terms = [left + right for left, right in zip(terms[:middle], terms[middle:])]
    return terms[0]


def stack(operands):
    own, *others = [operand[...] for operand in operands]
    order = start_order(len(operands))
    return jnp.concatenate([own] + [others[order.index(d)] for d in range(1, len(operands))], axis=0)


def forward_kernel(n, matrix, *refs):
    operands, own, sends = refs[:n], refs[n], refs[n + 1 :]
    rows = own.shape[0]
    product = dot(matrix[...], stack(operands))
    own[...] = product[:rows]
    for d, send in enumerate(sends, 1):
        send[...] = product[d * rows : (d + 1) * rows].astype(send.dtype)


def layer(total, weight, cotangent):
    high, low = split(total)
    pre = dot(high, weight) + dot(low, weight)
    sigma = jax.nn.sigmoid(pre)
    grad = wide(cotangent) * sigma * (1.0 + pre * (1.0 - sigma))
    grad_high, grad_low = split(grad)
    across, down = ((1,), (1,)), ((0,), (0,))
    back = dot(grad_high, weight, across) + dot(grad_low, weight, across)
    term = dot(high, grad_high, down) + dot(low, grad_high, down) + dot(high, grad_low, down)
    return pre, back, term


def halve(term, mine, other):
    half = mine.shape[1]
    odd = odd_row()
    left, right = term[:, :half], term[:, half:]
    mine[...] = jnp.where(odd, right, left)
    other[...] = jnp.where(odd, left, right).astype(other.dtype)


def layer_kernel(*refs):
    *parts, weight, cotangent, back_out, mine, other, pre_out = refs
    total = tree([wide(part[...]) for part in parts])
    pre, back, term = layer(total, weight[...], cotangent[...])
    pre_out[...] = pre
    back_out[...] = back.astype(back_out.dtype)
    halve(term, mine, other)


def in_middle():
    my_col = lax.axis_index("col")
    return (my_col == 1) | (my_col == 2)


def paired_forward_kernel(n, matrix, *refs):
    operands, (own, first, second, third) = refs[:n], refs[n:]
    product = dot(matrix[...], stack(operands)).astype(own.dtype)
    rows = own.shape[0]
    same, other = product[:rows], product[rows:]
    middle = in_middle()
    own[...] = same
    first[...] = jnp.where(middle, same, other)
    second[...] = other
    third[...] = jnp.where(middle, other, same)


def paired_layer_kernel(own, first, second, third, weight, cotangent, beyond, *refs):
    back_out, mine, other, pre_out = refs
    nodes = cotangent.shape[0]
    middle = in_middle()
    partner = jnp.where(middle, third[...], first[...])
    side = jnp.where(middle, first[...], third[...])
    total = (wide(own[...]) + wide(partner)) + (wide(second[...]) + wide(side))
    high_col = lax.axis_index("col") >= 2
    here, there = cotangent[...], beyond[...]
    both = jnp.concatenate(
        [jnp.where(high_col, there, here), jnp.where(high_col, here, there)], axis=0
    )
    pre, back, term = layer(total, weight[...], both)
    pre_out[...] = jnp.where(high_col, pre[nodes:], pre[:nodes])
    back_out[...] = back.astype(back_out.dtype)
    halve(term, mine, other)


def add_kernel(mine, came, out):
    out[...] = (mine[...] + wide(came[...])).astype(out.dtype)


def act_kernel(pre, act):
    act[...] = (pre[...] * jax.nn.sigmoid(pre[...])).astype(act.dtype)


def backward_kernel(n, matrix, *refs):
    backs, halves, (own, kept, *sends, product) = refs[:n], refs[n : 2 * n], refs[2 * n :]
    rows = own.shape[0]
    product[...] = dot(matrix[...], jnp.concatenate([back[...] for back in backs], axis=0))
    own[...] = product[:rows]
    term = tree([wide(half[...]) for half in halves]).astype(kept.dtype)
    kept[...] = term
    here, size = lax.axis_index("row"), lax.axis_size("row")
    for d, send in enumerate(sends, 1):
        start = pl.multiple_of((lax.rem(here + d, size) ^ here) * rows, rows)
        send[:rows] = product[pl.ds(start, rows)].astype(send.dtype)
        send[rows:] = term


def last_kernel(scale, own, kept, *refs):
    *messages, features_out, weight_out = refs
    nodes, half = own.shape[0], kept.shape[1]
    features_out[...] = tree(
        [own[...]] + [wide(message[:nodes]) for message in messages]
    ).astype(features_out.dtype)
    terms = [wide(kept[...])] + [wide(message[nodes:]) for message in messages]
    mine, other = tree(terms[::2]) * scale, tree(terms[1::2]) * scale
    odd = odd_row()
    weight_out[:, :half] = jnp.where(odd, other, mine)
    weight_out[:, half:] = jnp.where(odd, mine, other)


def per_device(features, weight, cotangent, tile_values, tile_rows, tile_cols, tile_count):
    slots, side = tile_values.shape[2:4]
    n_row, n_col = lax.axis_size("row"), lax.axis_size("col")
    nodes, width = features.shape
    hidden = weight.shape[1]
    down, across = n_col * nodes, n_row * nodes
    dense_bytes = 2 * down * across

    paired = n_col == 4
    gathered = [swap(features, "row", d) for d in start_order(n_row)]
    (blank,) = call(zero_kernel, [((down, across), NARROW)], [], need=dense_bytes)()
    (near,) = call(
        functools.partial(dense_kernel, nodes // side, paired),
        [((down, across), NARROW)],
        [VMEM] * 5,
        aliases={0: 0},
        scratch=[
            pltpu.SMEM(tile_rows.shape, jnp.int32),
            pltpu.SMEM(tile_cols.shape, jnp.int32),
            pltpu.SMEM(tile_count.shape, jnp.int32),
            pltpu.SemaphoreType.DMA((3,)),
        ],
        need=2 * dense_bytes,
    )(blank, tile_values, tile_rows, tile_cols, tile_count)

    forward = dict(flops=2 * down * across * width, need=2 * dense_bytes)
    if paired:
        layers = 2
        own, *sends = call(
            functools.partial(paired_forward_kernel, n_row),
            [((2 * nodes, width), NARROW)] * 4,
            [VMEM] * (1 + n_row),
            **forward,
        )(near, features, *gathered)
        layer_call, cotangents = paired_layer_kernel, [cotangent, swap(cotangent, "col", 2)]
    else:
        layers = 1
        own, *sends = call(
            functools.partial(forward_kernel, n_row),
            [((nodes, width), jnp.float32)] + [((nodes, width), NARROW)] * (n_col - 1),
            [VMEM] * (1 + n_row),
            **forward,
        )(near, features, *gathered)
        layer_call, cotangents = layer_kernel, [cotangent]
    parts = exchange(sends, "col", True)
    (far,) = call(
        functools.partial(turn_kernel, side),
        [((across, down), NARROW)],
        [VMEM],
        need=3 * dense_bytes,
    )(near)

    half = hidden // 2
    square = (width, half)
    back, mine, other, pre = call(
        layer_call,
        [
            ((layers * nodes, width), NARROW),
            (square, jnp.float32),
            (square, NARROW),
            ((nodes, hidden), jnp.float32),
        ],
        [VMEM] * (n_col + 1 + len(cotangents)),
        flops=14 * layers * nodes * width * hidden,
        after=[far],
    )(own, *parts, weight, *cotangents)
    (term,) = call(add_kernel, [(square, NARROW)], [VMEM] * 2)(mine, swap(other, "row", 1))
    if paired:
        backs, terms = [back, swap(back, "col", 1)], [term, swap(term, "col", 1)]
    else:
        backs = [back] + exchange([back] * (n_col - 1), "col", False)
        terms = [term] + exchange([term] * (n_col - 1), "col", False)
    (act,) = call(act_kernel, [((nodes, hidden), NARROW)], [VMEM])(pre)

    message = ((nodes + width, width), NARROW)
    own, kept, *sends = call(
        functools.partial(backward_kernel, len(backs)),
        [((nodes, width), jnp.float32), (square, NARROW)] + [message] * (n_row - 1),
        [VMEM] * (1 + 2 * len(backs)),
        scratch=[pltpu.VMEM((across, width), jnp.float32)],
        **forward,
    )(far, *backs, *terms)
    parts = exchange(sends, "row", True)

    scale = float(nodes * n_row * n_col) ** -0.5
    grad_features, grad_weight = call(
        functools.partial(last_kernel, scale),
        [((nodes, width), NARROW), ((width, hidden), jnp.float32)],
        [VMEM] * (n_row + 1),
    )(own, kept, *parts)
    return act, grad_features, grad_weight


def solution(mesh):
    placed = (
        P(("groups", "row", "col"), None),
        P(),
        P(("groups", "row", "col"), None),
        P(("groups", "row"), "col", None, None, None),
        P(("groups", "row"), "col", None),
        P(("groups", "row"), "col", None),
        P(("groups", "row"), "col"),
    )
    return jax.shard_map(
        per_device,
        mesh=mesh,
        in_specs=placed,
        out_specs=(
            P(("groups", "row", "col"), None),
            P(("groups", "row", "col"), None),
            P("groups", None),
        ),
        check_vma=False,
    )
```

```python
import functools

import jax
import jax.numpy as jnp
from jax import lax
from jax.experimental import pallas as pl
from jax.experimental.pallas import tpu as pltpu
from jax.sharding import PartitionSpec as P

VMEM = pl.BlockSpec(memory_space=pltpu.VMEM)
ANY = pl.BlockSpec(memory_space=pl.ANY)
LEAST = 16 * 1024 * 1024
NARROW = jnp.bfloat16


def call(kernel, outs, in_specs, scratch=(), flops=0, need=0, after=(), aliases=None):
    outs = tuple(jax.ShapeDtypeStruct(shape, dtype) for shape, dtype in outs)
    late = len(after)
    run = pl.pallas_call(
        (lambda *refs: kernel(*refs[late:])) if late else kernel,
        out_shape=outs,
        in_specs=[ANY] * late + list(in_specs),
        out_specs=(VMEM,) * len(outs),
        input_output_aliases=aliases or {},
        scratch_shapes=scratch,
        compiler_params=pltpu.CompilerParams(vmem_limit_bytes=LEAST + need),
        cost_estimate=pl.CostEstimate(flops=flops, bytes_accessed=need, transcendentals=0),
    )
    return functools.partial(run, *after)


def ring_place(k, axis):
    return k ^ (k >> 1) if axis == "col" and lax.axis_size(axis) == 4 else k


def exchange(sends, axis, ahead):
    n = lax.axis_size(axis)

    def target(s, d):
        return ring_place((ring_place(s, axis) + (d if ahead else -d)) % n, axis)

    return [
        lax.ppermute(send, axis, [(s, target(s, d)) for s in range(n)])
        for d, send in enumerate(sends, 1)
    ]


def odd_row():
    return lax.rem(lax.axis_index("row"), 2) == 1


def start_order(n):
    return [*range(2, n), 1]


def swap(value, axis, distance):
    n = lax.axis_size(axis)
    return lax.ppermute(value, axis, [(s, s ^ distance) for s in range(n)])


def wide(value):
    return value.astype(jnp.float32)


def split(value):
    high = value.astype(NARROW)
    return high, (value - wide(high)).astype(NARROW)


def dot(left, right, dims=((1,), (0,))):
    return lax.dot_general(left, right, (dims, ((), ())), preferred_element_type=jnp.float32)


def zero_kernel(out):
    out[...] = jnp.zeros_like(out)


def dense_kernel(piece, paired, blank, vals, rows_in, cols_in, count_in, near, rows, cols, count, sems):
    copies = [
        pltpu.make_async_copy(source, target, sems.at[k])
        for k, (source, target) in enumerate(((rows_in, rows), (cols_in, cols), (count_in, count)))
    ]
    for copy in copies:
        copy.start()
    side = vals.shape[-1]
    for copy in copies:
        copy.wait()

    def ahead(there):
        n, here = lax.axis_size("col"), lax.axis_index("col")
        return lax.rem(ring_place(there, "col") - ring_place(here, "col") + n, n)

    def add(t, _):
        row, col = rows[0, 0, t], cols[0, 0, t]
        if paired:
            place = lax.rem((row // piece) ^ lax.axis_index("col"), 2) * 2 + row // piece // 2
        else:
            place = ahead(row // piece)
        row = place * piece + lax.rem(row, piece)
        col = ((col // piece) ^ lax.axis_index("row")) * piece + lax.rem(col, piece)
        down = pl.ds(pl.multiple_of(row * side, side), side)
        across = pl.ds(pl.multiple_of(col * side, side), side)
        near[down, across] = vals[0, 0, t]
        return 0

    lax.fori_loop(0, count[0, 0], add, 0)


def turn_kernel(step, near, far):
    def turn(k, _):
        band = pl.ds(pl.multiple_of(k * step, step), step)
        far[:, band] = near[band, :].T
        return 0

    lax.fori_loop(0, near.shape[0] // step, turn, 0)


def tree(terms):
    while len(terms) > 1:
        middle = len(terms) // 2
        terms = [left + right for left, right in zip(terms[:middle], terms[middle:])]
    return terms[0]


def stack(operands):
    own, *others = [operand[...] for operand in operands]
    order = start_order(len(operands))
    return jnp.concatenate([own] + [others[order.index(d)] for d in range(1, len(operands))], axis=0)


def forward_kernel(n, matrix, *refs):
    operands, own, sends = refs[:n], refs[n], refs[n + 1 :]
    rows = own.shape[0]
    product = dot(matrix[...], stack(operands))
    own[...] = product[:rows]
    for d, send in enumerate(sends, 1):
        send[...] = product[d * rows : (d + 1) * rows].astype(send.dtype)


def layer(total, weight, cotangent):
    high, low = split(total)
    pre = dot(high, weight) + dot(low, weight)
    sigma = jax.nn.sigmoid(pre)
    grad = wide(cotangent) * sigma * (1.0 + pre * (1.0 - sigma))
    grad_high, grad_low = split(grad)
    across, down = ((1,), (1,)), ((0,), (0,))
    back = dot(grad_high, weight, across) + dot(grad_low, weight, across)
    term = dot(high, grad_high, down) + dot(low, grad_high, down) + dot(high, grad_low, down)
    return pre, back, term


def halve(term, mine, other):
    half = mine.shape[1]
    odd = odd_row()
    left, right = term[:, :half], term[:, half:]
    mine[...] = jnp.where(odd, right, left)
    other[...] = jnp.where(odd, left, right).astype(other.dtype)


def layer_kernel(*refs):
    *parts, weight, cotangent, back_out, mine, other, pre_out = refs
    total = tree([wide(part[...]) for part in parts])
    pre, back, term = layer(total, weight[...], cotangent[...])
    pre_out[...] = pre
    back_out[...] = back.astype(back_out.dtype)
    halve(term, mine, other)


def in_middle():
    my_col = lax.axis_index("col")
    return (my_col == 1) | (my_col == 2)


def paired_forward_kernel(n, matrix, *refs):
    operands, (own, first, second, third) = refs[:n], refs[n:]
    product = dot(matrix[...], stack(operands)).astype(own.dtype)
    rows = own.shape[0]
    same, other = product[:rows], product[rows:]
    middle = in_middle()
    own[...] = same
    first[...] = jnp.where(middle, same, other)
    second[...] = other
    third[...] = jnp.where(middle, other, same)


def paired_layer_kernel(own, first, second, third, weight, cotangent, beyond, *refs):
    back_out, mine, other, pre_out = refs
    nodes = cotangent.shape[0]
    middle = in_middle()
    partner = jnp.where(middle, third[...], first[...])
    side = jnp.where(middle, first[...], third[...])
    total = (wide(own[...]) + wide(partner)) + (wide(second[...]) + wide(side))
    high_col = lax.axis_index("col") >= 2
    here, there = cotangent[...], beyond[...]
    both = jnp.concatenate(
        [jnp.where(high_col, there, here), jnp.where(high_col, here, there)], axis=0
    )
    pre, back, term = layer(total, weight[...], both)
    pre_out[...] = jnp.where(high_col, pre[nodes:], pre[:nodes])
    back_out[...] = back.astype(back_out.dtype)
    halve(term, mine, other)


def add_kernel(mine, came, out):
    out[...] = (mine[...] + wide(came[...])).astype(out.dtype)


def act_kernel(pre, act):
    act[...] = (pre[...] * jax.nn.sigmoid(pre[...])).astype(act.dtype)


def backward_kernel(n, matrix, *refs):
    backs, halves, (own, kept, *sends, product) = refs[:n], refs[n : 2 * n], refs[2 * n :]
    rows = own.shape[0]
    product[...] = dot(matrix[...], jnp.concatenate([back[...] for back in backs], axis=0))
    own[...] = product[:rows]
    term = tree([wide(half[...]) for half in halves]).astype(kept.dtype)
    kept[...] = term
    here, size = lax.axis_index("row"), lax.axis_size("row")
    for d, send in enumerate(sends, 1):
        start = pl.multiple_of((lax.rem(here + d, size) ^ here) * rows, rows)
        send[:rows] = product[pl.ds(start, rows)].astype(send.dtype)
        send[rows:] = term


def last_kernel(scale, own, kept, *refs):
    *messages, features_out, weight_out = refs
    nodes, half = own.shape[0], kept.shape[1]
    features_out[...] = tree(
        [own[...]] + [wide(message[:nodes]) for message in messages]
    ).astype(features_out.dtype)
    terms = [wide(kept[...])] + [wide(message[nodes:]) for message in messages]
    mine, other = tree(terms[::2]) * scale, tree(terms[1::2]) * scale
    odd = odd_row()
    weight_out[:, :half] = jnp.where(odd, other, mine)
    weight_out[:, half:] = jnp.where(odd, mine, other)


def per_device(features, weight, cotangent, tile_values, tile_rows, tile_cols, tile_count):
    slots, side = tile_values.shape[2:4]
    n_row, n_col = lax.axis_size("row"), lax.axis_size("col")
    nodes, width = features.shape
    hidden = weight.shape[1]
    down, across = n_col * nodes, n_row * nodes
    dense_bytes = 2 * down * across

    paired = n_col == 4
    gathered = [swap(features, "row", d) for d in start_order(n_row)]
    (blank,) = call(zero_kernel, [((down, across), NARROW)], [], need=dense_bytes)()
    (near,) = call(
        functools.partial(dense_kernel, nodes // side, paired),
        [((down, across), NARROW)],
        [VMEM] * 5,
        aliases={0: 0},
        scratch=[
            pltpu.SMEM(tile_rows.shape, jnp.int32),
            pltpu.SMEM(tile_cols.shape, jnp.int32),
            pltpu.SMEM(tile_count.shape, jnp.int32),
            pltpu.SemaphoreType.DMA((3,)),
        ],
        need=2 * dense_bytes,
    )(blank, tile_values, tile_rows, tile_cols, tile_count)

    forward = dict(flops=2 * down * across * width, need=2 * dense_bytes)
    if paired:
        layers = 2
        cotangents = [cotangent, swap(cotangent, "col", 2)]
        own, *sends = call(
            functools.partial(paired_forward_kernel, n_row),
            [((2 * nodes, width), NARROW)] * 4,
            [VMEM] * (1 + n_row),
            after=cotangents[1:],
            **forward,
        )(near, features, *gathered)
        layer_call = paired_layer_kernel
    else:
        layers = 1
        own, *sends = call(
            functools.partial(forward_kernel, n_row),
            [((nodes, width), jnp.float32)] + [((nodes, width), NARROW)] * (n_col - 1),
            [VMEM] * (1 + n_row),
            **forward,
        )(near, features, *gathered)
        layer_call, cotangents = layer_kernel, [cotangent]
    parts = exchange(sends, "col", True)
    (far,) = call(
        functools.partial(turn_kernel, side),
        [((across, down), NARROW)],
        [VMEM],
        need=3 * dense_bytes,
    )(near)

    half = hidden // 2
    square = (width, half)
    back, mine, other, pre = call(
        layer_call,
        [
            ((layers * nodes, width), NARROW),
            (square, jnp.float32),
            (square, NARROW),
            ((nodes, hidden), jnp.float32),
        ],
        [VMEM] * (n_col + 1 + len(cotangents)),
        flops=14 * layers * nodes * width * hidden,
        after=[far],
    )(own, *parts, weight, *cotangents)
    (term,) = call(add_kernel, [(square, NARROW)], [VMEM] * 2)(mine, swap(other, "row", 1))
    if paired:
        backs, terms = [back, swap(back, "col", 1)], [term, swap(term, "col", 1)]
    else:
        backs = [back] + exchange([back] * (n_col - 1), "col", False)
        terms = [term] + exchange([term] * (n_col - 1), "col", False)
    (act,) = call(act_kernel, [((nodes, hidden), NARROW)], [VMEM])(pre)

    message = ((nodes + width, width), NARROW)
    own, kept, *sends = call(
        functools.partial(backward_kernel, len(backs)),
        [((nodes, width), jnp.float32), (square, NARROW)] + [message] * (n_row - 1),
        [VMEM] * (1 + 2 * len(backs)),
        scratch=[pltpu.VMEM((across, width), jnp.float32)],
        **forward,
    )(far, *backs, *terms)
    parts = exchange(sends, "row", True)

    scale = float(nodes * n_row * n_col) ** -0.5
    grad_features, grad_weight = call(
        functools.partial(last_kernel, scale),
        [((nodes, width), NARROW), ((width, hidden), jnp.float32)],
        [VMEM] * (n_row + 1),
    )(own, kept, *parts)
    return act, grad_features, grad_weight


def solution(mesh):
    placed = (
        P(("groups", "row", "col"), None),
        P(),
        P(("groups", "row", "col"), None),
        P(("groups", "row"), "col", None, None, None),
        P(("groups", "row"), "col", None),
        P(("groups", "row"), "col", None),
        P(("groups", "row"), "col"),
    )
    return jax.shard_map(
        per_device,
        mesh=mesh,
        in_specs=placed,
        out_specs=(
            P(("groups", "row", "col"), None),
            P(("groups", "row", "col"), None),
            P("groups", None),
        ),
        check_vma=False,
    )
```

```python
import functools

import jax
import jax.numpy as jnp
from jax import lax
from jax.experimental import pallas as pl
from jax.experimental.pallas import tpu as pltpu
from jax.sharding import PartitionSpec as P

VMEM = pl.BlockSpec(memory_space=pltpu.VMEM)
ANY = pl.BlockSpec(memory_space=pl.ANY)
LEAST = 16 * 1024 * 1024
NARROW = jnp.bfloat16


def call(kernel, outs, in_specs, scratch=(), flops=0, need=0, after=(), aliases=None):
    outs = tuple(jax.ShapeDtypeStruct(shape, dtype) for shape, dtype in outs)
    late = len(after)
    run = pl.pallas_call(
        (lambda *refs: kernel(*refs[late:])) if late else kernel,
        out_shape=outs,
        in_specs=[ANY] * late + list(in_specs),
        out_specs=(VMEM,) * len(outs),
        input_output_aliases=aliases or {},
        scratch_shapes=scratch,
        compiler_params=pltpu.CompilerParams(vmem_limit_bytes=LEAST + need),
        cost_estimate=pl.CostEstimate(flops=flops, bytes_accessed=need, transcendentals=0),
    )
    return functools.partial(run, *after)


def ring_place(k, axis):
    return k ^ (k >> 1) if axis == "col" and lax.axis_size(axis) == 4 else k


def exchange(sends, axis, ahead):
    n = lax.axis_size(axis)

    def target(s, d):
        return ring_place((ring_place(s, axis) + (d if ahead else -d)) % n, axis)

    return [
        lax.ppermute(send, axis, [(s, target(s, d)) for s in range(n)])
        for d, send in enumerate(sends, 1)
    ]


def odd_row():
    return lax.rem(lax.axis_index("row"), 2) == 1


def start_order(n):
    return [*range(2, n), 1]


def swap(value, axis, distance):
    n = lax.axis_size(axis)
    return lax.ppermute(value, axis, [(s, s ^ distance) for s in range(n)])


def wide(value):
    return value.astype(jnp.float32)


def split(value):
    high = value.astype(NARROW)
    return high, (value - wide(high)).astype(NARROW)


def dot(left, right, dims=((1,), (0,))):
    return lax.dot_general(left, right, (dims, ((), ())), preferred_element_type=jnp.float32)


def zero_kernel(out):
    out[...] = jnp.zeros_like(out)


def dense_kernel(piece, paired, blank, vals, rows_in, cols_in, count_in, near, rows, cols, count, sems):
    copies = [
        pltpu.make_async_copy(source, target, sems.at[k])
        for k, (source, target) in enumerate(((rows_in, rows), (cols_in, cols), (count_in, count)))
    ]
    for copy in copies:
        copy.start()
    side = vals.shape[-1]
    for copy in copies:
        copy.wait()

    def ahead(there):
        n, here = lax.axis_size("col"), lax.axis_index("col")
        return lax.rem(ring_place(there, "col") - ring_place(here, "col") + n, n)

    def add(t, _):
        row, col = rows[0, 0, t], cols[0, 0, t]
        if paired:
            place = lax.rem((row // piece) ^ lax.axis_index("col"), 2) * 2 + row // piece // 2
        else:
            place = ahead(row // piece)
        row = place * piece + lax.rem(row, piece)
        col = ((col // piece) ^ lax.axis_index("row")) * piece + lax.rem(col, piece)
        down = pl.ds(pl.multiple_of(row * side, side), side)
        across = pl.ds(pl.multiple_of(col * side, side), side)
        near[down, across] = vals[0, 0, t]
        return 0

    lax.fori_loop(0, count[0, 0], add, 0)


def turn_kernel(step, near, far):
    def turn(k, _):
        band = pl.ds(pl.multiple_of(k * step, step), step)
        far[:, band] = near[band, :].T
        return 0

    lax.fori_loop(0, near.shape[0] // step, turn, 0)


def tree(terms):
    while len(terms) > 1:
        middle = len(terms) // 2
        terms = [left + right for left, right in zip(terms[:middle], terms[middle:])]
    return terms[0]


def stack(operands):
    own, *others = [operand[...] for operand in operands]
    order = start_order(len(operands))
    return jnp.concatenate([own] + [others[order.index(d)] for d in range(1, len(operands))], axis=0)


def forward_kernel(n, matrix, *refs):
    operands, own, sends = refs[:n], refs[n], refs[n + 1 :]
    rows = own.shape[0]
    product = dot(matrix[...], stack(operands))
    own[...] = product[:rows]
    for d, send in enumerate(sends, 1):
        send[...] = product[d * rows : (d + 1) * rows].astype(send.dtype)


def layer(total, weight, cotangent):
    high, low = split(total)
    pre = dot(high, weight) + dot(low, weight)
    sigma = jax.nn.sigmoid(pre)
    grad = wide(cotangent) * sigma * (1.0 + pre * (1.0 - sigma))
    grad_high, grad_low = split(grad)
    across, down = ((1,), (1,)), ((0,), (0,))
    back = dot(grad_high, weight, across) + dot(grad_low, weight, across)
    term = dot(high, grad_high, down) + dot(low, grad_high, down) + dot(high, grad_low, down)
    return pre, back, term


def halve(term, mine, other):
    half = mine.shape[1]
    odd = odd_row()
    left, right = term[:, :half], term[:, half:]
    mine[...] = jnp.where(odd, right, left)
    other[...] = jnp.where(odd, left, right).astype(other.dtype)


def layer_kernel(*refs):
    *parts, weight, cotangent, back_out, mine, other, pre_out = refs
    total = tree([wide(part[...]) for part in parts])
    pre, back, term = layer(total, weight[...], cotangent[...])
    pre_out[...] = pre
    back_out[...] = back.astype(back_out.dtype)
    halve(term, mine, other)


def paired_forward_kernel(n, matrix, *refs):
    operands, (same, other) = refs[:n], refs[n:]
    product = dot(matrix[...], stack(operands)).astype(same.dtype)
    rows = same.shape[0]
    same[...] = product[:rows]
    other[...] = product[rows:]


def paired_layer_kernel(own, first, second, third, weight, cotangent, beyond, *refs):
    back_out, mine, other, pre_out = refs
    nodes = cotangent.shape[0]
    total = (wide(own[...]) + wide(second[...])) + (wide(first[...]) + wide(third[...]))
    high_col = lax.axis_index("col") >= 2
    here, there = cotangent[...], beyond[...]
    both = jnp.concatenate(
        [jnp.where(high_col, there, here), jnp.where(high_col, here, there)], axis=0
    )
    pre, back, term = layer(total, weight[...], both)
    pre_out[...] = jnp.where(high_col, pre[nodes:], pre[:nodes])
    back_out[...] = back.astype(back_out.dtype)
    halve(term, mine, other)


def add_kernel(mine, came, out):
    out[...] = (mine[...] + wide(came[...])).astype(out.dtype)


def act_kernel(pre, act):
    act[...] = (pre[...] * jax.nn.sigmoid(pre[...])).astype(act.dtype)


def backward_kernel(n, matrix, *refs):
    backs, halves, (own, kept, *sends, product) = refs[:n], refs[n : 2 * n], refs[2 * n :]
    rows = own.shape[0]
    product[...] = dot(matrix[...], jnp.concatenate([back[...] for back in backs], axis=0))
    own[...] = product[:rows]
    term = tree([wide(half[...]) for half in halves]).astype(kept.dtype)
    kept[...] = term
    here, size = lax.axis_index("row"), lax.axis_size("row")
    for d, send in enumerate(sends, 1):
        start = pl.multiple_of((lax.rem(here + d, size) ^ here) * rows, rows)
        send[:rows] = product[pl.ds(start, rows)].astype(send.dtype)
        send[rows:] = term


def last_kernel(scale, own, kept, *refs):
    *messages, features_out, weight_out = refs
    nodes, half = own.shape[0], kept.shape[1]
    features_out[...] = tree(
        [own[...]] + [wide(message[:nodes]) for message in messages]
    ).astype(features_out.dtype)
    terms = [wide(kept[...])] + [wide(message[nodes:]) for message in messages]
    mine, other = tree(terms[::2]) * scale, tree(terms[1::2]) * scale
    odd = odd_row()
    weight_out[:, :half] = jnp.where(odd, other, mine)
    weight_out[:, half:] = jnp.where(odd, mine, other)


def per_device(features, weight, cotangent, tile_values, tile_rows, tile_cols, tile_count):
    slots, side = tile_values.shape[2:4]
    n_row, n_col = lax.axis_size("row"), lax.axis_size("col")
    nodes, width = features.shape
    hidden = weight.shape[1]
    down, across = n_col * nodes, n_row * nodes
    dense_bytes = 2 * down * across

    paired = n_col == 4
    gathered = [swap(features, "row", d) for d in start_order(n_row)]
    (blank,) = call(zero_kernel, [((down, across), NARROW)], [], need=dense_bytes)()
    (near,) = call(
        functools.partial(dense_kernel, nodes // side, paired),
        [((down, across), NARROW)],
        [VMEM] * 5,
        aliases={0: 0},
        scratch=[
            pltpu.SMEM(tile_rows.shape, jnp.int32),
            pltpu.SMEM(tile_cols.shape, jnp.int32),
            pltpu.SMEM(tile_count.shape, jnp.int32),
            pltpu.SemaphoreType.DMA((3,)),
        ],
        need=2 * dense_bytes,
    )(blank, tile_values, tile_rows, tile_cols, tile_count)

    forward = dict(flops=2 * down * across * width, need=2 * dense_bytes)
    if paired:
        layers = 2
        own, other = call(
            functools.partial(paired_forward_kernel, n_row),
            [((2 * nodes, width), NARROW)] * 2,
            [VMEM] * (1 + n_row),
            **forward,
        )(near, features, *gathered)
        parts = [swap(send, "col", d) for d, send in enumerate([other, own, other], 1)]
        layer_call, cotangents = paired_layer_kernel, [cotangent, swap(cotangent, "col", 2)]
    else:
        layers = 1
        own, *sends = call(
            functools.partial(forward_kernel, n_row),
            [((nodes, width), jnp.float32)] + [((nodes, width), NARROW)] * (n_col - 1),
            [VMEM] * (1 + n_row),
            **forward,
        )(near, features, *gathered)
        layer_call, cotangents = layer_kernel, [cotangent]
        parts = exchange(sends, "col", True)
    (far,) = call(
        functools.partial(turn_kernel, side),
        [((across, down), NARROW)],
        [VMEM],
        need=3 * dense_bytes,
    )(near)

    half = hidden // 2
    square = (width, half)
    back, mine, other, pre = call(
        layer_call,
        [
            ((layers * nodes, width), NARROW),
            (square, jnp.float32),
            (square, NARROW),
            ((nodes, hidden), jnp.float32),
        ],
        [VMEM] * (n_col + 1 + len(cotangents)),
        flops=14 * layers * nodes * width * hidden,
        after=[far],
    )(own, *parts, weight, *cotangents)
    (term,) = call(add_kernel, [(square, NARROW)], [VMEM] * 2)(mine, swap(other, "row", 1))
    if paired:
        backs, terms = [back, swap(back, "col", 1)], [term, swap(term, "col", 1)]
    else:
        backs = [back] + exchange([back] * (n_col - 1), "col", False)
        terms = [term] + exchange([term] * (n_col - 1), "col", False)
    (act,) = call(act_kernel, [((nodes, hidden), NARROW)], [VMEM])(pre)

    message = ((nodes + width, width), NARROW)
    own, kept, *sends = call(
        functools.partial(backward_kernel, len(backs)),
        [((nodes, width), jnp.float32), (square, NARROW)] + [message] * (n_row - 1),
        [VMEM] * (1 + 2 * len(backs)),
        scratch=[pltpu.VMEM((across, width), jnp.float32)],
        **forward,
    )(far, *backs, *terms)
    parts = exchange(sends, "row", True)

    scale = float(nodes * n_row * n_col) ** -0.5
    grad_features, grad_weight = call(
        functools.partial(last_kernel, scale),
        [((nodes, width), NARROW), ((width, hidden), jnp.float32)],
        [VMEM] * (n_row + 1),
    )(own, kept, *parts)
    return act, grad_features, grad_weight


def solution(mesh):
    placed = (
        P(("groups", "row", "col"), None),
        P(),
        P(("groups", "row", "col"), None),
        P(("groups", "row"), "col", None, None, None),
        P(("groups", "row"), "col", None),
        P(("groups", "row"), "col", None),
        P(("groups", "row"), "col"),
    )
    return jax.shard_map(
        per_device,
        mesh=mesh,
        in_specs=placed,
        out_specs=(
            P(("groups", "row", "col"), None),
            P(("groups", "row", "col"), None),
            P("groups", None),
        ),
        check_vma=False,
    )
```

```python
import functools

import jax
import jax.numpy as jnp
from jax import lax
from jax.experimental import pallas as pl
from jax.experimental.pallas import tpu as pltpu
from jax.sharding import PartitionSpec as P

VMEM = pl.BlockSpec(memory_space=pltpu.VMEM)
ANY = pl.BlockSpec(memory_space=pl.ANY)
LEAST = 16 * 1024 * 1024
NARROW = jnp.bfloat16


def call(kernel, outs, in_specs, scratch=(), flops=0, need=0, after=(), aliases=None):
    outs = tuple(jax.ShapeDtypeStruct(shape, dtype) for shape, dtype in outs)
    late = len(after)
    run = pl.pallas_call(
        (lambda *refs: kernel(*refs[late:])) if late else kernel,
        out_shape=outs,
        in_specs=[ANY] * late + list(in_specs),
        out_specs=(VMEM,) * len(outs),
        input_output_aliases=aliases or {},
        scratch_shapes=scratch,
        compiler_params=pltpu.CompilerParams(vmem_limit_bytes=LEAST + need),
        cost_estimate=pl.CostEstimate(flops=flops, bytes_accessed=need, transcendentals=0),
    )
    return functools.partial(run, *after)


def ring_place(k, axis):
    return k ^ (k >> 1) if axis == "col" and lax.axis_size(axis) == 4 else k


def exchange(sends, axis, ahead):
    n = lax.axis_size(axis)

    def target(s, d):
        return ring_place((ring_place(s, axis) + (d if ahead else -d)) % n, axis)

    return [
        lax.ppermute(send, axis, [(s, target(s, d)) for s in range(n)])
        for d, send in enumerate(sends, 1)
    ]


def odd_row():
    return lax.rem(lax.axis_index("row"), 2) == 1


def start_order(n):
    return [*range(2, n), 1]


def swap(value, axis, distance):
    n = lax.axis_size(axis)
    return lax.ppermute(value, axis, [(s, s ^ distance) for s in range(n)])


def wide(value):
    return value.astype(jnp.float32)


def split(value):
    high = value.astype(NARROW)
    return high, (value - wide(high)).astype(NARROW)


def dot(left, right, dims=((1,), (0,))):
    return lax.dot_general(left, right, (dims, ((), ())), preferred_element_type=jnp.float32)


def zero_kernel(out):
    out[...] = jnp.zeros_like(out)


def dense_kernel(piece, paired, blank, vals, rows_in, cols_in, count_in, near, rows, cols, count, sems):
    copies = [
        pltpu.make_async_copy(source, target, sems.at[k])
        for k, (source, target) in enumerate(((rows_in, rows), (cols_in, cols), (count_in, count)))
    ]
    for copy in copies:
        copy.start()
    side = vals.shape[-1]
    for copy in copies:
        copy.wait()

    def ahead(there):
        n, here = lax.axis_size("col"), lax.axis_index("col")
        return lax.rem(ring_place(there, "col") - ring_place(here, "col") + n, n)

    def add(t, _):
        row, col = rows[0, 0, t], cols[0, 0, t]
        if paired:
            place = lax.rem((row // piece) ^ lax.axis_index("col"), 2) * 2 + row // piece // 2
        else:
            place = ahead(row // piece)
        row = place * piece + lax.rem(row, piece)
        col = ((col // piece) ^ lax.axis_index("row")) * piece + lax.rem(col, piece)
        down = pl.ds(pl.multiple_of(row * side, side), side)
        across = pl.ds(pl.multiple_of(col * side, side), side)
        near[down, across] = vals[0, 0, t]
        return 0

    lax.fori_loop(0, count[0, 0], add, 0)


def turn_kernel(step, near, far):
    def turn(k, _):
        band = pl.ds(pl.multiple_of(k * step, step), step)
        far[:, band] = near[band, :].T
        return 0

    lax.fori_loop(0, near.shape[0] // step, turn, 0)


def tree(terms):
    while len(terms) > 1:
        middle = len(terms) // 2
        terms = [left + right for left, right in zip(terms[:middle], terms[middle:])]
    return terms[0]


def stack(operands):
    own, *others = [operand[...] for operand in operands]
    order = start_order(len(operands))
    return jnp.concatenate([own] + [others[order.index(d)] for d in range(1, len(operands))], axis=0)


def forward_kernel(n, matrix, *refs):
    operands, own, sends = refs[:n], refs[n], refs[n + 1 :]
    rows = own.shape[0]
    product = dot(matrix[...], stack(operands))
    own[...] = product[:rows]
    for d, send in enumerate(sends, 1):
        send[...] = product[d * rows : (d + 1) * rows].astype(send.dtype)


def layer(total, weight, cotangent):
    high, low = split(total)
    pre = dot(high, weight) + dot(low, weight)
    sigma = jax.nn.sigmoid(pre)
    grad = wide(cotangent) * sigma * (1.0 + pre * (1.0 - sigma))
    grad_high, grad_low = split(grad)
    across, down = ((1,), (1,)), ((0,), (0,))
    back = dot(grad_high, weight, across) + dot(grad_low, weight, across)
    term = dot(high, grad_high, down) + dot(low, grad_high, down) + dot(high, grad_low, down)
    return pre, back, term


def halve(term, mine, other):
    half = mine.shape[1]
    odd = odd_row()
    left, right = term[:, :half], term[:, half:]
    mine[...] = jnp.where(odd, right, left)
    other[...] = jnp.where(odd, left, right).astype(other.dtype)


def layer_kernel(*refs):
    *parts, weight, cotangent, back_out, mine, other, pre_out = refs
    total = tree([wide(part[...]) for part in parts])
    pre, back, term = layer(total, weight[...], cotangent[...])
    pre_out[...] = pre
    back_out[...] = back.astype(back_out.dtype)
    halve(term, mine, other)


def in_middle():
    my_col = lax.axis_index("col")
    return (my_col == 1) | (my_col == 2)


def paired_forward_kernel(n, matrix, *refs):
    operands, (own, first, second, third) = refs[:n], refs[n:]
    product = dot(matrix[...], stack(operands)).astype(own.dtype)
    rows = own.shape[0]
    same, other = product[:rows], product[rows:]
    middle = in_middle()
    own[...] = same
    first[...] = jnp.where(middle, same, other)
    second[...] = other
    third[...] = jnp.where(middle, other, same)


def paired_layer_kernel(own, first, third, second, weight, cotangent, beyond, *refs):
    back_out, mine, other, pre_out = refs
    nodes = cotangent.shape[0]
    middle = in_middle()
    partner = jnp.where(middle, third[...], first[...])
    side = jnp.where(middle, first[...], third[...])
    total = (wide(own[...]) + wide(partner)) + (wide(second[...]) + wide(side))
    high_col = lax.axis_index("col") >= 2
    here, there = cotangent[...], beyond[...]
    both = jnp.concatenate(
        [jnp.where(high_col, there, here), jnp.where(high_col, here, there)], axis=0
    )
    pre, back, term = layer(total, weight[...], both)
    pre_out[...] = jnp.where(high_col, pre[nodes:], pre[:nodes])
    back_out[...] = back.astype(back_out.dtype)
    halve(term, mine, other)


def add_kernel(mine, came, out):
    out[...] = (mine[...] + wide(came[...])).astype(out.dtype)


def act_kernel(pre, act):
    act[...] = (pre[...] * jax.nn.sigmoid(pre[...])).astype(act.dtype)


def begin_kernel(matrix, back, product):
    product[...] = dot(matrix[:, : back.shape[0]], back[...])


def backward_kernel(n, matrix, begun, *refs):
    backs, halves, (own, kept, *sends, product) = refs[: n - 1], refs[n - 1 : 2 * n - 1], refs[2 * n - 1 :]
    rows = own.shape[0]
    late = sum(back.shape[0] for back in backs)
    stacked = jnp.concatenate([back[...] for back in backs], axis=0)
    product[...] = begun[...] + dot(matrix[:, -late:], stacked)
    own[...] = product[:rows]
    term = tree([wide(half[...]) for half in halves]).astype(kept.dtype)
    kept[...] = term
    here, size = lax.axis_index("row"), lax.axis_size("row")
    for d, send in enumerate(sends, 1):
        start = pl.multiple_of((lax.rem(here + d, size) ^ here) * rows, rows)
        send[:rows] = product[pl.ds(start, rows)].astype(send.dtype)
        send[rows:] = term


def last_kernel(scale, own, kept, *refs):
    *messages, features_out, weight_out = refs
    messages = messages[:1] + messages[-1:] + messages[1:-1]
    nodes, half = own.shape[0], kept.shape[1]
    features_out[...] = tree(
        [own[...]] + [wide(message[:nodes]) for message in messages]
    ).astype(features_out.dtype)
    terms = [wide(kept[...])] + [wide(message[nodes:]) for message in messages]
    mine, other = tree(terms[::2]) * scale, tree(terms[1::2]) * scale
    odd = odd_row()
    weight_out[:, :half] = jnp.where(odd, other, mine)
    weight_out[:, half:] = jnp.where(odd, mine, other)


def per_device(features, weight, cotangent, tile_values, tile_rows, tile_cols, tile_count):
    slots, side = tile_values.shape[2:4]
    n_row, n_col = lax.axis_size("row"), lax.axis_size("col")
    nodes, width = features.shape
    hidden = weight.shape[1]
    down, across = n_col * nodes, n_row * nodes
    dense_bytes = 2 * down * across

    paired = n_col == 4
    gathered = [swap(features, "row", d) for d in start_order(n_row)]
    (blank,) = call(zero_kernel, [((down, across), NARROW)], [], need=dense_bytes)()
    (near,) = call(
        functools.partial(dense_kernel, nodes // side, paired),
        [((down, across), NARROW)],
        [VMEM] * 5,
        aliases={0: 0},
        scratch=[
            pltpu.SMEM(tile_rows.shape, jnp.int32),
            pltpu.SMEM(tile_cols.shape, jnp.int32),
            pltpu.SMEM(tile_count.shape, jnp.int32),
            pltpu.SemaphoreType.DMA((3,)),
        ],
        need=2 * dense_bytes,
    )(blank, tile_values, tile_rows, tile_cols, tile_count)

    forward = dict(flops=2 * down * across * width, need=2 * dense_bytes)
    if paired:
        layers = 2
        own, *sends = call(
            functools.partial(paired_forward_kernel, n_row),
            [((2 * nodes, width), NARROW)] * 4,
            [VMEM] * (1 + n_row),
            **forward,
        )(near, features, *gathered)
        layer_call, cotangents = paired_layer_kernel, [cotangent, swap(cotangent, "col", 2)]
        first, second, third = exchange(sends, "col", True)
        parts = [first, third, second]
    else:
        layers = 1
        own, *sends = call(
            functools.partial(forward_kernel, n_row),
            [((nodes, width), jnp.float32)] + [((nodes, width), NARROW)] * (n_col - 1),
            [VMEM] * (1 + n_row),
            **forward,
        )(near, features, *gathered)
        layer_call, cotangents = layer_kernel, [cotangent]
        parts = exchange(sends, "col", True)
    (far,) = call(
        functools.partial(turn_kernel, side),
        [((across, down), NARROW)],
        [VMEM],
        need=3 * dense_bytes,
    )(near)

    half = hidden // 2
    square = (width, half)
    back, mine, other, pre = call(
        layer_call,
        [
            ((layers * nodes, width), NARROW),
            (square, jnp.float32),
            (square, NARROW),
            ((nodes, hidden), jnp.float32),
        ],
        [VMEM] * (n_col + 1 + len(cotangents)),
        flops=14 * layers * nodes * width * hidden,
        after=[far],
    )(own, *parts, weight, *cotangents)
    (term,) = call(add_kernel, [(square, NARROW)], [VMEM] * 2)(mine, swap(other, "row", 1))
    if paired:
        backs, terms = [back, swap(back, "col", 1)], [term, swap(term, "col", 1)]
    else:
        backs = [back] + exchange([back] * (n_col - 1), "col", False)
        terms = [term] + exchange([term] * (n_col - 1), "col", False)
    (act,) = call(act_kernel, [((nodes, hidden), NARROW)], [VMEM])(pre)

    message = ((nodes + width, width), NARROW)
    (begun,) = call(begin_kernel, [((across, width), jnp.float32)], [VMEM] * 2, **forward)(far, back)
    own, kept, *sends = call(
        functools.partial(backward_kernel, len(backs)),
        [((nodes, width), jnp.float32), (square, NARROW)] + [message] * (n_row - 1),
        [VMEM] * (1 + 2 * len(backs)),
        scratch=[pltpu.VMEM((across, width), jnp.float32)],
        **forward,
    )(far, begun, *backs[1:], *terms)
    parts = exchange(sends, "row", True)

    scale = float(nodes * n_row * n_col) ** -0.5
    grad_features, grad_weight = call(
        functools.partial(last_kernel, scale),
        [((nodes, width), NARROW), ((width, hidden), jnp.float32)],
        [VMEM] * (n_row + 1),
    )(own, kept, parts[0], *parts[2:], parts[1])
    return act, grad_features, grad_weight


def solution(mesh):
    placed = (
        P(("groups", "row", "col"), None),
        P(),
        P(("groups", "row", "col"), None),
        P(("groups", "row"), "col", None, None, None),
        P(("groups", "row"), "col", None),
        P(("groups", "row"), "col", None),
        P(("groups", "row"), "col"),
    )
    return jax.shard_map(
        per_device,
        mesh=mesh,
        in_specs=placed,
        out_specs=(
            P(("groups", "row", "col"), None),
            P(("groups", "row", "col"), None),
            P("groups", None),
        ),
        check_vma=False,
    )
```

```python
import functools

import jax
import jax.numpy as jnp
from jax import lax
from jax.experimental import pallas as pl
from jax.experimental.pallas import tpu as pltpu
from jax.sharding import PartitionSpec as P

VMEM = pl.BlockSpec(memory_space=pltpu.VMEM)
ANY = pl.BlockSpec(memory_space=pl.ANY)
LEAST = 16 * 1024 * 1024
NARROW = jnp.bfloat16


def call(kernel, outs, in_specs, scratch=(), flops=0, need=0, after=(), aliases=None):
    outs = tuple(jax.ShapeDtypeStruct(shape, dtype) for shape, dtype in outs)
    late = len(after)
    run = pl.pallas_call(
        (lambda *refs: kernel(*refs[late:])) if late else kernel,
        out_shape=outs,
        in_specs=[ANY] * late + list(in_specs),
        out_specs=(VMEM,) * len(outs),
        input_output_aliases=aliases or {},
        scratch_shapes=scratch,
        compiler_params=pltpu.CompilerParams(vmem_limit_bytes=LEAST + need),
        cost_estimate=pl.CostEstimate(flops=flops, bytes_accessed=need, transcendentals=0),
    )
    return functools.partial(run, *after)


def ring_place(k, axis):
    return k ^ (k >> 1) if axis == "col" and lax.axis_size(axis) == 4 else k


def exchange(sends, axis, ahead):
    n = lax.axis_size(axis)

    def target(s, d):
        return ring_place((ring_place(s, axis) + (d if ahead else -d)) % n, axis)

    return [
        lax.ppermute(send, axis, [(s, target(s, d)) for s in range(n)])
        for d, send in enumerate(sends, 1)
    ]


def odd_row():
    return lax.rem(lax.axis_index("row"), 2) == 1


def start_order(n):
    return [*range(2, n), 1]


def swap(value, axis, distance):
    n = lax.axis_size(axis)
    return lax.ppermute(value, axis, [(s, s ^ distance) for s in range(n)])


def wide(value):
    return value.astype(jnp.float32)


def split(value):
    high = value.astype(NARROW)
    return high, (value - wide(high)).astype(NARROW)


def dot(left, right, dims=((1,), (0,))):
    return lax.dot_general(left, right, (dims, ((), ())), preferred_element_type=jnp.float32)


def zero_kernel(out):
    out[...] = jnp.zeros_like(out)


def dense_kernel(piece, paired, blank, vals, rows_in, cols_in, count_in, near, rows, cols, count, sems):
    copies = [
        pltpu.make_async_copy(source, target, sems.at[k])
        for k, (source, target) in enumerate(((rows_in, rows), (cols_in, cols), (count_in, count)))
    ]
    for copy in copies:
        copy.start()
    side = vals.shape[-1]
    for copy in copies:
        copy.wait()

    def ahead(there):
        n, here = lax.axis_size("col"), lax.axis_index("col")
        return lax.rem(ring_place(there, "col") - ring_place(here, "col") + n, n)

    def add(t, _):
        row, col = rows[0, 0, t], cols[0, 0, t]
        if paired:
            place = lax.rem((row // piece) ^ lax.axis_index("col"), 2) * 2 + row // piece // 2
        else:
            place = ahead(row // piece)
        row = place * piece + lax.rem(row, piece)
        col = ((col // piece) ^ lax.axis_index("row")) * piece + lax.rem(col, piece)
        down = pl.ds(pl.multiple_of(row * side, side), side)
        across = pl.ds(pl.multiple_of(col * side, side), side)
        near[down, across] = vals[0, 0, t]
        return 0

    lax.fori_loop(0, count[0, 0], add, 0)


def turn_kernel(step, near, far):
    def turn(k, _):
        band = pl.ds(pl.multiple_of(k * step, step), step)
        far[:, band] = near[band, :].T
        return 0

    lax.fori_loop(0, near.shape[0] // step, turn, 0)


def tree(terms):
    while len(terms) > 1:
        middle = len(terms) // 2
        terms = [left + right for left, right in zip(terms[:middle], terms[middle:])]
    return terms[0]


def stack(operands):
    own, *others = [operand[...] for operand in operands]
    order = start_order(len(operands))
    return jnp.concatenate([own] + [others[order.index(d)] for d in range(1, len(operands))], axis=0)


def forward_kernel(n, matrix, *refs):
    operands, own, sends = refs[:n], refs[n], refs[n + 1 :]
    rows = own.shape[0]
    product = dot(matrix[...], stack(operands))
    own[...] = product[:rows]
    for d, send in enumerate(sends, 1):
        send[...] = product[d * rows : (d + 1) * rows].astype(send.dtype)


def layer(total, weight, cotangent):
    high, low = split(total)
    pre = dot(high, weight) + dot(low, weight)
    sigma = 0.5 + 0.5 * jnp.tanh(0.5 * pre)
    grad = wide(cotangent) * sigma * (1.0 + pre * (1.0 - sigma))
    grad_high, grad_low = split(grad)
    across, down = ((1,), (1,)), ((0,), (0,))
    back = dot(grad_high, weight, across) + dot(grad_low, weight, across)
    term = dot(high, grad_high, down) + dot(low, grad_high, down) + dot(high, grad_low, down)
    return pre, back, term


def halve(term, mine, other):
    half = mine.shape[1]
    odd = odd_row()
    left, right = term[:, :half], term[:, half:]
    mine[...] = jnp.where(odd, right, left)
    other[...] = jnp.where(odd, left, right).astype(other.dtype)


def layer_kernel(*refs):
    *parts, weight, cotangent, back_out, mine, other, pre_out = refs
    total = tree([wide(part[...]) for part in parts])
    pre, back, term = layer(total, weight[...], cotangent[...])
    pre_out[...] = pre
    back_out[...] = back.astype(back_out.dtype)
    halve(term, mine, other)


def in_middle():
    my_col = lax.axis_index("col")
    return (my_col == 1) | (my_col == 2)


def paired_forward_kernel(n, matrix, *refs):
    operands, (own, first, second, third) = refs[:n], refs[n:]
    product = dot(matrix[...], stack(operands)).astype(own.dtype)
    rows = own.shape[0]
    same, other = product[:rows], product[rows:]
    middle = in_middle()
    own[...] = same
    first[...] = jnp.where(middle, same, other)
    second[...] = other
    third[...] = jnp.where(middle, other, same)


def paired_layer_kernel(own, first, second, third, weight, cotangent, beyond, *refs):
    back_out, mine, other, pre_out = refs
    nodes = cotangent.shape[0]
    middle = in_middle()
    partner = jnp.where(middle, third[...], first[...])
    side = jnp.where(middle, first[...], third[...])
    total = (wide(own[...]) + wide(partner)) + (wide(second[...]) + wide(side))
    high_col = lax.axis_index("col") >= 2
    here, there = cotangent[...], beyond[...]
    both = jnp.concatenate(
        [jnp.where(high_col, there, here), jnp.where(high_col, here, there)], axis=0
    )
    pre, back, term = layer(total, weight[...], both)
    pre_out[...] = jnp.where(high_col, pre[nodes:], pre[:nodes])
    back_out[...] = back.astype(back_out.dtype)
    halve(term, mine, other)


def add_kernel(mine, came, out):
    out[...] = (mine[...] + wide(came[...])).astype(out.dtype)


def act_kernel(pre, act):
    act[...] = (pre[...] * jax.nn.sigmoid(pre[...])).astype(act.dtype)


def begin_kernel(matrix, back, product):
    product[...] = dot(matrix[:, : back.shape[0]], back[...])


def backward_kernel(n, matrix, begun, *refs):
    backs, halves, (own, kept, *sends, product) = refs[: n - 1], refs[n - 1 : 2 * n - 1], refs[2 * n - 1 :]
    rows = own.shape[0]
    late = sum(back.shape[0] for back in backs)
    stacked = jnp.concatenate([back[...] for back in backs], axis=0)
    product[...] = begun[...] + dot(matrix[:, -late:], stacked)
    own[...] = product[:rows]
    term = tree([wide(half[...]) for half in halves]).astype(kept.dtype)
    kept[...] = term
    here, size = lax.axis_index("row"), lax.axis_size("row")
    for d, send in enumerate(sends, 1):
        start = pl.multiple_of((lax.rem(here + d, size) ^ here) * rows, rows)
        send[:rows] = product[pl.ds(start, rows)].astype(send.dtype)
        send[rows:] = term


def last_kernel(scale, own, kept, *refs):
    *messages, features_out, weight_out = refs
    nodes, half = own.shape[0], kept.shape[1]
    features_out[...] = tree(
        [own[...]] + [wide(message[:nodes]) for message in messages]
    ).astype(features_out.dtype)
    terms = [wide(kept[...])] + [wide(message[nodes:]) for message in messages]
    mine, other = tree(terms[::2]) * scale, tree(terms[1::2]) * scale
    odd = odd_row()
    weight_out[:, :half] = jnp.where(odd, other, mine)
    weight_out[:, half:] = jnp.where(odd, mine, other)


def per_device(features, weight, cotangent, tile_values, tile_rows, tile_cols, tile_count):
    slots, side = tile_values.shape[2:4]
    n_row, n_col = lax.axis_size("row"), lax.axis_size("col")
    nodes, width = features.shape
    hidden = weight.shape[1]
    down, across = n_col * nodes, n_row * nodes
    dense_bytes = 2 * down * across

    paired = n_col == 4
    gathered = [swap(features, "row", d) for d in start_order(n_row)]
    (blank,) = call(zero_kernel, [((down, across), NARROW)], [], need=dense_bytes)()
    (near,) = call(
        functools.partial(dense_kernel, nodes // side, paired),
        [((down, across), NARROW)],
        [VMEM] * 5,
        aliases={0: 0},
        scratch=[
            pltpu.SMEM(tile_rows.shape, jnp.int32),
            pltpu.SMEM(tile_cols.shape, jnp.int32),
            pltpu.SMEM(tile_count.shape, jnp.int32),
            pltpu.SemaphoreType.DMA((3,)),
        ],
        need=2 * dense_bytes,
    )(blank, tile_values, tile_rows, tile_cols, tile_count)

    forward = dict(flops=2 * down * across * width, need=2 * dense_bytes)
    if paired:
        layers = 2
        own, *sends = call(
            functools.partial(paired_forward_kernel, n_row),
            [((2 * nodes, width), NARROW)] * 4,
            [VMEM] * (1 + n_row),
            **forward,
        )(near, features, *gathered)
        layer_call, cotangents = paired_layer_kernel, [cotangent, swap(cotangent, "col", 2)]
    else:
        layers = 1
        own, *sends = call(
            functools.partial(forward_kernel, n_row),
            [((nodes, width), jnp.float32)] + [((nodes, width), NARROW)] * (n_col - 1),
            [VMEM] * (1 + n_row),
            **forward,
        )(near, features, *gathered)
        layer_call, cotangents = layer_kernel, [cotangent]
    parts = exchange(sends, "col", True)
    (far,) = call(
        functools.partial(turn_kernel, side),
        [((across, down), NARROW)],
        [VMEM],
        need=3 * dense_bytes,
    )(near)

    half = hidden // 2
    square = (width, half)
    back, mine, other, pre = call(
        layer_call,
        [
            ((layers * nodes, width), NARROW),
            (square, jnp.float32),
            (square, NARROW),
            ((nodes, hidden), jnp.float32),
        ],
        [VMEM] * (n_col + 1 + len(cotangents)),
        flops=14 * layers * nodes * width * hidden,
        after=[far],
    )(own, *parts, weight, *cotangents)
    (term,) = call(add_kernel, [(square, NARROW)], [VMEM] * 2)(mine, swap(other, "row", 1))
    if paired:
        backs, terms = [back, swap(back, "col", 1)], [term, swap(term, "col", 1)]
    else:
        backs = [back] + exchange([back] * (n_col - 1), "col", False)
        terms = [term] + exchange([term] * (n_col - 1), "col", False)
    (act,) = call(act_kernel, [((nodes, hidden), NARROW)], [VMEM])(pre)

    message = ((nodes + width, width), NARROW)
    (begun,) = call(begin_kernel, [((across, width), jnp.float32)], [VMEM] * 2, **forward)(far, back)
    own, kept, *sends = call(
        functools.partial(backward_kernel, len(backs)),
        [((nodes, width), jnp.float32), (square, NARROW)] + [message] * (n_row - 1),
        [VMEM] * (1 + 2 * len(backs)),
        scratch=[pltpu.VMEM((across, width), jnp.float32)],
        **forward,
    )(far, begun, *backs[1:], *terms)
    parts = exchange(sends, "row", True)

    scale = float(nodes * n_row * n_col) ** -0.5
    grad_features, grad_weight = call(
        functools.partial(last_kernel, scale),
        [((nodes, width), NARROW), ((width, hidden), jnp.float32)],
        [VMEM] * (n_row + 1),
    )(own, kept, *parts)
    return act, grad_features, grad_weight


def solution(mesh):
    placed = (
        P(("groups", "row", "col"), None),
        P(),
        P(("groups", "row", "col"), None),
        P(("groups", "row"), "col", None, None, None),
        P(("groups", "row"), "col", None),
        P(("groups", "row"), "col", None),
        P(("groups", "row"), "col"),
    )
    return jax.shard_map(
        per_device,
        mesh=mesh,
        in_specs=placed,
        out_specs=(
            P(("groups", "row", "col"), None),
            P(("groups", "row", "col"), None),
            P("groups", None),
        ),
        check_vma=False,
    )
```

```python
import functools

import jax
import jax.numpy as jnp
from jax import lax
from jax.experimental import pallas as pl
from jax.experimental.pallas import tpu as pltpu
from jax.sharding import PartitionSpec as P

VMEM = pl.BlockSpec(memory_space=pltpu.VMEM)
ANY = pl.BlockSpec(memory_space=pl.ANY)
LEAST = 16 * 1024 * 1024
NARROW = jnp.bfloat16


def call(kernel, outs, in_specs, scratch=(), flops=0, need=0, after=(), aliases=None):
    outs = tuple(jax.ShapeDtypeStruct(shape, dtype) for shape, dtype in outs)
    late = len(after)
    run = pl.pallas_call(
        (lambda *refs: kernel(*refs[late:])) if late else kernel,
        out_shape=outs,
        in_specs=[ANY] * late + list(in_specs),
        out_specs=(VMEM,) * len(outs),
        input_output_aliases=aliases or {},
        scratch_shapes=scratch,
        compiler_params=pltpu.CompilerParams(vmem_limit_bytes=LEAST + need),
        cost_estimate=pl.CostEstimate(flops=flops, bytes_accessed=need, transcendentals=0),
    )
    return functools.partial(run, *after)


def ring_place(k, axis):
    return k ^ (k >> 1) if axis == "col" and lax.axis_size(axis) == 4 else k


def exchange(sends, axis, ahead):
    n = lax.axis_size(axis)

    def target(s, d):
        return ring_place((ring_place(s, axis) + (d if ahead else -d)) % n, axis)

    return [
        lax.ppermute(send, axis, [(s, target(s, d)) for s in range(n)])
        for d, send in enumerate(sends, 1)
    ]


def odd_row():
    return lax.rem(lax.axis_index("row"), 2) == 1


def start_order(n):
    return [*range(2, n), 1]


def swap(value, axis, distance):
    n = lax.axis_size(axis)
    return lax.ppermute(value, axis, [(s, s ^ distance) for s in range(n)])


def wide(value):
    return value.astype(jnp.float32)


def split(value):
    high = value.astype(NARROW)
    return high, (value - wide(high)).astype(NARROW)


def dot(left, right, dims=((1,), (0,))):
    return lax.dot_general(left, right, (dims, ((), ())), preferred_element_type=jnp.float32)


def zero_kernel(out):
    out[...] = jnp.zeros_like(out)


def dense_kernel(piece, paired, blank, vals, rows_in, cols_in, count_in, near, rows, cols, count, sems):
    copies = [
        pltpu.make_async_copy(source, target, sems.at[k])
        for k, (source, target) in enumerate(((rows_in, rows), (cols_in, cols), (count_in, count)))
    ]
    for copy in copies:
        copy.start()
    side = vals.shape[-1]
    for copy in copies:
        copy.wait()

    def ahead(there):
        n, here = lax.axis_size("col"), lax.axis_index("col")
        return lax.rem(ring_place(there, "col") - ring_place(here, "col") + n, n)

    def add(t, _):
        row, col = rows[0, 0, t], cols[0, 0, t]
        if paired:
            place = lax.rem((row // piece) ^ lax.axis_index("col"), 2) * 2 + row // piece // 2
        else:
            place = ahead(row // piece)
        row = place * piece + lax.rem(row, piece)
        col = ((col // piece) ^ lax.axis_index("row")) * piece + lax.rem(col, piece)
        down = pl.ds(pl.multiple_of(row * side, side), side)
        across = pl.ds(pl.multiple_of(col * side, side), side)
        near[down, across] = vals[0, 0, t]
        return 0

    lax.fori_loop(0, count[0, 0], add, 0)


def turn_kernel(step, near, far):
    def turn(k, _):
        band = pl.ds(pl.multiple_of(k * step, step), step)
        far[:, band] = near[band, :].T
        return 0

    lax.fori_loop(0, near.shape[0] // step, turn, 0)


def tree(terms):
    while len(terms) > 1:
        middle = len(terms) // 2
        terms = [left + right for left, right in zip(terms[:middle], terms[middle:])]
    return terms[0]


def stack(operands):
    own, *others = [operand[...] for operand in operands]
    order = start_order(len(operands))
    return jnp.concatenate([own] + [others[order.index(d)] for d in range(1, len(operands))], axis=0)


def forward_kernel(n, matrix, *refs):
    operands, own, sends = refs[:n], refs[n], refs[n + 1 :]
    rows = own.shape[0]
    product = dot(matrix[...], stack(operands))
    own[...] = product[:rows]
    for d, send in enumerate(sends, 1):
        send[...] = product[d * rows : (d + 1) * rows].astype(send.dtype)


def layer(total, weight, cotangent):
    high, low = split(total)
    pre = dot(high, weight) + dot(low, weight)
    sigma = jax.nn.sigmoid(pre)
    grad = wide(cotangent) * sigma * (1.0 + pre * (1.0 - sigma))
    grad_high, grad_low = split(grad)
    across, down = ((1,), (1,)), ((0,), (0,))
    back = dot(grad_high, weight, across) + dot(grad_low, weight, across)
    term = dot(high, grad_high, down) + dot(low, grad_high, down) + dot(high, grad_low, down)
    return pre, back, term


def store_layer(back, term, message, other):
    nodes, half = back.shape[0], other.shape[1]
    odd = odd_row()
    left, right = term[:, :half], term[:, half:]
    message[:nodes] = back.astype(message.dtype)
    message[nodes:] = jnp.where(odd, right, left).astype(message.dtype)
    other[...] = jnp.where(odd, left, right).astype(other.dtype)


def layer_kernel(*refs):
    *parts, weight, cotangent, message, other, pre_out = refs
    total = tree([wide(part[...]) for part in parts])
    pre, back, term = layer(total, weight[...], cotangent[...])
    pre_out[...] = pre
    store_layer(back, term, message, other)


def in_middle():
    my_col = lax.axis_index("col")
    return (my_col == 1) | (my_col == 2)


def paired_forward_kernel(n, matrix, *refs):
    operands, (own, first, second, third) = refs[:n], refs[n:]
    product = dot(matrix[...], stack(operands)).astype(own.dtype)
    rows = own.shape[0]
    same, other = product[:rows], product[rows:]
    middle = in_middle()
    own[...] = same
    first[...] = jnp.where(middle, same, other)
    second[...] = other
    third[...] = jnp.where(middle, other, same)


def paired_layer_kernel(own, first, second, third, weight, cotangent, beyond, *refs):
    message, other, pre_out = refs
    nodes = cotangent.shape[0]
    middle = in_middle()
    partner = jnp.where(middle, third[...], first[...])
    side = jnp.where(middle, first[...], third[...])
    total = (wide(own[...]) + wide(partner)) + (wide(second[...]) + wide(side))
    high_col = lax.axis_index("col") >= 2
    here, there = cotangent[...], beyond[...]
    both = jnp.concatenate(
        [jnp.where(high_col, there, here), jnp.where(high_col, here, there)], axis=0
    )
    pre, back, term = layer(total, weight[...], both)
    pre_out[...] = jnp.where(high_col, pre[nodes:], pre[:nodes])
    store_layer(back, term, message, other)


def message_kernel(sent, came, message):
    nodes = sent.shape[0] - came.shape[0]
    message[:nodes] = sent[:nodes]
    message[nodes:] = (wide(sent[nodes:]) + wide(came[...])).astype(message.dtype)


def act_kernel(pre, act):
    act[...] = (pre[...] * jax.nn.sigmoid(pre[...])).astype(act.dtype)


def begin_kernel(backs, matrix, message, product):
    product[...] = dot(matrix[:, :backs], message[:backs])


def backward_kernel(n, n_others, matrix, begun, *refs):
    messages, others, refs = refs[:n], refs[n : n + n_others], refs[n + n_others :]
    own, kept, *sends, product = refs
    rows = own.shape[0]
    backs = messages[0].shape[0] - kept.shape[0]
    stacked = jnp.concatenate([message[:backs] for message in messages[1:]], axis=0)
    product[...] = begun[...] + dot(matrix[:, backs:], stacked)
    own[...] = product[:rows]
    term = tree([wide(message[backs:]) for message in messages])
    if others:
        term = term + tree([wide(other[...]) for other in others])
    term = term.astype(kept.dtype)
    kept[...] = term
    here, size = lax.axis_index("row"), lax.axis_size("row")
    for d, send in enumerate(sends, 1):
        start = pl.multiple_of((lax.rem(here + d, size) ^ here) * rows, rows)
        send[:rows] = product[pl.ds(start, rows)].astype(send.dtype)
        send[rows:] = term


def last_kernel(scale, own, kept, *refs):
    *messages, features_out, weight_out = refs
    nodes, half = own.shape[0], kept.shape[1]
    features_out[...] = tree(
        [own[...]] + [wide(message[:nodes]) for message in messages]
    ).astype(features_out.dtype)
    terms = [wide(kept[...])] + [wide(message[nodes:]) for message in messages]
    mine, other = tree(terms[::2]) * scale, tree(terms[1::2]) * scale
    odd = odd_row()
    weight_out[:, :half] = jnp.where(odd, other, mine)
    weight_out[:, half:] = jnp.where(odd, mine, other)


def per_device(features, weight, cotangent, tile_values, tile_rows, tile_cols, tile_count):
    slots, side = tile_values.shape[2:4]
    n_row, n_col = lax.axis_size("row"), lax.axis_size("col")
    nodes, width = features.shape
    hidden = weight.shape[1]
    down, across = n_col * nodes, n_row * nodes
    dense_bytes = 2 * down * across

    paired = n_col == 4
    gathered = [swap(features, "row", d) for d in start_order(n_row)]
    (blank,) = call(zero_kernel, [((down, across), NARROW)], [], need=dense_bytes)()
    (near,) = call(
        functools.partial(dense_kernel, nodes // side, paired),
        [((down, across), NARROW)],
        [VMEM] * 5,
        aliases={0: 0},
        scratch=[
            pltpu.SMEM(tile_rows.shape, jnp.int32),
            pltpu.SMEM(tile_cols.shape, jnp.int32),
            pltpu.SMEM(tile_count.shape, jnp.int32),
            pltpu.SemaphoreType.DMA((3,)),
        ],
        need=2 * dense_bytes,
    )(blank, tile_values, tile_rows, tile_cols, tile_count)

    forward = dict(flops=2 * down * across * width, need=2 * dense_bytes)
    if paired:
        layers = 2
        own, *sends = call(
            functools.partial(paired_forward_kernel, n_row),
            [((2 * nodes, width), NARROW)] * 4,
            [VMEM] * (1 + n_row),
            **forward,
        )(near, features, *gathered)
        layer_call, cotangents = paired_layer_kernel, [cotangent, swap(cotangent, "col", 2)]
    else:
        layers = 1
        own, *sends = call(
            functools.partial(forward_kernel, n_row),
            [((nodes, width), jnp.float32)] + [((nodes, width), NARROW)] * (n_col - 1),
            [VMEM] * (1 + n_row),
            **forward,
        )(near, features, *gathered)
        layer_call, cotangents = layer_kernel, [cotangent]
    parts = exchange(sends, "col", True)
    (far,) = call(
        functools.partial(turn_kernel, side),
        [((across, down), NARROW)],
        [VMEM],
        need=3 * dense_bytes,
    )(near)

    half = hidden // 2
    square = (width, half)
    message = ((layers * nodes + width, width), NARROW)
    sent, other, pre = call(
        layer_call,
        [message, (square, NARROW), ((nodes, hidden), jnp.float32)],
        [VMEM] * (n_col + 1 + len(cotangents)),
        flops=14 * layers * nodes * width * hidden,
        after=[far],
    )(own, *parts, weight, *cotangents)
    if paired:
        corner = [
            (r * n_col + c, (r ^ 1) * n_col + (c ^ 1)) for r in range(n_row) for c in range(n_col)
        ]
        messages = [sent, swap(sent, "col", 1)]
        others = [swap(other, "row", 1), lax.ppermute(other, ("row", "col"), corner)]
    else:
        (sent,) = call(message_kernel, [message], [VMEM] * 2)(sent, swap(other, "row", 1))
        messages = [sent] + exchange([sent] * (n_col - 1), "col", False)
        others = []
    (act,) = call(act_kernel, [((nodes, hidden), NARROW)], [VMEM])(pre)

    message = ((nodes + width, width), NARROW)
    (begun,) = call(
        functools.partial(begin_kernel, layers * nodes),
        [((across, width), jnp.float32)],
        [VMEM] * 2,
        **forward,
    )(far, sent)
    message = ((nodes + width, width), NARROW)
    own, kept, *sends = call(
        functools.partial(backward_kernel, len(messages), len(others)),
        [((nodes, width), jnp.float32), (square, NARROW)] + [message] * (n_row - 1),
        [VMEM] * (2 + len(messages) + len(others)),
        scratch=[pltpu.VMEM((across, width), jnp.float32)],
        **forward,
    )(far, begun, *messages, *others)
    parts = exchange(sends, "row", True)

    scale = float(nodes * n_row * n_col) ** -0.5
    grad_features, grad_weight = call(
        functools.partial(last_kernel, scale),
        [((nodes, width), NARROW), ((width, hidden), jnp.float32)],
        [VMEM] * (n_row + 1),
    )(own, kept, *parts)
    return act, grad_features, grad_weight


def solution(mesh):
    placed = (
        P(("groups", "row", "col"), None),
        P(),
        P(("groups", "row", "col"), None),
        P(("groups", "row"), "col", None, None, None),
        P(("groups", "row"), "col", None),
        P(("groups", "row"), "col", None),
        P(("groups", "row"), "col"),
    )
    return jax.shard_map(
        per_device,
        mesh=mesh,
        in_specs=placed,
        out_specs=(
            P(("groups", "row", "col"), None),
            P(("groups", "row", "col"), None),
            P("groups", None),
        ),
        check_vma=False,
    )
```

```python
import functools

import jax
import jax.numpy as jnp
from jax import lax
from jax.experimental import pallas as pl
from jax.experimental.pallas import tpu as pltpu
from jax.sharding import PartitionSpec as P

VMEM = pl.BlockSpec(memory_space=pltpu.VMEM)
ANY = pl.BlockSpec(memory_space=pl.ANY)
LEAST = 16 * 1024 * 1024
NARROW = jnp.bfloat16


def call(kernel, outs, in_specs, scratch=(), flops=0, need=0, after=(), aliases=None):
    outs = tuple(jax.ShapeDtypeStruct(shape, dtype) for shape, dtype in outs)
    late = len(after)
    run = pl.pallas_call(
        (lambda *refs: kernel(*refs[late:])) if late else kernel,
        out_shape=outs,
        in_specs=[ANY] * late + list(in_specs),
        out_specs=(VMEM,) * len(outs),
        input_output_aliases=aliases or {},
        scratch_shapes=scratch,
        compiler_params=pltpu.CompilerParams(vmem_limit_bytes=LEAST + need),
        cost_estimate=pl.CostEstimate(flops=flops, bytes_accessed=need, transcendentals=0),
    )
    return functools.partial(run, *after)


def ring_place(k, axis):
    return k ^ (k >> 1) if axis == "col" and lax.axis_size(axis) == 4 else k


def exchange(sends, axis, ahead):
    n = lax.axis_size(axis)

    def target(s, d):
        return ring_place((ring_place(s, axis) + (d if ahead else -d)) % n, axis)

    return [
        lax.ppermute(send, axis, [(s, target(s, d)) for s in range(n)])
        for d, send in enumerate(sends, 1)
    ]


def odd_row():
    return lax.rem(lax.axis_index("row"), 2) == 1


def start_order(n):
    return [*range(2, n), 1]


def swap(value, axis, distance):
    n = lax.axis_size(axis)
    return lax.ppermute(value, axis, [(s, s ^ distance) for s in range(n)])


def wide(value):
    return value.astype(jnp.float32)


def split(value):
    high = value.astype(NARROW)
    return high, (value - wide(high)).astype(NARROW)


def dot(left, right, dims=((1,), (0,))):
    return lax.dot_general(left, right, (dims, ((), ())), preferred_element_type=jnp.float32)


def zero_kernel(out):
    out[...] = jnp.zeros_like(out)


def dense_kernel(piece, paired, blank, vals, rows_in, cols_in, count_in, near, rows, cols, count, sems):
    copies = [
        pltpu.make_async_copy(source, target, sems.at[k])
        for k, (source, target) in enumerate(((rows_in, rows), (cols_in, cols), (count_in, count)))
    ]
    for copy in copies:
        copy.start()
    side = vals.shape[-1]
    for copy in copies:
        copy.wait()

    def ahead(there):
        n, here = lax.axis_size("col"), lax.axis_index("col")
        return lax.rem(ring_place(there, "col") - ring_place(here, "col") + n, n)

    def add(t, _):
        row, col = rows[0, 0, t], cols[0, 0, t]
        if paired:
            place = lax.rem((row // piece) ^ lax.axis_index("col"), 2) * 2 + row // piece // 2
        else:
            place = ahead(row // piece)
        row = place * piece + lax.rem(row, piece)
        col = ((col // piece) ^ lax.axis_index("row")) * piece + lax.rem(col, piece)
        down = pl.ds(pl.multiple_of(row * side, side), side)
        across = pl.ds(pl.multiple_of(col * side, side), side)
        near[down, across] = vals[0, 0, t]
        return 0

    lax.fori_loop(0, count[0, 0], add, 0)


def turn_kernel(step, near, far):
    def turn(k, _):
        band = pl.ds(pl.multiple_of(k * step, step), step)
        far[:, band] = near[band, :].T
        return 0

    lax.fori_loop(0, near.shape[0] // step, turn, 0)


def tree(terms):
    while len(terms) > 1:
        middle = len(terms) // 2
        terms = [left + right for left, right in zip(terms[:middle], terms[middle:])]
    return terms[0]


def stack(operands):
    own, *others = [operand[...] for operand in operands]
    order = start_order(len(operands))
    return jnp.concatenate([own] + [others[order.index(d)] for d in range(1, len(operands))], axis=0)


def forward_kernel(n, matrix, *refs):
    operands, own, sends = refs[:n], refs[n], refs[n + 1 :]
    rows = own.shape[0]
    product = dot(matrix[...], stack(operands))
    own[...] = product[:rows]
    for d, send in enumerate(sends, 1):
        send[...] = product[d * rows : (d + 1) * rows].astype(send.dtype)


def layer(total, weight, cotangent):
    high, low = split(total)
    pre = dot(high, weight) + dot(low, weight)
    sigma = jax.nn.sigmoid(pre)
    grad = wide(cotangent) * sigma * (1.0 + pre * (1.0 - sigma))
    grad_high, grad_low = split(grad)
    across, down = ((1,), (1,)), ((0,), (0,))
    back = dot(grad_high, weight, across) + dot(grad_low, weight, across)
    term = dot(high, grad_high, down) + dot(low, grad_high, down) + dot(high, grad_low, down)
    return pre, back, term


def store_layer(back, term, message, other):
    nodes, half = back.shape[0], other.shape[1]
    odd = odd_row()
    left, right = term[:, :half], term[:, half:]
    message[:nodes] = back.astype(message.dtype)
    message[nodes:] = jnp.where(odd, right, left).astype(message.dtype)
    other[...] = jnp.where(odd, left, right).astype(other.dtype)


def layer_kernel(*refs):
    *parts, weight, cotangent, message, other, pre_out = refs
    total = tree([wide(part[...]) for part in parts])
    pre, back, term = layer(total, weight[...], cotangent[...])
    pre_out[...] = pre
    store_layer(back, term, message, other)


def in_middle():
    my_col = lax.axis_index("col")
    return (my_col == 1) | (my_col == 2)


def paired_forward_kernel(n, matrix, *refs):
    operands, (own, first, second, third) = refs[:n], refs[n:]
    product = dot(matrix[...], stack(operands)).astype(own.dtype)
    rows = own.shape[0]
    same, other = product[:rows], product[rows:]
    middle = in_middle()
    own[...] = same
    first[...] = jnp.where(middle, same, other)
    second[...] = other
    third[...] = jnp.where(middle, other, same)


def paired_layer_kernel(own, third, second, first, weight, cotangent, beyond, *refs):
    message, other, pre_out = refs
    nodes = cotangent.shape[0]
    middle = in_middle()
    partner = jnp.where(middle, third[...], first[...])
    side = jnp.where(middle, first[...], third[...])
    total = (wide(own[...]) + wide(partner)) + (wide(second[...]) + wide(side))
    high_col = lax.axis_index("col") >= 2
    here, there = cotangent[...], beyond[...]
    both = jnp.concatenate(
        [jnp.where(high_col, there, here), jnp.where(high_col, here, there)], axis=0
    )
    pre, back, term = layer(total, weight[...], both)
    pre_out[...] = jnp.where(high_col, pre[nodes:], pre[:nodes])
    store_layer(back, term, message, other)


def message_kernel(sent, came, message):
    nodes = sent.shape[0] - came.shape[0]
    message[:nodes] = sent[:nodes]
    message[nodes:] = (wide(sent[nodes:]) + wide(came[...])).astype(message.dtype)


def act_kernel(pre, act):
    act[...] = (pre[...] * jax.nn.sigmoid(pre[...])).astype(act.dtype)


def begin_kernel(backs, matrix, message, product):
    product[...] = dot(matrix[:, :backs], message[:backs])


def backward_kernel(n, n_others, matrix, begun, *refs):
    messages, others, refs = refs[:n], refs[n : n + n_others], refs[n + n_others :]
    own, kept, *sends, product = refs
    rows = own.shape[0]
    backs = messages[0].shape[0] - kept.shape[0]
    stacked = jnp.concatenate([message[:backs] for message in messages[1:]], axis=0)
    product[...] = begun[...] + dot(matrix[:, backs:], stacked)
    own[...] = product[:rows]
    term = tree([wide(message[backs:]) for message in messages])
    if others:
        term = term + tree([wide(other[...]) for other in others])
    term = term.astype(kept.dtype)
    kept[...] = term
    here, size = lax.axis_index("row"), lax.axis_size("row")
    for d, send in enumerate(sends, 1):
        start = pl.multiple_of((lax.rem(here + d, size) ^ here) * rows, rows)
        send[:rows] = product[pl.ds(start, rows)].astype(send.dtype)
        send[rows:] = term


def last_kernel(scale, own, kept, *refs):
    *messages, features_out, weight_out = refs
    nodes, half = own.shape[0], kept.shape[1]
    features_out[...] = tree(
        [own[...]] + [wide(message[:nodes]) for message in messages]
    ).astype(features_out.dtype)
    terms = [wide(kept[...])] + [wide(message[nodes:]) for message in messages]
    mine, other = tree(terms[::2]) * scale, tree(terms[1::2]) * scale
    odd = odd_row()
    weight_out[:, :half] = jnp.where(odd, other, mine)
    weight_out[:, half:] = jnp.where(odd, mine, other)


def per_device(features, weight, cotangent, tile_values, tile_rows, tile_cols, tile_count):
    slots, side = tile_values.shape[2:4]
    n_row, n_col = lax.axis_size("row"), lax.axis_size("col")
    nodes, width = features.shape
    hidden = weight.shape[1]
    down, across = n_col * nodes, n_row * nodes
    dense_bytes = 2 * down * across

    paired = n_col == 4
    gathered = [swap(features, "row", d) for d in start_order(n_row)]
    (blank,) = call(zero_kernel, [((down, across), NARROW)], [], need=dense_bytes)()
    (near,) = call(
        functools.partial(dense_kernel, nodes // side, paired),
        [((down, across), NARROW)],
        [VMEM] * 5,
        aliases={0: 0},
        scratch=[
            pltpu.SMEM(tile_rows.shape, jnp.int32),
            pltpu.SMEM(tile_cols.shape, jnp.int32),
            pltpu.SMEM(tile_count.shape, jnp.int32),
            pltpu.SemaphoreType.DMA((3,)),
        ],
        need=2 * dense_bytes,
    )(blank, tile_values, tile_rows, tile_cols, tile_count)

    forward = dict(flops=2 * down * across * width, need=2 * dense_bytes)
    if paired:
        layers = 2
        own, *sends = call(
            functools.partial(paired_forward_kernel, n_row),
            [((2 * nodes, width), NARROW)] * 4,
            [VMEM] * (1 + n_row),
            **forward,
        )(near, features, *gathered)
        layer_call, cotangents = paired_layer_kernel, [cotangent, swap(cotangent, "col", 2)]
        parts = exchange(sends, "col", True)[::-1]
    else:
        layers = 1
        own, *sends = call(
            functools.partial(forward_kernel, n_row),
            [((nodes, width), jnp.float32)] + [((nodes, width), NARROW)] * (n_col - 1),
            [VMEM] * (1 + n_row),
            **forward,
        )(near, features, *gathered)
        layer_call, cotangents = layer_kernel, [cotangent]
        parts = exchange(sends, "col", True)
    (far,) = call(
        functools.partial(turn_kernel, side),
        [((across, down), NARROW)],
        [VMEM],
        need=3 * dense_bytes,
    )(near)

    half = hidden // 2
    square = (width, half)
    message = ((layers * nodes + width, width), NARROW)
    sent, other, pre = call(
        layer_call,
        [message, (square, NARROW), ((nodes, hidden), jnp.float32)],
        [VMEM] * (n_col + 1 + len(cotangents)),
        flops=14 * layers * nodes * width * hidden,
        after=[far],
    )(own, *parts, weight, *cotangents)
    if paired:
        corner = [
            (r * n_col + c, (r ^ 1) * n_col + (c ^ 1)) for r in range(n_row) for c in range(n_col)
        ]
        messages = [sent, swap(sent, "col", 1)]
        others = [swap(other, "row", 1), lax.ppermute(other, ("row", "col"), corner)]
    else:
        (sent,) = call(message_kernel, [message], [VMEM] * 2)(sent, swap(other, "row", 1))
        messages = [sent] + exchange([sent] * (n_col - 1), "col", False)
        others = []
    (act,) = call(act_kernel, [((nodes, hidden), NARROW)], [VMEM])(pre)

    message = ((nodes + width, width), NARROW)
    (begun,) = call(
        functools.partial(begin_kernel, layers * nodes),
        [((across, width), jnp.float32)],
        [VMEM] * 2,
        **forward,
    )(far, sent)
    message = ((nodes + width, width), NARROW)
    own, kept, *sends = call(
        functools.partial(backward_kernel, len(messages), len(others)),
        [((nodes, width), jnp.float32), (square, NARROW)] + [message] * (n_row - 1),
        [VMEM] * (2 + len(messages) + len(others)),
        scratch=[pltpu.VMEM((across, width), jnp.float32)],
        **forward,
    )(far, begun, *messages, *others)
    parts = exchange(sends, "row", True)

    scale = float(nodes * n_row * n_col) ** -0.5
    grad_features, grad_weight = call(
        functools.partial(last_kernel, scale),
        [((nodes, width), NARROW), ((width, hidden), jnp.float32)],
        [VMEM] * (n_row + 1),
    )(own, kept, *parts)
    return act, grad_features, grad_weight


def solution(mesh):
    placed = (
        P(("groups", "row", "col"), None),
        P(),
        P(("groups", "row", "col"), None),
        P(("groups", "row"), "col", None, None, None),
        P(("groups", "row"), "col", None),
        P(("groups", "row"), "col", None),
        P(("groups", "row"), "col"),
    )
    return jax.shard_map(
        per_device,
        mesh=mesh,
        in_specs=placed,
        out_specs=(
            P(("groups", "row", "col"), None),
            P(("groups", "row", "col"), None),
            P("groups", None),
        ),
        check_vma=False,
    )
```

```python
import functools

import jax
import jax.numpy as jnp
from jax import lax
from jax.experimental import pallas as pl
from jax.experimental.pallas import tpu as pltpu
from jax.sharding import PartitionSpec as P

VMEM = pl.BlockSpec(memory_space=pltpu.VMEM)
ANY = pl.BlockSpec(memory_space=pl.ANY)
LEAST = 16 * 1024 * 1024
NARROW = jnp.bfloat16


def call(kernel, outs, in_specs, scratch=(), flops=0, need=0, after=(), aliases=None):
    outs = tuple(jax.ShapeDtypeStruct(shape, dtype) for shape, dtype in outs)
    late = len(after)
    run = pl.pallas_call(
        (lambda *refs: kernel(*refs[late:])) if late else kernel,
        out_shape=outs,
        in_specs=[ANY] * late + list(in_specs),
        out_specs=(VMEM,) * len(outs),
        input_output_aliases=aliases or {},
        scratch_shapes=scratch,
        compiler_params=pltpu.CompilerParams(vmem_limit_bytes=LEAST + need),
        cost_estimate=pl.CostEstimate(flops=flops, bytes_accessed=need, transcendentals=0),
    )
    return functools.partial(run, *after)


def ring_place(k, axis):
    return k ^ (k >> 1) if axis == "col" and lax.axis_size(axis) == 4 else k


def exchange(sends, axis, ahead):
    n = lax.axis_size(axis)

    def target(s, d):
        return ring_place((ring_place(s, axis) + (d if ahead else -d)) % n, axis)

    return [
        lax.ppermute(send, axis, [(s, target(s, d)) for s in range(n)])
        for d, send in enumerate(sends, 1)
    ]


def odd_row():
    return lax.rem(lax.axis_index("row"), 2) == 1


def start_order(n):
    return [*range(n - 1, 0, -1)]


def swap(value, axis, distance):
    n = lax.axis_size(axis)
    return lax.ppermute(value, axis, [(s, s ^ distance) for s in range(n)])


def wide(value):
    return value.astype(jnp.float32)


def split(value):
    high = value.astype(NARROW)
    return high, (value - wide(high)).astype(NARROW)


def dot(left, right, dims=((1,), (0,))):
    return lax.dot_general(left, right, (dims, ((), ())), preferred_element_type=jnp.float32)


def zero_kernel(out):
    out[...] = jnp.zeros_like(out)


def dense_kernel(piece, paired, blank, vals, rows_in, cols_in, count_in, near, rows, cols, count, sems):
    copies = [
        pltpu.make_async_copy(source, target, sems.at[k])
        for k, (source, target) in enumerate(((rows_in, rows), (cols_in, cols), (count_in, count)))
    ]
    for copy in copies:
        copy.start()
    side = vals.shape[-1]
    for copy in copies:
        copy.wait()

    def ahead(there):
        n, here = lax.axis_size("col"), lax.axis_index("col")
        return lax.rem(ring_place(there, "col") - ring_place(here, "col") + n, n)

    def add(t, _):
        row, col = rows[0, 0, t], cols[0, 0, t]
        if paired:
            place = lax.rem((row // piece) ^ lax.axis_index("col"), 2) * 2 + row // piece // 2
        else:
            place = ahead(row // piece)
        row = place * piece + lax.rem(row, piece)
        col = ((col // piece) ^ lax.axis_index("row")) * piece + lax.rem(col, piece)
        down = pl.ds(pl.multiple_of(row * side, side), side)
        across = pl.ds(pl.multiple_of(col * side, side), side)
        near[down, across] = vals[0, 0, t]
        return 0

    lax.fori_loop(0, count[0, 0], add, 0)


def turn_kernel(step, near, far):
    def turn(k, _):
        band = pl.ds(pl.multiple_of(k * step, step), step)
        far[:, band] = near[band, :].T
        return 0

    lax.fori_loop(0, near.shape[0] // step, turn, 0)


def tree(terms):
    while len(terms) > 1:
        middle = len(terms) // 2
        terms = [left + right for left, right in zip(terms[:middle], terms[middle:])]
    return terms[0]


def stack(operands):
    own, *others = [operand[...] for operand in operands]
    order = start_order(len(operands))
    return jnp.concatenate([own] + [others[order.index(d)] for d in range(1, len(operands))], axis=0)


def forward_kernel(n, matrix, *refs):
    operands, own, sends = refs[:n], refs[n], refs[n + 1 :]
    rows = own.shape[0]
    product = dot(matrix[...], stack(operands))
    own[...] = product[:rows]
    for d, send in enumerate(sends, 1):
        send[...] = product[d * rows : (d + 1) * rows].astype(send.dtype)


def layer(total, weight, cotangent):
    high, low = split(total)
    pre = dot(high, weight) + dot(low, weight)
    sigma = jax.nn.sigmoid(pre)
    grad = wide(cotangent) * sigma * (1.0 + pre * (1.0 - sigma))
    grad_high, grad_low = split(grad)
    across, down = ((1,), (1,)), ((0,), (0,))
    back = dot(grad_high, weight, across) + dot(grad_low, weight, across)
    term = dot(high, grad_high, down) + dot(low, grad_high, down) + dot(high, grad_low, down)
    return pre, back, term


def store_layer(back, term, message, other):
    nodes, half = back.shape[0], other.shape[1]
    odd = odd_row()
    left, right = term[:, :half], term[:, half:]
    message[:nodes] = back.astype(message.dtype)
    message[nodes:] = jnp.where(odd, right, left).astype(message.dtype)
    other[...] = jnp.where(odd, left, right).astype(other.dtype)


def layer_kernel(*refs):
    *parts, weight, cotangent, message, other, pre_out = refs
    total = tree([wide(part[...]) for part in parts])
    pre, back, term = layer(total, weight[...], cotangent[...])
    pre_out[...] = pre
    store_layer(back, term, message, other)


def in_middle():
    my_col = lax.axis_index("col")
    return (my_col == 1) | (my_col == 2)


def paired_forward_kernel(n, matrix, *refs):
    operands, (own, first, second, third) = refs[:n], refs[n:]
    product = dot(matrix[...], stack(operands)).astype(own.dtype)
    rows = own.shape[0]
    same, other = product[:rows], product[rows:]
    middle = in_middle()
    own[...] = same
    first[...] = jnp.where(middle, same, other)
    second[...] = other
    third[...] = jnp.where(middle, other, same)


def paired_layer_kernel(own, first, second, third, weight, cotangent, beyond, *refs):
    message, other, pre_out = refs
    nodes = cotangent.shape[0]
    middle = in_middle()
    partner = jnp.where(middle, third[...], first[...])
    side = jnp.where(middle, first[...], third[...])
    total = (wide(own[...]) + wide(partner)) + (wide(second[...]) + wide(side))
    high_col = lax.axis_index("col") >= 2
    here, there = cotangent[...], beyond[...]
    both = jnp.concatenate(
        [jnp.where(high_col, there, here), jnp.where(high_col, here, there)], axis=0
    )
    pre, back, term = layer(total, weight[...], both)
    pre_out[...] = jnp.where(high_col, pre[nodes:], pre[:nodes])
    store_layer(back, term, message, other)


def message_kernel(sent, came, message):
    nodes = sent.shape[0] - came.shape[0]
    message[:nodes] = sent[:nodes]
    message[nodes:] = (wide(sent[nodes:]) + wide(came[...])).astype(message.dtype)


def act_kernel(pre, act):
    act[...] = (pre[...] * jax.nn.sigmoid(pre[...])).astype(act.dtype)


def begin_kernel(backs, matrix, message, product):
    product[...] = dot(matrix[:, :backs], message[:backs])


def backward_kernel(n, n_others, matrix, begun, *refs):
    messages, others, refs = refs[:n], refs[n : n + n_others], refs[n + n_others :]
    own, kept, *sends, product = refs
    rows = own.shape[0]
    backs = messages[0].shape[0] - kept.shape[0]
    stacked = jnp.concatenate([message[:backs] for message in messages[1:]], axis=0)
    product[...] = begun[...] + dot(matrix[:, backs:], stacked)
    own[...] = product[:rows]
    term = tree([wide(message[backs:]) for message in messages])
    if others:
        term = term + tree([wide(other[...]) for other in others])
    term = term.astype(kept.dtype)
    kept[...] = term
    here, size = lax.axis_index("row"), lax.axis_size("row")
    for d, send in enumerate(sends, 1):
        start = pl.multiple_of((lax.rem(here + d, size) ^ here) * rows, rows)
        send[:rows] = product[pl.ds(start, rows)].astype(send.dtype)
        send[rows:] = term


def last_kernel(scale, own, kept, *refs):
    *messages, features_out, weight_out = refs
    messages = messages[::-1]
    nodes, half = own.shape[0], kept.shape[1]
    features_out[...] = tree(
        [own[...]] + [wide(message[:nodes]) for message in messages]
    ).astype(features_out.dtype)
    terms = [wide(kept[...])] + [wide(message[nodes:]) for message in messages]
    mine, other = tree(terms[::2]) * scale, tree(terms[1::2]) * scale
    odd = odd_row()
    weight_out[:, :half] = jnp.where(odd, other, mine)
    weight_out[:, half:] = jnp.where(odd, mine, other)


def per_device(features, weight, cotangent, tile_values, tile_rows, tile_cols, tile_count):
    slots, side = tile_values.shape[2:4]
    n_row, n_col = lax.axis_size("row"), lax.axis_size("col")
    nodes, width = features.shape
    hidden = weight.shape[1]
    down, across = n_col * nodes, n_row * nodes
    dense_bytes = 2 * down * across

    paired = n_col == 4
    gathered = [swap(features, "row", d) for d in start_order(n_row)]
    (blank,) = call(zero_kernel, [((down, across), NARROW)], [], need=dense_bytes)()
    (near,) = call(
        functools.partial(dense_kernel, nodes // side, paired),
        [((down, across), NARROW)],
        [VMEM] * 5,
        aliases={0: 0},
        scratch=[
            pltpu.SMEM(tile_rows.shape, jnp.int32),
            pltpu.SMEM(tile_cols.shape, jnp.int32),
            pltpu.SMEM(tile_count.shape, jnp.int32),
            pltpu.SemaphoreType.DMA((3,)),
        ],
        need=2 * dense_bytes,
    )(blank, tile_values, tile_rows, tile_cols, tile_count)

    forward = dict(flops=2 * down * across * width, need=2 * dense_bytes)
    if paired:
        layers = 2
        own, *sends = call(
            functools.partial(paired_forward_kernel, n_row),
            [((2 * nodes, width), NARROW)] * 4,
            [VMEM] * (1 + n_row),
            **forward,
        )(near, features, *gathered)
        layer_call, cotangents = paired_layer_kernel, [cotangent, swap(cotangent, "col", 2)]
    else:
        layers = 1
        own, *sends = call(
            functools.partial(forward_kernel, n_row),
            [((nodes, width), jnp.float32)] + [((nodes, width), NARROW)] * (n_col - 1),
            [VMEM] * (1 + n_row),
            **forward,
        )(near, features, *gathered)
        layer_call, cotangents = layer_kernel, [cotangent]
    parts = exchange(sends, "col", True)
    (far,) = call(
        functools.partial(turn_kernel, side),
        [((across, down), NARROW)],
        [VMEM],
        need=3 * dense_bytes,
    )(near)

    half = hidden // 2
    square = (width, half)
    message = ((layers * nodes + width, width), NARROW)
    sent, other, pre = call(
        layer_call,
        [message, (square, NARROW), ((nodes, hidden), jnp.float32)],
        [VMEM] * (n_col + 1 + len(cotangents)),
        flops=14 * layers * nodes * width * hidden,
        after=[far],
    )(own, *parts, weight, *cotangents)
    if paired:
        corner = [
            (r * n_col + c, (r ^ 1) * n_col + (c ^ 1)) for r in range(n_row) for c in range(n_col)
        ]
        messages = [sent, swap(sent, "col", 1)]
        others = [lax.ppermute(other, ("row", "col"), corner), swap(other, "row", 1)]
    else:
        (sent,) = call(message_kernel, [message], [VMEM] * 2)(sent, swap(other, "row", 1))
        messages = [sent] + exchange([sent] * (n_col - 1), "col", False)
        others = []
    (act,) = call(act_kernel, [((nodes, hidden), NARROW)], [VMEM])(pre)

    message = ((nodes + width, width), NARROW)
    (begun,) = call(
        functools.partial(begin_kernel, layers * nodes),
        [((across, width), jnp.float32)],
        [VMEM] * 2,
        **forward,
    )(far, sent)
    message = ((nodes + width, width), NARROW)
    own, kept, *sends = call(
        functools.partial(backward_kernel, len(messages), len(others)),
        [((nodes, width), jnp.float32), (square, NARROW)] + [message] * (n_row - 1),
        [VMEM] * (2 + len(messages) + len(others)),
        scratch=[pltpu.VMEM((across, width), jnp.float32)],
        **forward,
    )(far, begun, *messages, *others)
    parts = exchange(sends, "row", True)

    scale = float(nodes * n_row * n_col) ** -0.5
    grad_features, grad_weight = call(
        functools.partial(last_kernel, scale),
        [((nodes, width), NARROW), ((width, hidden), jnp.float32)],
        [VMEM] * (n_row + 1),
    )(own, kept, *parts[::-1])
    return act, grad_features, grad_weight


def solution(mesh):
    placed = (
        P(("groups", "row", "col"), None),
        P(),
        P(("groups", "row", "col"), None),
        P(("groups", "row"), "col", None, None, None),
        P(("groups", "row"), "col", None),
        P(("groups", "row"), "col", None),
        P(("groups", "row"), "col"),
    )
    return jax.shard_map(
        per_device,
        mesh=mesh,
        in_specs=placed,
        out_specs=(
            P(("groups", "row", "col"), None),
            P(("groups", "row", "col"), None),
            P("groups", None),
        ),
        check_vma=False,
    )
```

```python
import functools

import jax
import jax.numpy as jnp
from jax import lax
from jax.experimental import pallas as pl
from jax.experimental.pallas import tpu as pltpu
from jax.sharding import PartitionSpec as P

VMEM = pl.BlockSpec(memory_space=pltpu.VMEM)
ANY = pl.BlockSpec(memory_space=pl.ANY)
LEAST = 16 * 1024 * 1024
NARROW = jnp.bfloat16


def call(kernel, outs, in_specs, scratch=(), flops=0, need=0, after=(), aliases=None):
    outs = tuple(jax.ShapeDtypeStruct(shape, dtype) for shape, dtype in outs)
    late = len(after)
    run = pl.pallas_call(
        (lambda *refs: kernel(*refs[late:])) if late else kernel,
        out_shape=outs,
        in_specs=[ANY] * late + list(in_specs),
        out_specs=(VMEM,) * len(outs),
        input_output_aliases=aliases or {},
        scratch_shapes=scratch,
        compiler_params=pltpu.CompilerParams(vmem_limit_bytes=LEAST + need),
        cost_estimate=pl.CostEstimate(flops=flops, bytes_accessed=need, transcendentals=0),
    )
    return functools.partial(run, *after)


def ring_place(k, axis):
    return k ^ (k >> 1) if axis == "col" and lax.axis_size(axis) == 4 else k


def exchange(sends, axis, ahead):
    n = lax.axis_size(axis)

    def target(s, d):
        return ring_place((ring_place(s, axis) + (d if ahead else -d)) % n, axis)

    return [
        lax.ppermute(send, axis, [(s, target(s, d)) for s in range(n)])
        for d, send in enumerate(sends, 1)
    ]


def odd_row():
    return lax.rem(lax.axis_index("row"), 2) == 1


def start_order(n):
    return [*range(2, n), 1]


def swap(value, axis, distance):
    n = lax.axis_size(axis)
    return lax.ppermute(value, axis, [(s, s ^ distance) for s in range(n)])


def wide(value):
    return value.astype(jnp.float32)


def split(value):
    high = value.astype(NARROW)
    return high, (value - wide(high)).astype(NARROW)


def dot(left, right, dims=((1,), (0,))):
    return lax.dot_general(left, right, (dims, ((), ())), preferred_element_type=jnp.float32)


def zero_kernel(out):
    out[...] = jnp.zeros_like(out)


def dense_kernel(piece, paired, blank, vals, rows_in, cols_in, count_in, near, rows, cols, count, sems):
    copies = [
        pltpu.make_async_copy(source, target, sems.at[k])
        for k, (source, target) in enumerate(((rows_in, rows), (cols_in, cols), (count_in, count)))
    ]
    for copy in copies:
        copy.start()
    side = vals.shape[-1]
    for copy in copies:
        copy.wait()

    def ahead(there):
        n, here = lax.axis_size("col"), lax.axis_index("col")
        return lax.rem(ring_place(there, "col") - ring_place(here, "col") + n, n)

    def add(t, _):
        row, col = rows[0, 0, t], cols[0, 0, t]
        if paired:
            place = lax.rem((row // piece) ^ lax.axis_index("col"), 2) * 2 + row // piece // 2
        else:
            place = ahead(row // piece)
        row = place * piece + lax.rem(row, piece)
        col = ((col // piece) ^ lax.axis_index("row")) * piece + lax.rem(col, piece)
        down = pl.ds(pl.multiple_of(row * side, side), side)
        across = pl.ds(pl.multiple_of(col * side, side), side)
        near[down, across] = vals[0, 0, t]
        return 0

    lax.fori_loop(0, count[0, 0], add, 0)


def turn_kernel(step, near, far):
    def turn(k, _):
        band = pl.ds(pl.multiple_of(k * step, step), step)
        far[:, band] = near[band, :].T
        return 0

    lax.fori_loop(0, near.shape[0] // step, turn, 0)


def tree(terms):
    while len(terms) > 1:
        middle = len(terms) // 2
        terms = [left + right for left, right in zip(terms[:middle], terms[middle:])]
    return terms[0]


def stack(operands):
    own, *others = [operand[...] for operand in operands]
    order = start_order(len(operands))
    return jnp.concatenate([own] + [others[order.index(d)] for d in range(1, len(operands))], axis=0)


def forward_kernel(n, matrix, *refs):
    operands, own, sends = refs[:n], refs[n], refs[n + 1 :]
    rows = own.shape[0]
    product = dot(matrix[...], stack(operands))
    own[...] = product[:rows]
    for d, send in enumerate(sends, 1):
        send[...] = product[d * rows : (d + 1) * rows].astype(send.dtype)


def layer(total, weight, cotangent):
    high, low = split(total)
    pre = dot(high, weight) + dot(low, weight)
    sigma = jax.nn.sigmoid(pre)
    grad = wide(cotangent) * sigma * (1.0 + pre * (1.0 - sigma))
    grad_high, grad_low = split(grad)
    across, down = ((1,), (1,)), ((0,), (0,))
    back = dot(grad_high, weight, across) + dot(grad_low, weight, across)
    term = dot(high, grad_high, down) + dot(low, grad_high, down) + dot(high, grad_low, down)
    return pre, back, term


def store_layer(back, term, message, other):
    nodes, half = back.shape[0], other.shape[1]
    odd = odd_row()
    left, right = term[:, :half], term[:, half:]
    message[:nodes] = back.astype(message.dtype)
    message[nodes:] = jnp.where(odd, right, left).astype(message.dtype)
    other[...] = jnp.where(odd, left, right).astype(other.dtype)


def layer_kernel(*refs):
    *parts, weight, cotangent, message, other, pre_out = refs
    total = tree([wide(part[...]) for part in parts])
    pre, back, term = layer(total, weight[...], cotangent[...])
    pre_out[...] = pre
    store_layer(back, term, message, other)


def in_middle():
    my_col = lax.axis_index("col")
    return (my_col == 1) | (my_col == 2)


def paired_forward_kernel(n, matrix, *refs):
    operands, (own, first, second, third) = refs[:n], refs[n:]
    product = dot(matrix[...], stack(operands)).astype(own.dtype)
    rows = own.shape[0]
    same, other = product[:rows], product[rows:]
    middle = in_middle()
    own[...] = same
    first[...] = jnp.where(middle, same, other)
    second[...] = other
    third[...] = jnp.where(middle, other, same)


def paired_layer_kernel(own, first, second, third, weight, cotangent, beyond, *refs):
    message, other, pre_out = refs
    nodes = cotangent.shape[0]
    middle = in_middle()
    partner = jnp.where(middle, third[...], first[...])
    side = jnp.where(middle, first[...], third[...])
    total = (wide(own[...]) + wide(partner)) + (wide(second[...]) + wide(side))
    high_col = lax.axis_index("col") >= 2
    here, there = cotangent[...], beyond[...]
    both = jnp.concatenate(
        [jnp.where(high_col, there, here), jnp.where(high_col, here, there)], axis=0
    )
    pre, back, term = layer(total, weight[...], both)
    pre_out[...] = jnp.where(high_col, pre[nodes:], pre[:nodes])
    store_layer(back, term, message, other)


def message_kernel(sent, came, message):
    nodes = sent.shape[0] - came.shape[0]
    message[:nodes] = sent[:nodes]
    message[nodes:] = (wide(sent[nodes:]) + wide(came[...])).astype(message.dtype)


def act_kernel(pre, act):
    act[...] = (pre[...] * jax.nn.sigmoid(pre[...])).astype(act.dtype)


def begin_kernel(backs, matrix, message, product):
    product[...] = dot(matrix[:, :backs], message[:backs])


def backward_kernel(n, n_others, matrix, begun, *refs):
    messages, others, refs = refs[:n], refs[n : n + n_others], refs[n + n_others :]
    own, kept, *sends, product = refs
    rows = own.shape[0]
    backs = messages[0].shape[0] - kept.shape[0]
    stacked = jnp.concatenate([message[:backs] for message in messages[1:]], axis=0)
    product[...] = begun[...] + dot(matrix[:, backs:], stacked)
    own[...] = product[:rows]
    term = tree([wide(message[backs:]) for message in messages])
    if others:
        term = term + tree([wide(other[...]) for other in others])
    term = term.astype(kept.dtype)
    kept[...] = term
    here, size = lax.axis_index("row"), lax.axis_size("row")
    odd_col = lax.rem(lax.axis_index("col"), 2) == 1
    for d, send in enumerate(sends, 1):
        there = lax.rem(here + jnp.where(odd_col, size - d, d), size)
        start = pl.multiple_of((there ^ here) * rows, rows)
        send[:rows] = product[pl.ds(start, rows)].astype(send.dtype)
        send[rows:] = term


def last_kernel(scale, own, kept, *refs):
    *messages, features_out, weight_out = refs
    nodes, half = own.shape[0], kept.shape[1]
    features_out[...] = tree(
        [own[...]] + [wide(message[:nodes]) for message in messages]
    ).astype(features_out.dtype)
    terms = [wide(kept[...])] + [wide(message[nodes:]) for message in messages]
    mine, other = tree(terms[::2]) * scale, tree(terms[1::2]) * scale
    odd = odd_row()
    weight_out[:, :half] = jnp.where(odd, other, mine)
    weight_out[:, half:] = jnp.where(odd, mine, other)


def per_device(features, weight, cotangent, tile_values, tile_rows, tile_cols, tile_count):
    slots, side = tile_values.shape[2:4]
    n_row, n_col = lax.axis_size("row"), lax.axis_size("col")
    nodes, width = features.shape
    hidden = weight.shape[1]
    down, across = n_col * nodes, n_row * nodes
    dense_bytes = 2 * down * across

    paired = n_col == 4
    gathered = [swap(features, "row", d) for d in start_order(n_row)]
    (blank,) = call(zero_kernel, [((down, across), NARROW)], [], need=dense_bytes)()
    (near,) = call(
        functools.partial(dense_kernel, nodes // side, paired),
        [((down, across), NARROW)],
        [VMEM] * 5,
        aliases={0: 0},
        scratch=[
            pltpu.SMEM(tile_rows.shape, jnp.int32),
            pltpu.SMEM(tile_cols.shape, jnp.int32),
            pltpu.SMEM(tile_count.shape, jnp.int32),
            pltpu.SemaphoreType.DMA((3,)),
        ],
        need=2 * dense_bytes,
    )(blank, tile_values, tile_rows, tile_cols, tile_count)

    forward = dict(flops=2 * down * across * width, need=2 * dense_bytes)
    if paired:
        layers = 2
        own, *sends = call(
            functools.partial(paired_forward_kernel, n_row),
            [((2 * nodes, width), NARROW)] * 4,
            [VMEM] * (1 + n_row),
            **forward,
        )(near, features, *gathered)
        layer_call, cotangents = paired_layer_kernel, [cotangent, swap(cotangent, "col", 2)]
    else:
        layers = 1
        own, *sends = call(
            functools.partial(forward_kernel, n_row),
            [((nodes, width), jnp.float32)] + [((nodes, width), NARROW)] * (n_col - 1),
            [VMEM] * (1 + n_row),
            **forward,
        )(near, features, *gathered)
        layer_call, cotangents = layer_kernel, [cotangent]
    parts = exchange(sends, "col", True)
    (far,) = call(
        functools.partial(turn_kernel, side),
        [((across, down), NARROW)],
        [VMEM],
        need=3 * dense_bytes,
    )(near)

    half = hidden // 2
    square = (width, half)
    message = ((layers * nodes + width, width), NARROW)
    sent, other, pre = call(
        layer_call,
        [message, (square, NARROW), ((nodes, hidden), jnp.float32)],
        [VMEM] * (n_col + 1 + len(cotangents)),
        flops=14 * layers * nodes * width * hidden,
        after=[far],
    )(own, *parts, weight, *cotangents)
    if paired:
        corner = [
            (r * n_col + c, (r ^ 1) * n_col + (c ^ 1)) for r in range(n_row) for c in range(n_col)
        ]
        messages = [sent, swap(sent, "col", 1)]
        others = [swap(other, "row", 1), lax.ppermute(other, ("row", "col"), corner)]
    else:
        (sent,) = call(message_kernel, [message], [VMEM] * 2)(sent, swap(other, "row", 1))
        messages = [sent] + exchange([sent] * (n_col - 1), "col", False)
        others = []
    (act,) = call(act_kernel, [((nodes, hidden), NARROW)], [VMEM])(pre)

    message = ((nodes + width, width), NARROW)
    (begun,) = call(
        functools.partial(begin_kernel, layers * nodes),
        [((across, width), jnp.float32)],
        [VMEM] * 2,
        **forward,
    )(far, sent)
    message = ((nodes + width, width), NARROW)
    own, kept, *sends = call(
        functools.partial(backward_kernel, len(messages), len(others)),
        [((nodes, width), jnp.float32), (square, NARROW)] + [message] * (n_row - 1),
        [VMEM] * (2 + len(messages) + len(others)),
        scratch=[pltpu.VMEM((across, width), jnp.float32)],
        **forward,
    )(far, begun, *messages, *others)
    parts = []
    for d, send in enumerate(sends, 1):
        pairs = []
        for r in range(n_row):
            for c in range(n_col):
                there = (r + (-d if c % 2 else d)) % n_row
                pairs.append((r * n_col + c, there * n_col + c))
        parts.append(lax.ppermute(send, ("row", "col"), pairs))

    scale = float(nodes * n_row * n_col) ** -0.5
    grad_features, grad_weight = call(
        functools.partial(last_kernel, scale),
        [((nodes, width), NARROW), ((width, hidden), jnp.float32)],
        [VMEM] * (n_row + 1),
    )(own, kept, *parts)
    return act, grad_features, grad_weight


def solution(mesh):
    placed = (
        P(("groups", "row", "col"), None),
        P(),
        P(("groups", "row", "col"), None),
        P(("groups", "row"), "col", None, None, None),
        P(("groups", "row"), "col", None),
        P(("groups", "row"), "col", None),
        P(("groups", "row"), "col"),
    )
    return jax.shard_map(
        per_device,
        mesh=mesh,
        in_specs=placed,
        out_specs=(
            P(("groups", "row", "col"), None),
            P(("groups", "row", "col"), None),
            P("groups", None),
        ),
        check_vma=False,
    )
```

```python
import functools

import jax
import jax.numpy as jnp
from jax import lax
from jax.experimental import pallas as pl
from jax.experimental.pallas import tpu as pltpu
from jax.sharding import PartitionSpec as P

VMEM = pl.BlockSpec(memory_space=pltpu.VMEM)
ANY = pl.BlockSpec(memory_space=pl.ANY)
LEAST = 16 * 1024 * 1024
NARROW = jnp.bfloat16


def call(kernel, outs, in_specs, scratch=(), flops=0, need=0, after=(), aliases=None):
    outs = tuple(jax.ShapeDtypeStruct(shape, dtype) for shape, dtype in outs)
    late = len(after)
    run = pl.pallas_call(
        (lambda *refs: kernel(*refs[late:])) if late else kernel,
        out_shape=outs,
        in_specs=[ANY] * late + list(in_specs),
        out_specs=(VMEM,) * len(outs),
        input_output_aliases=aliases or {},
        scratch_shapes=scratch,
        compiler_params=pltpu.CompilerParams(vmem_limit_bytes=LEAST + need),
        cost_estimate=pl.CostEstimate(flops=flops, bytes_accessed=need, transcendentals=0),
    )
    return functools.partial(run, *after)


def ring_place(k, axis):
    return k ^ (k >> 1) if axis == "col" and lax.axis_size(axis) == 4 else k


def exchange(sends, axis, ahead):
    n = lax.axis_size(axis)

    def target(s, d):
        return ring_place((ring_place(s, axis) + (d if ahead else -d)) % n, axis)

    return [
        lax.ppermute(send, axis, [(s, target(s, d)) for s in range(n)])
        for d, send in enumerate(sends, 1)
    ]


def odd_row():
    return lax.rem(lax.axis_index("row"), 2) == 1


def start_order(n):
    return [*range(2, n), 1]


def swap(value, axis, distance):
    n = lax.axis_size(axis)
    return lax.ppermute(value, axis, [(s, s ^ distance) for s in range(n)])


def wide(value):
    return value.astype(jnp.float32)


def split(value):
    high = value.astype(NARROW)
    return high, (value - wide(high)).astype(NARROW)


def dot(left, right, dims=((1,), (0,))):
    return lax.dot_general(left, right, (dims, ((), ())), preferred_element_type=jnp.float32)


def zero_kernel(out):
    out[...] = jnp.zeros_like(out)


def dense_kernel(piece, paired, blank, vals, rows_in, cols_in, count_in, near, rows, cols, count, sems):
    copies = [
        pltpu.make_async_copy(source, target, sems.at[k])
        for k, (source, target) in enumerate(((rows_in, rows), (cols_in, cols), (count_in, count)))
    ]
    for copy in copies:
        copy.start()
    side = vals.shape[-1]
    for copy in copies:
        copy.wait()

    def ahead(there):
        n, here = lax.axis_size("col"), lax.axis_index("col")
        return lax.rem(ring_place(there, "col") - ring_place(here, "col") + n, n)

    def add(t, _):
        row, col = rows[0, 0, t], cols[0, 0, t]
        if paired:
            place = lax.rem((row // piece) ^ lax.axis_index("col"), 2) * 2 + row // piece // 2
        else:
            place = ahead(row // piece)
        row = place * piece + lax.rem(row, piece)
        col = ((col // piece) ^ lax.axis_index("row")) * piece + lax.rem(col, piece)
        down = pl.ds(pl.multiple_of(row * side, side), side)
        across = pl.ds(pl.multiple_of(col * side, side), side)
        near[down, across] = vals[0, 0, t]
        return 0

    lax.fori_loop(0, count[0, 0], add, 0)


def turn_kernel(step, near, far):
    def turn(k, _):
        band = pl.ds(pl.multiple_of(k * step, step), step)
        far[:, band] = near[band, :].T
        return 0

    lax.fori_loop(0, near.shape[0] // step, turn, 0)


def tree(terms):
    while len(terms) > 1:
        middle = len(terms) // 2
        terms = [left + right for left, right in zip(terms[:middle], terms[middle:])]
    return terms[0]


def stack(operands):
    own, *others = [operand[...] for operand in operands]
    order = start_order(len(operands))
    return jnp.concatenate([own] + [others[order.index(d)] for d in range(1, len(operands))], axis=0)


def forward_kernel(n, matrix, *refs):
    operands, own, sends = refs[:n], refs[n], refs[n + 1 :]
    rows = own.shape[0]
    product = dot(matrix[...], stack(operands))
    own[...] = product[:rows]
    for d, send in enumerate(sends, 1):
        send[...] = product[d * rows : (d + 1) * rows].astype(send.dtype)


def layer(total, weight, cotangent):
    nodes = total.shape[0]
    high, low = split(total)
    pre = dot(jnp.concatenate([high, low], axis=0), weight)
    pre = pre[:nodes] + pre[nodes:]
    sigma = jax.nn.sigmoid(pre)
    grad = wide(cotangent) * sigma * (1.0 + pre * (1.0 - sigma))
    grad_high, grad_low = split(grad)
    across, down = ((1,), (1,)), ((0,), (0,))
    back = dot(jnp.concatenate([grad_high, grad_low], axis=0), weight, across)
    back = back[:nodes] + back[nodes:]
    left = jnp.concatenate([high, low, high], axis=0)
    term = dot(left, jnp.concatenate([grad_high, grad_high, grad_low], axis=0), down)
    return pre, back, term


def store_layer(back, term, message, other):
    nodes, half = back.shape[0], other.shape[1]
    odd = odd_row()
    left, right = term[:, :half], term[:, half:]
    message[:nodes] = back.astype(message.dtype)
    message[nodes:] = jnp.where(odd, right, left).astype(message.dtype)
    other[...] = jnp.where(odd, left, right).astype(other.dtype)


def layer_kernel(*refs):
    *parts, weight, cotangent, message, other, pre_out = refs
    total = tree([wide(part[...]) for part in parts])
    pre, back, term = layer(total, weight[...], cotangent[...])
    pre_out[...] = pre
    store_layer(back, term, message, other)


def in_middle():
    my_col = lax.axis_index("col")
    return (my_col == 1) | (my_col == 2)


def paired_forward_kernel(n, matrix, *refs):
    operands, (own, first, second, third) = refs[:n], refs[n:]
    product = dot(matrix[...], stack(operands)).astype(own.dtype)
    rows = own.shape[0]
    same, other = product[:rows], product[rows:]
    middle = in_middle()
    own[...] = same
    first[...] = jnp.where(middle, same, other)
    second[...] = other
    third[...] = jnp.where(middle, other, same)


def paired_layer_kernel(own, first, second, third, weight, cotangent, beyond, *refs):
    message, other, pre_out = refs
    nodes = cotangent.shape[0]
    middle = in_middle()
    partner = jnp.where(middle, third[...], first[...])
    side = jnp.where(middle, first[...], third[...])
    total = (wide(own[...]) + wide(partner)) + (wide(second[...]) + wide(side))
    high_col = lax.axis_index("col") >= 2
    here, there = cotangent[...], beyond[...]
    both = jnp.concatenate(
        [jnp.where(high_col, there, here), jnp.where(high_col, here, there)], axis=0
    )
    pre, back, term = layer(total, weight[...], both)
    pre_out[...] = jnp.where(high_col, pre[nodes:], pre[:nodes])
    store_layer(back, term, message, other)


def message_kernel(sent, came, message):
    nodes = sent.shape[0] - came.shape[0]
    message[:nodes] = sent[:nodes]
    message[nodes:] = (wide(sent[nodes:]) + wide(came[...])).astype(message.dtype)


def act_kernel(pre, act):
    act[...] = (pre[...] * jax.nn.sigmoid(pre[...])).astype(act.dtype)


def begin_kernel(backs, matrix, message, product):
    product[...] = dot(matrix[:, :backs], message[:backs])


def backward_kernel(n, n_others, matrix, begun, *refs):
    messages, others, refs = refs[:n], refs[n : n + n_others], refs[n + n_others :]
    own, kept, *sends, product = refs
    rows = own.shape[0]
    backs = messages[0].shape[0] - kept.shape[0]
    stacked = jnp.concatenate([message[:backs] for message in messages[1:]], axis=0)
    product[...] = begun[...] + dot(matrix[:, backs:], stacked)
    own[...] = product[:rows]
    term = tree([wide(message[backs:]) for message in messages])
    if others:
        term = term + tree([wide(other[...]) for other in others])
    term = term.astype(kept.dtype)
    kept[...] = term
    here, size = lax.axis_index("row"), lax.axis_size("row")
    for d, send in enumerate(sends, 1):
        start = pl.multiple_of((lax.rem(here + d, size) ^ here) * rows, rows)
        send[:rows] = product[pl.ds(start, rows)].astype(send.dtype)
        send[rows:] = term


def last_kernel(scale, own, kept, *refs):
    *messages, features_out, weight_out = refs
    nodes, half = own.shape[0], kept.shape[1]
    features_out[...] = tree(
        [own[...]] + [wide(message[:nodes]) for message in messages]
    ).astype(features_out.dtype)
    terms = [wide(kept[...])] + [wide(message[nodes:]) for message in messages]
    mine, other = tree(terms[::2]) * scale, tree(terms[1::2]) * scale
    odd = odd_row()
    weight_out[:, :half] = jnp.where(odd, other, mine)
    weight_out[:, half:] = jnp.where(odd, mine, other)


def per_device(features, weight, cotangent, tile_values, tile_rows, tile_cols, tile_count):
    slots, side = tile_values.shape[2:4]
    n_row, n_col = lax.axis_size("row"), lax.axis_size("col")
    nodes, width = features.shape
    hidden = weight.shape[1]
    down, across = n_col * nodes, n_row * nodes
    dense_bytes = 2 * down * across

    paired = n_col == 4
    gathered = [swap(features, "row", d) for d in start_order(n_row)]
    (blank,) = call(zero_kernel, [((down, across), NARROW)], [], need=dense_bytes)()
    (near,) = call(
        functools.partial(dense_kernel, nodes // side, paired),
        [((down, across), NARROW)],
        [VMEM] * 5,
        aliases={0: 0},
        scratch=[
            pltpu.SMEM(tile_rows.shape, jnp.int32),
            pltpu.SMEM(tile_cols.shape, jnp.int32),
            pltpu.SMEM(tile_count.shape, jnp.int32),
            pltpu.SemaphoreType.DMA((3,)),
        ],
        need=2 * dense_bytes,
    )(blank, tile_values, tile_rows, tile_cols, tile_count)

    forward = dict(flops=2 * down * across * width, need=2 * dense_bytes)
    if paired:
        layers = 2
        own, *sends = call(
            functools.partial(paired_forward_kernel, n_row),
            [((2 * nodes, width), NARROW)] * 4,
            [VMEM] * (1 + n_row),
            **forward,
        )(near, features, *gathered)
        layer_call, cotangents = paired_layer_kernel, [cotangent, swap(cotangent, "col", 2)]
    else:
        layers = 1
        own, *sends = call(
            functools.partial(forward_kernel, n_row),
            [((nodes, width), jnp.float32)] + [((nodes, width), NARROW)] * (n_col - 1),
            [VMEM] * (1 + n_row),
            **forward,
        )(near, features, *gathered)
        layer_call, cotangents = layer_kernel, [cotangent]
    parts = exchange(sends, "col", True)
    (far,) = call(
        functools.partial(turn_kernel, side),
        [((across, down), NARROW)],
        [VMEM],
        need=3 * dense_bytes,
    )(near)

    half = hidden // 2
    square = (width, half)
    message = ((layers * nodes + width, width), NARROW)
    sent, other, pre = call(
        layer_call,
        [message, (square, NARROW), ((nodes, hidden), jnp.float32)],
        [VMEM] * (n_col + 1 + len(cotangents)),
        flops=14 * layers * nodes * width * hidden,
        after=[far],
    )(own, *parts, weight, *cotangents)
    if paired:
        corner = [
            (r * n_col + c, (r ^ 1) * n_col + (c ^ 1)) for r in range(n_row) for c in range(n_col)
        ]
        messages = [sent, swap(sent, "col", 1)]
        others = [swap(other, "row", 1), lax.ppermute(other, ("row", "col"), corner)]
    else:
        (sent,) = call(message_kernel, [message], [VMEM] * 2)(sent, swap(other, "row", 1))
        messages = [sent] + exchange([sent] * (n_col - 1), "col", False)
        others = []
    (act,) = call(act_kernel, [((nodes, hidden), NARROW)], [VMEM])(pre)

    message = ((nodes + width, width), NARROW)
    (begun,) = call(
        functools.partial(begin_kernel, layers * nodes),
        [((across, width), jnp.float32)],
        [VMEM] * 2,
        **forward,
    )(far, sent)
    message = ((nodes + width, width), NARROW)
    own, kept, *sends = call(
        functools.partial(backward_kernel, len(messages), len(others)),
        [((nodes, width), jnp.float32), (square, NARROW)] + [message] * (n_row - 1),
        [VMEM] * (2 + len(messages) + len(others)),
        scratch=[pltpu.VMEM((across, width), jnp.float32)],
        **forward,
    )(far, begun, *messages, *others)
    parts = exchange(sends, "row", True)

    scale = float(nodes * n_row * n_col) ** -0.5
    grad_features, grad_weight = call(
        functools.partial(last_kernel, scale),
        [((nodes, width), NARROW), ((width, hidden), jnp.float32)],
        [VMEM] * (n_row + 1),
    )(own, kept, *parts)
    return act, grad_features, grad_weight


def solution(mesh):
    placed = (
        P(("groups", "row", "col"), None),
        P(),
        P(("groups", "row", "col"), None),
        P(("groups", "row"), "col", None, None, None),
        P(("groups", "row"), "col", None),
        P(("groups", "row"), "col", None),
        P(("groups", "row"), "col"),
    )
    return jax.shard_map(
        per_device,
        mesh=mesh,
        in_specs=placed,
        out_specs=(
            P(("groups", "row", "col"), None),
            P(("groups", "row", "col"), None),
            P("groups", None),
        ),
        check_vma=False,
    )
```

```python
import functools

import jax
import jax.numpy as jnp
from jax import lax
from jax.experimental import pallas as pl
from jax.experimental.pallas import tpu as pltpu
from jax.sharding import PartitionSpec as P

VMEM = pl.BlockSpec(memory_space=pltpu.VMEM)
ANY = pl.BlockSpec(memory_space=pl.ANY)
LEAST = 16 * 1024 * 1024
NARROW = jnp.bfloat16


def call(kernel, outs, in_specs, scratch=(), flops=0, need=0, after=()):
    outs = tuple(jax.ShapeDtypeStruct(shape, dtype) for shape, dtype in outs)
    late = len(after)
    run = pl.pallas_call(
        (lambda *refs: kernel(*refs[late:])) if late else kernel,
        out_shape=outs,
        in_specs=[ANY] * late + list(in_specs),
        out_specs=(VMEM,) * len(outs),
        scratch_shapes=scratch,
        compiler_params=pltpu.CompilerParams(vmem_limit_bytes=LEAST + need),
        cost_estimate=pl.CostEstimate(flops=flops, bytes_accessed=need, transcendentals=0),
    )
    return functools.partial(run, *after)


def ring_place(k, axis):
    return k ^ (k >> 1) if axis == "col" and lax.axis_size(axis) == 4 else k


def exchange(sends, axis, ahead):
    n = lax.axis_size(axis)

    def target(s, d):
        return ring_place((ring_place(s, axis) + (d if ahead else -d)) % n, axis)

    return [
        lax.ppermute(send, axis, [(s, target(s, d)) for s in range(n)])
        for d, send in enumerate(sends, 1)
    ]


def odd_row():
    return lax.rem(lax.axis_index("row"), 2) == 1


def start_order(n):
    return [*range(2, n), 1]


def swap(value, axis, distance):
    n = lax.axis_size(axis)
    return lax.ppermute(value, axis, [(s, s ^ distance) for s in range(n)])


def wide(value):
    return value.astype(jnp.float32)


def split(value):
    high = value.astype(NARROW)
    return high, (value - wide(high)).astype(NARROW)


def dot(left, right, dims=((1,), (0,))):
    return lax.dot_general(left, right, (dims, ((), ())), preferred_element_type=jnp.float32)


def zero_kernel(out):
    out[...] = jnp.zeros_like(out)


def dense_kernel(piece, paired, blank, vals, rows_in, cols_in, count_in, near, rows, cols, count, sems):
    copies = [
        pltpu.make_async_copy(source, target, sems.at[k])
        for k, (source, target) in enumerate(((rows_in, rows), (cols_in, cols), (count_in, count)))
    ]
    for copy in copies:
        copy.start()
    side = vals.shape[-1]
    near[...] = blank[...]
    for copy in copies:
        copy.wait()

    def ahead(there):
        n, here = lax.axis_size("col"), lax.axis_index("col")
        return lax.rem(ring_place(there, "col") - ring_place(here, "col") + n, n)

    def add(t, _):
        row, col = rows[0, 0, t], cols[0, 0, t]
        if paired:
            place = lax.rem((row // piece) ^ lax.axis_index("col"), 2) * 2 + row // piece // 2
        else:
            place = ahead(row // piece)
        row = place * piece + lax.rem(row, piece)
        col = ((col // piece) ^ lax.axis_index("row")) * piece + lax.rem(col, piece)
        down = pl.ds(pl.multiple_of(row * side, side), side)
        across = pl.ds(pl.multiple_of(col * side, side), side)
        near[down, across] = vals[0, 0, t]
        return 0

    lax.fori_loop(0, count[0, 0], add, 0)


def turn_kernel(step, near, far):
    def turn(k, _):
        band = pl.ds(pl.multiple_of(k * step, step), step)
        far[:, band] = near[band, :].T
        return 0

    lax.fori_loop(0, near.shape[0] // step, turn, 0)


def tree(terms):
    while len(terms) > 1:
        middle = len(terms) // 2
        terms = [left + right for left, right in zip(terms[:middle], terms[middle:])]
    return terms[0]


def stack(operands):
    own, *others = [operand[...] for operand in operands]
    order = start_order(len(operands))
    return jnp.concatenate([own] + [others[order.index(d)] for d in range(1, len(operands))], axis=0)


def forward_kernel(n, matrix, *refs):
    operands, own, sends = refs[:n], refs[n], refs[n + 1 :]
    rows = own.shape[0]
    product = dot(matrix[...], stack(operands))
    own[...] = product[:rows]
    for d, send in enumerate(sends, 1):
        send[...] = product[d * rows : (d + 1) * rows].astype(send.dtype)


def layer(total, weight, cotangent):
    nodes = total.shape[0]
    high, low = split(total)
    pre = dot(jnp.concatenate([high, low], axis=0), weight)
    pre = pre[:nodes] + pre[nodes:]
    sigma = jax.nn.sigmoid(pre)
    grad = wide(cotangent) * sigma * (1.0 + pre * (1.0 - sigma))
    grad_high, grad_low = split(grad)
    across, down = ((1,), (1,)), ((0,), (0,))
    back = dot(jnp.concatenate([grad_high, grad_low], axis=0), weight, across)
    back = back[:nodes] + back[nodes:]
    left = jnp.concatenate([high, low, high], axis=0)
    term = dot(left, jnp.concatenate([grad_high, grad_high, grad_low], axis=0), down)
    return pre, back, term


def store_layer(back, term, message, other):
    nodes, half = back.shape[0], other.shape[1]
    odd = odd_row()
    left, right = term[:, :half], term[:, half:]
    message[:nodes] = back.astype(message.dtype)
    message[nodes:] = jnp.where(odd, right, left).astype(message.dtype)
    other[...] = jnp.where(odd, left, right).astype(other.dtype)


def layer_kernel(*refs):
    *parts, weight, cotangent, message, other, pre_out = refs
    total = tree([wide(part[...]) for part in parts])
    pre, back, term = layer(total, weight[...], cotangent[...])
    pre_out[...] = pre
    store_layer(back, term, message, other)


def in_middle():
    my_col = lax.axis_index("col")
    return (my_col == 1) | (my_col == 2)


def paired_forward_kernel(n, matrix, *refs):
    operands, (own, first, second, third) = refs[:n], refs[n:]
    product = dot(matrix[...], stack(operands)).astype(own.dtype)
    rows = own.shape[0]
    same, other = product[:rows], product[rows:]
    middle = in_middle()
    own[...] = same
    first[...] = jnp.where(middle, same, other)
    second[...] = other
    third[...] = jnp.where(middle, other, same)


def paired_layer_kernel(own, first, second, third, weight, cotangent, beyond, *refs):
    message, other, pre_out = refs
    nodes = cotangent.shape[0]
    middle = in_middle()
    partner = jnp.where(middle, third[...], first[...])
    side = jnp.where(middle, first[...], third[...])
    total = (wide(own[...]) + wide(partner)) + (wide(second[...]) + wide(side))
    high_col = lax.axis_index("col") >= 2
    here, there = cotangent[...], beyond[...]
    both = jnp.concatenate(
        [jnp.where(high_col, there, here), jnp.where(high_col, here, there)], axis=0
    )
    pre, back, term = layer(total, weight[...], both)
    pre_out[...] = jnp.where(high_col, pre[nodes:], pre[:nodes])
    store_layer(back, term, message, other)


def message_kernel(sent, came, message):
    nodes = sent.shape[0] - came.shape[0]
    message[:nodes] = sent[:nodes]
    message[nodes:] = (wide(sent[nodes:]) + wide(came[...])).astype(message.dtype)


def act_kernel(pre, act):
    act[...] = (pre[...] * jax.nn.sigmoid(pre[...])).astype(act.dtype)


def begin_kernel(backs, matrix, message, product):
    product[...] = dot(matrix[:, :backs], message[:backs])


def backward_kernel(n, n_others, matrix, begun, *refs):
    messages, others, refs = refs[:n], refs[n : n + n_others], refs[n + n_others :]
    own, kept, *sends, product = refs
    rows = own.shape[0]
    backs = messages[0].shape[0] - kept.shape[0]
    stacked = jnp.concatenate([message[:backs] for message in messages[1:]], axis=0)
    product[...] = begun[...] + dot(matrix[:, backs:], stacked)
    own[...] = product[:rows]
    term = tree([wide(message[backs:]) for message in messages])
    if others:
        term = term + tree([wide(other[...]) for other in others])
    term = term.astype(kept.dtype)
    kept[...] = term
    here, size = lax.axis_index("row"), lax.axis_size("row")
    for d, send in enumerate(sends, 1):
        start = pl.multiple_of((lax.rem(here + d, size) ^ here) * rows, rows)
        send[:rows] = product[pl.ds(start, rows)].astype(send.dtype)
        send[rows:] = term


def last_kernel(scale, own, kept, *refs):
    *messages, features_out, weight_out = refs
    nodes, half = own.shape[0], kept.shape[1]
    features_out[...] = tree(
        [own[...]] + [wide(message[:nodes]) for message in messages]
    ).astype(features_out.dtype)
    terms = [wide(kept[...])] + [wide(message[nodes:]) for message in messages]
    mine, other = tree(terms[::2]) * scale, tree(terms[1::2]) * scale
    odd = odd_row()
    weight_out[:, :half] = jnp.where(odd, other, mine)
    weight_out[:, half:] = jnp.where(odd, mine, other)


def per_device(features, weight, cotangent, tile_values, tile_rows, tile_cols, tile_count):
    slots, side = tile_values.shape[2:4]
    n_row, n_col = lax.axis_size("row"), lax.axis_size("col")
    nodes, width = features.shape
    hidden = weight.shape[1]
    down, across = n_col * nodes, n_row * nodes
    dense_bytes = 2 * down * across

    paired = n_col == 4
    gathered = [swap(features, "row", d) for d in start_order(n_row)]
    (blank,) = call(zero_kernel, [((down, across), NARROW)], [], need=dense_bytes)()
    (near,) = call(
        functools.partial(dense_kernel, nodes // side, paired),
        [((down, across), NARROW)],
        [VMEM] * 5,
        scratch=[
            pltpu.SMEM(tile_rows.shape, jnp.int32),
            pltpu.SMEM(tile_cols.shape, jnp.int32),
            pltpu.SMEM(tile_count.shape, jnp.int32),
            pltpu.SemaphoreType.DMA((3,)),
        ],
        need=2 * dense_bytes,
    )(blank, tile_values, tile_rows, tile_cols, tile_count)

    forward = dict(flops=2 * down * across * width, need=2 * dense_bytes)
    if paired:
        layers = 2
        own, *sends = call(
            functools.partial(paired_forward_kernel, n_row),
            [((2 * nodes, width), NARROW)] * 4,
            [VMEM] * (1 + n_row),
            **forward,
        )(near, features, *gathered)
        layer_call, cotangents = paired_layer_kernel, [cotangent, swap(cotangent, "col", 2)]
    else:
        layers = 1
        own, *sends = call(
            functools.partial(forward_kernel, n_row),
            [((nodes, width), jnp.float32)] + [((nodes, width), NARROW)] * (n_col - 1),
            [VMEM] * (1 + n_row),
            **forward,
        )(near, features, *gathered)
        layer_call, cotangents = layer_kernel, [cotangent]
    parts = exchange(sends, "col", True)
    (far,) = call(
        functools.partial(turn_kernel, side),
        [((across, down), NARROW)],
        [VMEM],
        need=3 * dense_bytes,
    )(near)

    half = hidden // 2
    square = (width, half)
    message = ((layers * nodes + width, width), NARROW)
    sent, other, pre = call(
        layer_call,
        [message, (square, NARROW), ((nodes, hidden), jnp.float32)],
        [VMEM] * (n_col + 1 + len(cotangents)),
        flops=14 * layers * nodes * width * hidden,
        after=[far],
    )(own, *parts, weight, *cotangents)
    if paired:
        corner = [
            (r * n_col + c, (r ^ 1) * n_col + (c ^ 1)) for r in range(n_row) for c in range(n_col)
        ]
        messages = [sent, swap(sent, "col", 1)]
        others = [swap(other, "row", 1), lax.ppermute(other, ("row", "col"), corner)]
    else:
        (sent,) = call(message_kernel, [message], [VMEM] * 2)(sent, swap(other, "row", 1))
        messages = [sent] + exchange([sent] * (n_col - 1), "col", False)
        others = []
    (act,) = call(act_kernel, [((nodes, hidden), NARROW)], [VMEM])(pre)

    message = ((nodes + width, width), NARROW)
    (begun,) = call(
        functools.partial(begin_kernel, layers * nodes),
        [((across, width), jnp.float32)],
        [VMEM] * 2,
        **forward,
    )(far, sent)
    message = ((nodes + width, width), NARROW)
    own, kept, *sends = call(
        functools.partial(backward_kernel, len(messages), len(others)),
        [((nodes, width), jnp.float32), (square, NARROW)] + [message] * (n_row - 1),
        [VMEM] * (2 + len(messages) + len(others)),
        scratch=[pltpu.VMEM((across, width), jnp.float32)],
        **forward,
    )(far, begun, *messages, *others)
    parts = exchange(sends, "row", True)

    scale = float(nodes * n_row * n_col) ** -0.5
    grad_features, grad_weight = call(
        functools.partial(last_kernel, scale),
        [((nodes, width), NARROW), ((width, hidden), jnp.float32)],
        [VMEM] * (n_row + 1),
    )(own, kept, *parts)
    return act, grad_features, grad_weight


def solution(mesh):
    placed = (
        P(("groups", "row", "col"), None),
        P(),
        P(("groups", "row", "col"), None),
        P(("groups", "row"), "col", None, None, None),
        P(("groups", "row"), "col", None),
        P(("groups", "row"), "col", None),
        P(("groups", "row"), "col"),
    )
    return jax.shard_map(
        per_device,
        mesh=mesh,
        in_specs=placed,
        out_specs=(
            P(("groups", "row", "col"), None),
            P(("groups", "row", "col"), None),
            P("groups", None),
        ),
        check_vma=False,
    )
```

```python
import functools

import jax
import jax.numpy as jnp
from jax import lax
from jax.experimental import pallas as pl
from jax.experimental.pallas import tpu as pltpu
from jax.sharding import PartitionSpec as P

VMEM = pl.BlockSpec(memory_space=pltpu.VMEM)
ANY = pl.BlockSpec(memory_space=pl.ANY)
LEAST = 16 * 1024 * 1024
NARROW = jnp.bfloat16


def call(kernel, outs, in_specs, scratch=(), flops=0, need=0, after=()):
    outs = tuple(jax.ShapeDtypeStruct(shape, dtype) for shape, dtype in outs)
    late = len(after)
    run = pl.pallas_call(
        (lambda *refs: kernel(*refs[late:])) if late else kernel,
        out_shape=outs,
        in_specs=[ANY] * late + list(in_specs),
        out_specs=(VMEM,) * len(outs),
        scratch_shapes=scratch,
        compiler_params=pltpu.CompilerParams(vmem_limit_bytes=LEAST + need),
        cost_estimate=pl.CostEstimate(flops=flops, bytes_accessed=need, transcendentals=0),
    )
    return functools.partial(run, *after)


def ring_place(k, axis):
    return k ^ (k >> 1) if axis == "col" and lax.axis_size(axis) == 4 else k


def exchange(sends, axis, ahead):
    n = lax.axis_size(axis)

    def target(s, d):
        return ring_place((ring_place(s, axis) + (d if ahead else -d)) % n, axis)

    return [
        lax.ppermute(send, axis, [(s, target(s, d)) for s in range(n)])
        for d, send in enumerate(sends, 1)
    ]


def odd_row():
    return lax.rem(lax.axis_index("row"), 2) == 1


def start_order(n):
    return [*range(2, n), 1]


def swap(value, axis, distance):
    n = lax.axis_size(axis)
    return lax.ppermute(value, axis, [(s, s ^ distance) for s in range(n)])


def wide(value):
    return value.astype(jnp.float32)


def split(value):
    high = value.astype(NARROW)
    return high, (value - wide(high)).astype(NARROW)


def dot(left, right, dims=((1,), (0,))):
    return lax.dot_general(left, right, (dims, ((), ())), preferred_element_type=jnp.float32)


def zero_kernel(out):
    out[...] = jnp.zeros_like(out)


def dense_kernel(piece, paired, blank, vals, rows_in, cols_in, count_in, near, rows, cols, count, sems):
    copies = [
        pltpu.make_async_copy(source, target, sems.at[k])
        for k, (source, target) in enumerate(((rows_in, rows), (cols_in, cols), (count_in, count)))
    ]
    for copy in copies:
        copy.start()
    side = vals.shape[-1]
    near[...] = blank[...]
    for copy in copies:
        copy.wait()

    def ahead(there):
        n, here = lax.axis_size("col"), lax.axis_index("col")
        return lax.rem(ring_place(there, "col") - ring_place(here, "col") + n, n)

    def add(t, _):
        row, col = rows[0, 0, t], cols[0, 0, t]
        if paired:
            place = lax.rem((row // piece) ^ lax.axis_index("col"), 2) * 2 + row // piece // 2
        else:
            place = ahead(row // piece)
        row = place * piece + lax.rem(row, piece)
        col = ((col // piece) ^ lax.axis_index("row")) * piece + lax.rem(col, piece)
        down = pl.ds(pl.multiple_of(row * side, side), side)
        across = pl.ds(pl.multiple_of(col * side, side), side)
        near[down, across] = vals[0, 0, t]
        return 0

    lax.fori_loop(0, count[0, 0], add, 0)


def turn_kernel(step, near, far):
    def turn(k, _):
        band = pl.ds(pl.multiple_of(k * step, step), step)
        far[:, band] = near[band, :].T
        return 0

    lax.fori_loop(0, near.shape[0] // step, turn, 0)


def tree(terms):
    while len(terms) > 1:
        middle = len(terms) // 2
        terms = [left + right for left, right in zip(terms[:middle], terms[middle:])]
    return terms[0]


def stack(operands):
    own, *others = [operand[...] for operand in operands]
    order = start_order(len(operands))
    return jnp.concatenate([own] + [others[order.index(d)] for d in range(1, len(operands))], axis=0)


def forward_kernel(n, matrix, *refs):
    operands, own, sends = refs[:n], refs[n], refs[n + 1 :]
    rows = own.shape[0]
    product = dot(matrix[...], stack(operands))
    own[...] = product[:rows]
    for d, send in enumerate(sends, 1):
        send[...] = product[d * rows : (d + 1) * rows].astype(send.dtype)


def layer(total, weight, cotangent):
    nodes = total.shape[0]
    high, low = split(total)
    pre = dot(jnp.concatenate([high, low], axis=0), weight)
    pre = pre[:nodes] + pre[nodes:]
    sigma = jax.nn.sigmoid(pre)
    grad = wide(cotangent) * sigma * (1.0 + pre * (1.0 - sigma))
    grad_high, grad_low = split(grad)
    across, down = ((1,), (1,)), ((0,), (0,))
    back = dot(jnp.concatenate([grad_high, grad_low], axis=0), weight, across)
    back = back[:nodes] + back[nodes:]
    left = jnp.concatenate([high, low, high], axis=0)
    term = dot(left, jnp.concatenate([grad_high, grad_high, grad_low], axis=0), down)
    return pre, back, term


def store_layer(back, term, message, other):
    nodes, half = back.shape[0], other.shape[1]
    odd = odd_row()
    left, right = term[:, :half], term[:, half:]
    message[:nodes] = back.astype(message.dtype)
    message[nodes:] = jnp.where(odd, right, left).astype(message.dtype)
    other[...] = jnp.where(odd, left, right).astype(other.dtype)


def layer_kernel(*refs):
    *parts, weight, cotangent, message, other, pre_out = refs
    total = tree([wide(part[...]) for part in parts])
    pre, back, term = layer(total, weight[...], cotangent[...])
    pre_out[...] = pre
    store_layer(back, term, message, other)


def in_middle():
    my_col = lax.axis_index("col")
    return (my_col == 1) | (my_col == 2)


def paired_forward_kernel(n, matrix, *refs):
    operands, (own, first, second, third) = refs[:n], refs[n:]
    product = dot(matrix[...], stack(operands)).astype(own.dtype)
    rows = own.shape[0]
    same, other = product[:rows], product[rows:]
    middle = in_middle()
    own[...] = same
    first[...] = jnp.where(middle, same, other)
    second[...] = other
    third[...] = jnp.where(middle, other, same)


def paired_layer_kernel(own, first, second, third, weight, cotangent, beyond, *refs):
    message, other, pre_out = refs
    nodes = cotangent.shape[0]
    middle = in_middle()
    partner = jnp.where(middle, third[...], first[...])
    side = jnp.where(middle, first[...], third[...])
    total = (wide(own[...]) + wide(partner)) + (wide(second[...]) + wide(side))
    high_col = lax.axis_index("col") >= 2
    here, there = cotangent[...], beyond[...]
    both = jnp.concatenate(
        [jnp.where(high_col, there, here), jnp.where(high_col, here, there)], axis=0
    )
    pre, back, term = layer(total, weight[...], both)
    pre_out[...] = jnp.where(high_col, pre[nodes:], pre[:nodes])
    store_layer(back, term, message, other)


def message_kernel(sent, came, message):
    nodes = sent.shape[0] - came.shape[0]
    message[:nodes] = sent[:nodes]
    message[nodes:] = (wide(sent[nodes:]) + wide(came[...])).astype(message.dtype)


def act_kernel(pre, act):
    act[...] = (pre[...] * jax.nn.sigmoid(pre[...])).astype(act.dtype)


def begin_kernel(backs, matrix, message, product):
    product[...] = dot(matrix[:, :backs], message[:backs])


def backward_kernel(n, n_others, matrix, begun, *refs):
    messages, others, refs = refs[:n], refs[n : n + n_others], refs[n + n_others :]
    own, kept, *sends, product = refs
    rows = own.shape[0]
    backs = messages[0].shape[0] - kept.shape[0]
    stacked = jnp.concatenate([message[:backs] for message in messages[1:]], axis=0)
    product[...] = begun[...] + dot(matrix[:, backs:], stacked)
    own[...] = product[:rows]
    term = tree([wide(message[backs:]) for message in messages])
    if others:
        term = term + tree([wide(other[...]) for other in others])
    term = term.astype(kept.dtype)
    kept[...] = term
    here, size = lax.axis_index("row"), lax.axis_size("row")
    for d, send in enumerate(sends, 1):
        start = pl.multiple_of((lax.rem(here + d, size) ^ here) * rows, rows)
        send[:rows] = product[pl.ds(start, rows)].astype(send.dtype)
        send[rows:] = term


def last_kernel(scale, own, kept, *refs):
    second, first, *messages, features_out, weight_out = refs
    messages = [first, second, *messages]
    nodes, half = own.shape[0], kept.shape[1]
    features_out[...] = tree(
        [own[...]] + [wide(message[:nodes]) for message in messages]
    ).astype(features_out.dtype)
    terms = [wide(kept[...])] + [wide(message[nodes:]) for message in messages]
    mine, other = tree(terms[::2]) * scale, tree(terms[1::2]) * scale
    odd = odd_row()
    weight_out[:, :half] = jnp.where(odd, other, mine)
    weight_out[:, half:] = jnp.where(odd, mine, other)


def per_device(features, weight, cotangent, tile_values, tile_rows, tile_cols, tile_count):
    slots, side = tile_values.shape[2:4]
    n_row, n_col = lax.axis_size("row"), lax.axis_size("col")
    nodes, width = features.shape
    hidden = weight.shape[1]
    down, across = n_col * nodes, n_row * nodes
    dense_bytes = 2 * down * across

    paired = n_col == 4
    gathered = [swap(features, "row", d) for d in start_order(n_row)]
    (blank,) = call(zero_kernel, [((down, across), NARROW)], [], need=dense_bytes)()
    (near,) = call(
        functools.partial(dense_kernel, nodes // side, paired),
        [((down, across), NARROW)],
        [VMEM] * 5,
        scratch=[
            pltpu.SMEM(tile_rows.shape, jnp.int32),
            pltpu.SMEM(tile_cols.shape, jnp.int32),
            pltpu.SMEM(tile_count.shape, jnp.int32),
            pltpu.SemaphoreType.DMA((3,)),
        ],
        need=2 * dense_bytes,
    )(blank, tile_values, tile_rows, tile_cols, tile_count)

    forward = dict(flops=2 * down * across * width, need=2 * dense_bytes)
    if paired:
        layers = 2
        own, *sends = call(
            functools.partial(paired_forward_kernel, n_row),
            [((2 * nodes, width), NARROW)] * 4,
            [VMEM] * (1 + n_row),
            **forward,
        )(near, features, *gathered)
        layer_call, cotangents = paired_layer_kernel, [cotangent, swap(cotangent, "col", 2)]
    else:
        layers = 1
        own, *sends = call(
            functools.partial(forward_kernel, n_row),
            [((nodes, width), jnp.float32)] + [((nodes, width), NARROW)] * (n_col - 1),
            [VMEM] * (1 + n_row),
            **forward,
        )(near, features, *gathered)
        layer_call, cotangents = layer_kernel, [cotangent]
    parts = exchange(sends, "col", True)
    (far,) = call(
        functools.partial(turn_kernel, side),
        [((across, down), NARROW)],
        [VMEM],
        need=3 * dense_bytes,
    )(near)

    half = hidden // 2
    square = (width, half)
    message = ((layers * nodes + width, width), NARROW)
    sent, other, pre = call(
        layer_call,
        [message, (square, NARROW), ((nodes, hidden), jnp.float32)],
        [VMEM] * (n_col + 1 + len(cotangents)),
        flops=14 * layers * nodes * width * hidden,
        after=[far],
    )(own, *parts, weight, *cotangents)
    if paired:
        corner = [
            (r * n_col + c, (r ^ 1) * n_col + (c ^ 1)) for r in range(n_row) for c in range(n_col)
        ]
        messages = [sent, swap(sent, "col", 1)]
        others = [swap(other, "row", 1), lax.ppermute(other, ("row", "col"), corner)]
    else:
        (sent,) = call(message_kernel, [message], [VMEM] * 2)(sent, swap(other, "row", 1))
        messages = [sent] + exchange([sent] * (n_col - 1), "col", False)
        others = []
    (act,) = call(act_kernel, [((nodes, hidden), NARROW)], [VMEM])(pre)

    message = ((nodes + width, width), NARROW)
    (begun,) = call(
        functools.partial(begin_kernel, layers * nodes),
        [((across, width), jnp.float32)],
        [VMEM] * 2,
        **forward,
    )(far, sent)
    message = ((nodes + width, width), NARROW)
    own, kept, *sends = call(
        functools.partial(backward_kernel, len(messages), len(others)),
        [((nodes, width), jnp.float32), (square, NARROW)] + [message] * (n_row - 1),
        [VMEM] * (2 + len(messages) + len(others)),
        scratch=[pltpu.VMEM((across, width), jnp.float32)],
        **forward,
    )(far, begun, *messages, *others)
    parts = exchange(sends, "row", True)

    scale = float(nodes * n_row * n_col) ** -0.5
    grad_features, grad_weight = call(
        functools.partial(last_kernel, scale),
        [((nodes, width), NARROW), ((width, hidden), jnp.float32)],
        [VMEM] * (n_row + 1),
    )(own, kept, parts[1], parts[0], *parts[2:])
    return act, grad_features, grad_weight


def solution(mesh):
    placed = (
        P(("groups", "row", "col"), None),
        P(),
        P(("groups", "row", "col"), None),
        P(("groups", "row"), "col", None, None, None),
        P(("groups", "row"), "col", None),
        P(("groups", "row"), "col", None),
        P(("groups", "row"), "col"),
    )
    return jax.shard_map(
        per_device,
        mesh=mesh,
        in_specs=placed,
        out_specs=(
            P(("groups", "row", "col"), None),
            P(("groups", "row", "col"), None),
            P("groups", None),
        ),
        check_vma=False,
    )
```

```python
import functools

import jax
import jax.numpy as jnp
from jax import lax
from jax.experimental import pallas as pl
from jax.experimental.pallas import tpu as pltpu
from jax.sharding import PartitionSpec as P

VMEM = pl.BlockSpec(memory_space=pltpu.VMEM)
ANY = pl.BlockSpec(memory_space=pl.ANY)
LEAST = 16 * 1024 * 1024
NARROW = jnp.bfloat16


def call(kernel, outs, in_specs, scratch=(), flops=0, need=0, after=()):
    outs = tuple(jax.ShapeDtypeStruct(shape, dtype) for shape, dtype in outs)
    late = len(after)
    run = pl.pallas_call(
        (lambda *refs: kernel(*refs[late:])) if late else kernel,
        out_shape=outs,
        in_specs=[ANY] * late + list(in_specs),
        out_specs=(VMEM,) * len(outs),
        scratch_shapes=scratch,
        compiler_params=pltpu.CompilerParams(vmem_limit_bytes=LEAST + need),
        cost_estimate=pl.CostEstimate(flops=flops, bytes_accessed=need, transcendentals=0),
    )
    return functools.partial(run, *after)


def ring_place(k, axis):
    return k ^ (k >> 1) if axis == "col" and lax.axis_size(axis) == 4 else k


def exchange(sends, axis, ahead):
    n = lax.axis_size(axis)

    def target(s, d):
        return ring_place((ring_place(s, axis) + (d if ahead else -d)) % n, axis)

    return [
        lax.ppermute(send, axis, [(s, target(s, d)) for s in range(n)])
        for d, send in enumerate(sends, 1)
    ]


def odd_row():
    return lax.rem(lax.axis_index("row"), 2) == 1


def start_order(n):
    return [*range(2, n), 1]


def swap(value, axis, distance):
    n = lax.axis_size(axis)
    return lax.ppermute(value, axis, [(s, s ^ distance) for s in range(n)])


def wide(value):
    return value.astype(jnp.float32)


def split(value):
    high = value.astype(NARROW)
    return high, (value - wide(high)).astype(NARROW)


def dot(left, right, dims=((1,), (0,))):
    return lax.dot_general(left, right, (dims, ((), ())), preferred_element_type=jnp.float32)


def zero_kernel(out):
    out[...] = jnp.zeros_like(out)


def dense_kernel(piece, paired, blank, vals, rows_in, cols_in, count_in, near, rows, cols, count, sems):
    copies = [
        pltpu.make_async_copy(source, target, sems.at[k])
        for k, (source, target) in enumerate(((rows_in, rows), (cols_in, cols), (count_in, count)))
    ]
    for copy in copies:
        copy.start()
    side = vals.shape[-1]
    near[...] = blank[...]
    for copy in copies:
        copy.wait()

    def ahead(there):
        n, here = lax.axis_size("col"), lax.axis_index("col")
        return lax.rem(ring_place(there, "col") - ring_place(here, "col") + n, n)

    def add(t, _):
        row, col = rows[0, 0, t], cols[0, 0, t]
        if paired:
            place = lax.rem((row // piece) ^ lax.axis_index("col"), 2) * 2 + row // piece // 2
        else:
            place = ahead(row // piece)
        row = place * piece + lax.rem(row, piece)
        col = ((col // piece) ^ lax.axis_index("row")) * piece + lax.rem(col, piece)
        down = pl.ds(pl.multiple_of(row * side, side), side)
        across = pl.ds(pl.multiple_of(col * side, side), side)
        near[down, across] = vals[0, 0, t]
        return 0

    lax.fori_loop(0, count[0, 0], add, 0)


def turn_kernel(step, near, far):
    def turn(k, _):
        band = pl.ds(pl.multiple_of(k * step, step), step)
        far[:, band] = near[band, :].T
        return 0

    lax.fori_loop(0, near.shape[0] // step, turn, 0)


def tree(terms):
    while len(terms) > 1:
        middle = len(terms) // 2
        terms = [left + right for left, right in zip(terms[:middle], terms[middle:])]
    return terms[0]


def stack(operands):
    own, *others = [operand[...] for operand in operands]
    order = start_order(len(operands))
    return jnp.concatenate([own] + [others[order.index(d)] for d in range(1, len(operands))], axis=0)


def forward_kernel(n, matrix, *refs):
    operands, own, sends = refs[:n], refs[n], refs[n + 1 :]
    rows = own.shape[0]
    product = dot(matrix[...], stack(operands))
    own[...] = product[:rows]
    for d, send in enumerate(sends, 1):
        send[...] = product[d * rows : (d + 1) * rows].astype(send.dtype)


def layer(total, weight, cotangent):
    nodes = total.shape[0]
    high, low = split(total)
    pre = dot(jnp.concatenate([high, low], axis=0), weight)
    pre = pre[:nodes] + pre[nodes:]
    sigma = jax.nn.sigmoid(pre)
    grad = wide(cotangent) * sigma * (1.0 + pre * (1.0 - sigma))
    grad_high, grad_low = split(grad)
    across, down = ((1,), (1,)), ((0,), (0,))
    back = dot(jnp.concatenate([grad_high, grad_low], axis=0), weight, across)
    back = back[:nodes] + back[nodes:]
    left = jnp.concatenate([high, low, high], axis=0)
    term = dot(left, jnp.concatenate([grad_high, grad_high, grad_low], axis=0), down)
    return pre, back, term


def store_layer(back, term, message, other):
    nodes, half = back.shape[0], other.shape[1]
    odd = odd_row()
    left, right = term[:, :half], term[:, half:]
    message[:nodes] = back.astype(message.dtype)
    message[nodes:] = jnp.where(odd, right, left).astype(message.dtype)
    other[...] = jnp.where(odd, left, right).astype(other.dtype)


def layer_kernel(*refs):
    *parts, weight, cotangent, message, other, pre_out = refs
    total = tree([wide(part[...]) for part in parts])
    pre, back, term = layer(total, weight[...], cotangent[...])
    pre_out[...] = pre
    store_layer(back, term, message, other)


def paired_forward_kernel(n, matrix, *refs):
    operands, (own, first, third, second) = refs[:n], refs[n:]
    product = dot(matrix[...], stack(operands)).astype(own.dtype)
    rows = own.shape[0]
    for target in (own, second):
        target[...] = product[:rows]
    for target in (first, third):
        target[...] = product[rows:]


def paired_layer_kernel(own, first, third, second, weight, cotangent, beyond, *refs):
    message, other, pre_out = refs
    nodes = cotangent.shape[0]
    total = (wide(own[...]) + wide(second[...])) + (wide(first[...]) + wide(third[...]))
    high_col = lax.axis_index("col") >= 2
    here, there = cotangent[...], beyond[...]
    both = jnp.concatenate(
        [jnp.where(high_col, there, here), jnp.where(high_col, here, there)], axis=0
    )
    pre, back, term = layer(total, weight[...], both)
    pre_out[...] = jnp.where(high_col, pre[nodes:], pre[:nodes])
    store_layer(back, term, message, other)


def message_kernel(sent, came, message):
    nodes = sent.shape[0] - came.shape[0]
    message[:nodes] = sent[:nodes]
    message[nodes:] = (wide(sent[nodes:]) + wide(came[...])).astype(message.dtype)


def act_kernel(pre, act):
    act[...] = (pre[...] * jax.nn.sigmoid(pre[...])).astype(act.dtype)


def begin_kernel(backs, matrix, message, product):
    product[...] = dot(matrix[:, :backs], message[:backs])


def backward_kernel(n, n_others, matrix, begun, *refs):
    messages, others, refs = refs[:n], refs[n : n + n_others], refs[n + n_others :]
    own, kept, *sends, product = refs
    rows = own.shape[0]
    backs = messages[0].shape[0] - kept.shape[0]
    stacked = jnp.concatenate([message[:backs] for message in messages[1:]], axis=0)
    product[...] = begun[...] + dot(matrix[:, backs:], stacked)
    own[...] = product[:rows]
    term = tree([wide(message[backs:]) for message in messages])
    if others:
        term = term + tree([wide(other[...]) for other in others])
    term = term.astype(kept.dtype)
    kept[...] = term
    here, size = lax.axis_index("row"), lax.axis_size("row")
    for d, send in enumerate(sends, 1):
        start = pl.multiple_of((lax.rem(here + d, size) ^ here) * rows, rows)
        send[:rows] = product[pl.ds(start, rows)].astype(send.dtype)
        send[rows:] = term


def last_kernel(scale, own, kept, *refs):
    *messages, features_out, weight_out = refs
    nodes, half = own.shape[0], kept.shape[1]
    features_out[...] = tree(
        [own[...]] + [wide(message[:nodes]) for message in messages]
    ).astype(features_out.dtype)
    terms = [wide(kept[...])] + [wide(message[nodes:]) for message in messages]
    mine, other = tree(terms[::2]) * scale, tree(terms[1::2]) * scale
    odd = odd_row()
    weight_out[:, :half] = jnp.where(odd, other, mine)
    weight_out[:, half:] = jnp.where(odd, mine, other)


def per_device(features, weight, cotangent, tile_values, tile_rows, tile_cols, tile_count):
    slots, side = tile_values.shape[2:4]
    n_row, n_col = lax.axis_size("row"), lax.axis_size("col")
    nodes, width = features.shape
    hidden = weight.shape[1]
    down, across = n_col * nodes, n_row * nodes
    dense_bytes = 2 * down * across

    paired = n_col == 4
    gathered = [swap(features, "row", d) for d in start_order(n_row)]
    (blank,) = call(zero_kernel, [((down, across), NARROW)], [], need=dense_bytes)()
    (near,) = call(
        functools.partial(dense_kernel, nodes // side, paired),
        [((down, across), NARROW)],
        [VMEM] * 5,
        scratch=[
            pltpu.SMEM(tile_rows.shape, jnp.int32),
            pltpu.SMEM(tile_cols.shape, jnp.int32),
            pltpu.SMEM(tile_count.shape, jnp.int32),
            pltpu.SemaphoreType.DMA((3,)),
        ],
        need=2 * dense_bytes,
    )(blank, tile_values, tile_rows, tile_cols, tile_count)

    forward = dict(flops=2 * down * across * width, need=2 * dense_bytes)
    if paired:
        layers = 2
        own, *sends = call(
            functools.partial(paired_forward_kernel, n_row),
            [((2 * nodes, width), NARROW)] * 4,
            [VMEM] * (1 + n_row),
            **forward,
        )(near, features, *gathered)
        parts = [swap(send, "col", d) for d, send in zip((1, 3, 2), sends)]
        layer_call, cotangents = paired_layer_kernel, [cotangent, swap(cotangent, "col", 2)]
    else:
        layers = 1
        own, *sends = call(
            functools.partial(forward_kernel, n_row),
            [((nodes, width), jnp.float32)] + [((nodes, width), NARROW)] * (n_col - 1),
            [VMEM] * (1 + n_row),
            **forward,
        )(near, features, *gathered)
        layer_call, cotangents = layer_kernel, [cotangent]
        parts = exchange(sends, "col", True)
    (far,) = call(
        functools.partial(turn_kernel, side),
        [((across, down), NARROW)],
        [VMEM],
        need=3 * dense_bytes,
    )(near)

    half = hidden // 2
    square = (width, half)
    message = ((layers * nodes + width, width), NARROW)
    sent, other, pre = call(
        layer_call,
        [message, (square, NARROW), ((nodes, hidden), jnp.float32)],
        [VMEM] * (n_col + 1 + len(cotangents)),
        flops=14 * layers * nodes * width * hidden,
        after=[far],
    )(own, *parts, weight, *cotangents)
    if paired:
        corner = [
            (r * n_col + c, (r ^ 1) * n_col + (c ^ 1)) for r in range(n_row) for c in range(n_col)
        ]
        messages = [sent, swap(sent, "col", 1)]
        others = [swap(other, "row", 1), lax.ppermute(other, ("row", "col"), corner)]
    else:
        (sent,) = call(message_kernel, [message], [VMEM] * 2)(sent, swap(other, "row", 1))
        messages = [sent] + exchange([sent] * (n_col - 1), "col", False)
        others = []
    (act,) = call(act_kernel, [((nodes, hidden), NARROW)], [VMEM])(pre)

    message = ((nodes + width, width), NARROW)
    (begun,) = call(
        functools.partial(begin_kernel, layers * nodes),
        [((across, width), jnp.float32)],
        [VMEM] * 2,
        **forward,
    )(far, sent)
    message = ((nodes + width, width), NARROW)
    own, kept, *sends = call(
        functools.partial(backward_kernel, len(messages), len(others)),
        [((nodes, width), jnp.float32), (square, NARROW)] + [message] * (n_row - 1),
        [VMEM] * (2 + len(messages) + len(others)),
        scratch=[pltpu.VMEM((across, width), jnp.float32)],
        **forward,
    )(far, begun, *messages, *others)
    parts = exchange(sends, "row", True)

    scale = float(nodes * n_row * n_col) ** -0.5
    grad_features, grad_weight = call(
        functools.partial(last_kernel, scale),
        [((nodes, width), NARROW), ((width, hidden), jnp.float32)],
        [VMEM] * (n_row + 1),
    )(own, kept, *parts)
    return act, grad_features, grad_weight


def solution(mesh):
    placed = (
        P(("groups", "row", "col"), None),
        P(),
        P(("groups", "row", "col"), None),
        P(("groups", "row"), "col", None, None, None),
        P(("groups", "row"), "col", None),
        P(("groups", "row"), "col", None),
        P(("groups", "row"), "col"),
    )
    return jax.shard_map(
        per_device,
        mesh=mesh,
        in_specs=placed,
        out_specs=(
            P(("groups", "row", "col"), None),
            P(("groups", "row", "col"), None),
            P("groups", None),
        ),
        check_vma=False,
    )
```

```python
import functools

import jax
import jax.numpy as jnp
from jax import lax
from jax.experimental import pallas as pl
from jax.experimental.pallas import tpu as pltpu
from jax.sharding import PartitionSpec as P

VMEM = pl.BlockSpec(memory_space=pltpu.VMEM)
ANY = pl.BlockSpec(memory_space=pl.ANY)
LEAST = 16 * 1024 * 1024
NARROW = jnp.bfloat16


def call(kernel, outs, in_specs, scratch=(), flops=0, need=0, after=()):
    outs = tuple(jax.ShapeDtypeStruct(shape, dtype) for shape, dtype in outs)
    late = len(after)
    run = pl.pallas_call(
        (lambda *refs: kernel(*refs[late:])) if late else kernel,
        out_shape=outs,
        in_specs=[ANY] * late + list(in_specs),
        out_specs=(VMEM,) * len(outs),
        scratch_shapes=scratch,
        compiler_params=pltpu.CompilerParams(vmem_limit_bytes=LEAST + need),
        cost_estimate=pl.CostEstimate(flops=flops, bytes_accessed=need, transcendentals=0),
    )
    return functools.partial(run, *after)


def ring_place(k, axis):
    return k ^ (k >> 1) if axis == "col" and lax.axis_size(axis) == 4 else k


def exchange(sends, axis, ahead):
    n = lax.axis_size(axis)

    def target(s, d):
        return ring_place((ring_place(s, axis) + (d if ahead else -d)) % n, axis)

    return [
        lax.ppermute(send, axis, [(s, target(s, d)) for s in range(n)])
        for d, send in enumerate(sends, 1)
    ]


def odd_row():
    return lax.rem(lax.axis_index("row"), 2) == 1


def start_order(n):
    return [*range(2, n), 1]


def swap(value, axis, distance):
    n = lax.axis_size(axis)
    return lax.ppermute(value, axis, [(s, s ^ distance) for s in range(n)])


def wide(value):
    return value.astype(jnp.float32)


def split(value):
    high = value.astype(NARROW)
    return high, (value - wide(high)).astype(NARROW)


def dot(left, right, dims=((1,), (0,))):
    return lax.dot_general(left, right, (dims, ((), ())), preferred_element_type=jnp.float32)


def zero_kernel(out):
    out[...] = jnp.zeros_like(out)


def dense_kernel(piece, paired, blank, vals, rows_in, cols_in, count_in, near, rows, cols, count, sems):
    copies = [
        pltpu.make_async_copy(source, target, sems.at[k])
        for k, (source, target) in enumerate(((rows_in, rows), (cols_in, cols), (count_in, count)))
    ]
    for copy in copies:
        copy.start()
    side = vals.shape[-1]
    near[...] = blank[...]
    for copy in copies:
        copy.wait()

    def ahead(there):
        n, here = lax.axis_size("col"), lax.axis_index("col")
        return lax.rem(ring_place(there, "col") - ring_place(here, "col") + n, n)

    def add(t, _):
        row, col = rows[0, 0, t], cols[0, 0, t]
        if paired:
            place = lax.rem((row // piece) ^ lax.axis_index("col"), 2) * 2 + row // piece // 2
        else:
            place = ahead(row // piece)
        row = place * piece + lax.rem(row, piece)
        col = ((col // piece) ^ lax.axis_index("row")) * piece + lax.rem(col, piece)
        down = pl.ds(pl.multiple_of(row * side, side), side)
        across = pl.ds(pl.multiple_of(col * side, side), side)
        near[down, across] = vals[0, 0, t]
        return 0

    lax.fori_loop(0, count[0, 0], add, 0)


def turn_kernel(step, near, far):
    def turn(k, _):
        band = pl.ds(pl.multiple_of(k * step, step), step)
        far[:, band] = near[band, :].T
        return 0

    lax.fori_loop(0, near.shape[0] // step, turn, 0)


def tree(terms):
    while len(terms) > 1:
        middle = len(terms) // 2
        terms = [left + right for left, right in zip(terms[:middle], terms[middle:])]
    return terms[0]


def stack(operands):
    own, *others = [operand[...] for operand in operands]
    order = start_order(len(operands))
    return jnp.concatenate([own] + [others[order.index(d)] for d in range(1, len(operands))], axis=0)


def forward_kernel(n, matrix, *refs):
    operands, own, sends = refs[:n], refs[n], refs[n + 1 :]
    rows = own.shape[0]
    product = dot(matrix[...], stack(operands))
    own[...] = product[:rows]
    for d, send in enumerate(sends, 1):
        send[...] = product[d * rows : (d + 1) * rows].astype(send.dtype)


def layer(total, weight, cotangent):
    nodes = total.shape[0]
    high, low = split(total)
    pre = dot(jnp.concatenate([high, low], axis=0), weight)
    pre = pre[:nodes] + pre[nodes:]
    sigma = jax.nn.sigmoid(pre)
    grad = wide(cotangent) * sigma * (1.0 + pre * (1.0 - sigma))
    grad_high, grad_low = split(grad)
    across, down = ((1,), (1,)), ((0,), (0,))
    back = dot(jnp.concatenate([grad_high, grad_low], axis=0), weight, across)
    back = back[:nodes] + back[nodes:]
    left = jnp.concatenate([high, low, high], axis=0)
    term = dot(left, jnp.concatenate([grad_high, grad_high, grad_low], axis=0), down)
    return pre, back, term


def store_layer(back, term, message, other):
    nodes, half = back.shape[0], other.shape[1]
    odd = odd_row()
    left, right = term[:, :half], term[:, half:]
    message[:nodes] = back.astype(message.dtype)
    message[nodes:] = jnp.where(odd, right, left).astype(message.dtype)
    other[...] = jnp.where(odd, left, right).astype(other.dtype)


def layer_kernel(*refs):
    *parts, weight, cotangent, message, other, pre_out = refs
    total = tree([wide(part[...]) for part in parts])
    pre, back, term = layer(total, weight[...], cotangent[...])
    pre_out[...] = pre
    store_layer(back, term, message, other)


def in_middle():
    my_col = lax.axis_index("col")
    return (my_col == 1) | (my_col == 2)


def paired_forward_kernel(n, matrix, *refs):
    operands, (own, first, second, third) = refs[:n], refs[n:]
    product = dot(matrix[...], stack(operands)).astype(own.dtype)
    rows = own.shape[0]
    same, other = product[:rows], product[rows:]
    middle = in_middle()
    own[...] = same
    first[...] = jnp.where(middle, same, other)
    second[...] = other
    third[...] = jnp.where(middle, other, same)


def paired_layer_kernel(own, first, second, third, weight, cotangent, beyond, *refs):
    message, other, pre_out = refs
    nodes = cotangent.shape[0]
    middle = in_middle()
    partner = jnp.where(middle, third[...], first[...])
    side = jnp.where(middle, first[...], third[...])
    total = (wide(own[...]) + wide(partner)) + (wide(second[...]) + wide(side))
    high_col = lax.axis_index("col") >= 2
    here, there = cotangent[...], beyond[...]
    both = jnp.concatenate(
        [jnp.where(high_col, there, here), jnp.where(high_col, here, there)], axis=0
    )
    pre, back, term = layer(total, weight[...], both)
    pre_out[...] = jnp.where(high_col, pre[nodes:], pre[:nodes])
    store_layer(back, term, message, other)


def message_kernel(sent, came, message):
    nodes = sent.shape[0] - came.shape[0]
    message[:nodes] = sent[:nodes]
    message[nodes:] = (wide(sent[nodes:]) + wide(came[...])).astype(message.dtype)


def act_kernel(pre, act):
    act[...] = (pre[...] * jax.nn.sigmoid(pre[...])).astype(act.dtype)


def begin_kernel(backs, matrix, message, product):
    product[...] = dot(matrix[:, :backs], message[:backs])


def backward_kernel(n, n_others, matrix, begun, *refs):
    messages, others, refs = refs[:n], refs[n : n + n_others], refs[n + n_others :]
    own, kept, *sends, product = refs
    rows = own.shape[0]
    backs = messages[0].shape[0] - kept.shape[0]
    stacked = jnp.concatenate([message[:backs] for message in messages[1:]], axis=0)
    product[...] = begun[...] + dot(matrix[:, backs:], stacked)
    own[...] = product[:rows]
    term = tree([wide(message[backs:]) for message in messages])
    if others:
        term = term + tree([wide(other[...]) for other in others])
    term = term.astype(kept.dtype)
    kept[...] = term
    here, size = lax.axis_index("row"), lax.axis_size("row")
    for d, send in enumerate(sends, 1):
        start = pl.multiple_of((lax.rem(here + d, size) ^ here) * rows, rows)
        send[:rows] = product[pl.ds(start, rows)].astype(send.dtype)
        send[rows:] = term


def last_kernel(scale, own, kept, *refs):
    *messages, features_out, weight_out = refs
    nodes, half = own.shape[0], kept.shape[1]
    features_out[...] = tree(
        [own[...]] + [wide(message[:nodes]) for message in messages]
    ).astype(features_out.dtype)
    terms = [wide(kept[...])] + [wide(message[nodes:]) for message in messages]
    mine, other = tree(terms[::2]) * scale, tree(terms[1::2]) * scale
    odd = odd_row()
    weight_out[:, :half] = jnp.where(odd, other, mine)
    weight_out[:, half:] = jnp.where(odd, mine, other)


def per_device(features, weight, cotangent, tile_values, tile_rows, tile_cols, tile_count):
    slots, side = tile_values.shape[2:4]
    n_row, n_col = lax.axis_size("row"), lax.axis_size("col")
    nodes, width = features.shape
    hidden = weight.shape[1]
    down, across = n_col * nodes, n_row * nodes
    dense_bytes = 2 * down * across

    paired = n_col == 4
    gathered = [swap(features, "row", d) for d in start_order(n_row)]
    (blank,) = call(zero_kernel, [((down, across), NARROW)], [], need=dense_bytes)()
    (near,) = call(
        functools.partial(dense_kernel, nodes // side, paired),
        [((down, across), NARROW)],
        [VMEM] * 5,
        scratch=[
            pltpu.SMEM(tile_rows.shape, jnp.int32),
            pltpu.SMEM(tile_cols.shape, jnp.int32),
            pltpu.SMEM(tile_count.shape, jnp.int32),
            pltpu.SemaphoreType.DMA((3,)),
        ],
        need=2 * dense_bytes,
    )(blank, tile_values, tile_rows, tile_cols, tile_count)

    forward = dict(flops=2 * down * across * width, need=2 * dense_bytes)
    if paired:
        layers = 2
        own, *sends = call(
            functools.partial(paired_forward_kernel, n_row),
            [((2 * nodes, width), NARROW)] * 4,
            [VMEM] * (1 + n_row),
            **forward,
        )(near, features, *gathered)
        layer_call, cotangents = paired_layer_kernel, [cotangent, swap(cotangent, "col", 2)]
    else:
        layers = 1
        own, *sends = call(
            functools.partial(forward_kernel, n_row),
            [((nodes, width), jnp.float32)] + [((nodes, width), NARROW)] * (n_col - 1),
            [VMEM] * (1 + n_row),
            **forward,
        )(near, features, *gathered)
        layer_call, cotangents = layer_kernel, [cotangent]
    parts = exchange(sends, "col", True)
    (far,) = call(
        functools.partial(turn_kernel, side),
        [((across, down), NARROW)],
        [VMEM],
        need=3 * dense_bytes,
    )(near)

    half = hidden // 2
    square = (width, half)
    message = ((layers * nodes + width, width), NARROW)
    sent, other, pre = call(
        layer_call,
        [message, (square, NARROW), ((nodes, hidden), jnp.float32)],
        [VMEM] * (n_col + 1 + len(cotangents)),
        flops=14 * layers * nodes * width * hidden,
        after=[far],
    )(own, *parts, weight, *cotangents)
    if paired:
        corner = [
            (r * n_col + c, (r ^ 1) * n_col + (c ^ 1)) for r in range(n_row) for c in range(n_col)
        ]
        messages = [sent, swap(sent, "col", 1)]
        others = [lax.ppermute(other, ("row", "col"), corner), swap(other, "row", 1)]
    else:
        (sent,) = call(message_kernel, [message], [VMEM] * 2)(sent, swap(other, "row", 1))
        messages = [sent] + exchange([sent] * (n_col - 1), "col", False)
        others = []
    (act,) = call(act_kernel, [((nodes, hidden), NARROW)], [VMEM])(pre)

    message = ((nodes + width, width), NARROW)
    (begun,) = call(
        functools.partial(begin_kernel, layers * nodes),
        [((across, width), jnp.float32)],
        [VMEM] * 2,
        **forward,
    )(far, sent)
    message = ((nodes + width, width), NARROW)
    own, kept, *sends = call(
        functools.partial(backward_kernel, len(messages), len(others)),
        [((nodes, width), jnp.float32), (square, NARROW)] + [message] * (n_row - 1),
        [VMEM] * (2 + len(messages) + len(others)),
        scratch=[pltpu.VMEM((across, width), jnp.float32)],
        **forward,
    )(far, begun, *messages, *others)
    parts = exchange(sends, "row", True)

    scale = float(nodes * n_row * n_col) ** -0.5
    grad_features, grad_weight = call(
        functools.partial(last_kernel, scale),
        [((nodes, width), NARROW), ((width, hidden), jnp.float32)],
        [VMEM] * (n_row + 1),
    )(own, kept, *parts)
    return act, grad_features, grad_weight


def solution(mesh):
    placed = (
        P(("groups", "row", "col"), None),
        P(),
        P(("groups", "row", "col"), None),
        P(("groups", "row"), "col", None, None, None),
        P(("groups", "row"), "col", None),
        P(("groups", "row"), "col", None),
        P(("groups", "row"), "col"),
    )
    return jax.shard_map(
        per_device,
        mesh=mesh,
        in_specs=placed,
        out_specs=(
            P(("groups", "row", "col"), None),
            P(("groups", "row", "col"), None),
            P("groups", None),
        ),
        check_vma=False,
    )
```

```python
import functools

import jax
import jax.numpy as jnp
from jax import lax
from jax.experimental import pallas as pl
from jax.experimental.pallas import tpu as pltpu
from jax.sharding import PartitionSpec as P

VMEM = pl.BlockSpec(memory_space=pltpu.VMEM)
ANY = pl.BlockSpec(memory_space=pl.ANY)
LEAST = 16 * 1024 * 1024
NARROW = jnp.bfloat16


def call(kernel, outs, in_specs, scratch=(), flops=0, need=0, after=()):
    outs = tuple(jax.ShapeDtypeStruct(shape, dtype) for shape, dtype in outs)
    late = len(after)
    run = pl.pallas_call(
        (lambda *refs: kernel(*refs[late:])) if late else kernel,
        out_shape=outs,
        in_specs=[ANY] * late + list(in_specs),
        out_specs=(VMEM,) * len(outs),
        scratch_shapes=scratch,
        compiler_params=pltpu.CompilerParams(vmem_limit_bytes=LEAST + need),
        cost_estimate=pl.CostEstimate(flops=flops, bytes_accessed=need, transcendentals=0),
    )
    return functools.partial(run, *after)


def ring_place(k, axis):
    return k ^ (k >> 1) if axis == "col" and lax.axis_size(axis) == 4 else k


def exchange(sends, axis, ahead):
    n = lax.axis_size(axis)

    def target(s, d):
        return ring_place((ring_place(s, axis) + (d if ahead else -d)) % n, axis)

    return [
        lax.ppermute(send, axis, [(s, target(s, d)) for s in range(n)])
        for d, send in enumerate(sends, 1)
    ]


def odd_row():
    return lax.rem(lax.axis_index("row"), 2) == 1


def start_order(n):
    return [*range(n - 1, 0, -1)]


def swap(value, axis, distance):
    n = lax.axis_size(axis)
    return lax.ppermute(value, axis, [(s, s ^ distance) for s in range(n)])


def wide(value):
    return value.astype(jnp.float32)


def split(value):
    high = value.astype(NARROW)
    return high, (value - wide(high)).astype(NARROW)


def dot(left, right, dims=((1,), (0,))):
    return lax.dot_general(left, right, (dims, ((), ())), preferred_element_type=jnp.float32)


def zero_kernel(out):
    out[...] = jnp.zeros_like(out)


def dense_kernel(piece, paired, blank, vals, rows_in, cols_in, count_in, near, rows, cols, count, sems):
    copies = [
        pltpu.make_async_copy(source, target, sems.at[k])
        for k, (source, target) in enumerate(((rows_in, rows), (cols_in, cols), (count_in, count)))
    ]
    for copy in copies:
        copy.start()
    side = vals.shape[-1]
    near[...] = blank[...]
    for copy in copies:
        copy.wait()

    def ahead(there):
        n, here = lax.axis_size("col"), lax.axis_index("col")
        return lax.rem(ring_place(there, "col") - ring_place(here, "col") + n, n)

    def add(t, _):
        row, col = rows[0, 0, t], cols[0, 0, t]
        if paired:
            place = lax.rem((row // piece) ^ lax.axis_index("col"), 2) * 2 + row // piece // 2
        else:
            place = ahead(row // piece)
        row = place * piece + lax.rem(row, piece)
        col = ((col // piece) ^ lax.axis_index("row")) * piece + lax.rem(col, piece)
        down = pl.ds(pl.multiple_of(row * side, side), side)
        across = pl.ds(pl.multiple_of(col * side, side), side)
        near[down, across] = vals[0, 0, t]
        return 0

    lax.fori_loop(0, count[0, 0], add, 0)


def turn_kernel(step, near, far):
    def turn(k, _):
        band = pl.ds(pl.multiple_of(k * step, step), step)
        far[:, band] = near[band, :].T
        return 0

    lax.fori_loop(0, near.shape[0] // step, turn, 0)


def tree(terms):
    while len(terms) > 1:
        middle = len(terms) // 2
        terms = [left + right for left, right in zip(terms[:middle], terms[middle:])]
    return terms[0]


def stack(operands):
    own, *others = [operand[...] for operand in operands]
    order = start_order(len(operands))
    return jnp.concatenate([own] + [others[order.index(d)] for d in range(1, len(operands))], axis=0)


def forward_kernel(n, matrix, *refs):
    operands, own, sends = refs[:n], refs[n], refs[n + 1 :]
    rows = own.shape[0]
    product = dot(matrix[...], stack(operands))
    own[...] = product[:rows]
    for d, send in enumerate(sends, 1):
        send[...] = product[d * rows : (d + 1) * rows].astype(send.dtype)


def layer(total, weight, cotangent):
    nodes = total.shape[0]
    high, low = split(total)
    pre = dot(jnp.concatenate([high, low], axis=0), weight)
    pre = pre[:nodes] + pre[nodes:]
    sigma = jax.nn.sigmoid(pre)
    grad = wide(cotangent) * sigma * (1.0 + pre * (1.0 - sigma))
    grad_high, grad_low = split(grad)
    across, down = ((1,), (1,)), ((0,), (0,))
    back = dot(jnp.concatenate([grad_high, grad_low], axis=0), weight, across)
    back = back[:nodes] + back[nodes:]
    left = jnp.concatenate([high, low, high], axis=0)
    term = dot(left, jnp.concatenate([grad_high, grad_high, grad_low], axis=0), down)
    return pre, back, term


def store_layer(back, term, message, other):
    nodes, half = back.shape[0], other.shape[1]
    odd = odd_row()
    left, right = term[:, :half], term[:, half:]
    message[:nodes] = back.astype(message.dtype)
    message[nodes:] = jnp.where(odd, right, left).astype(message.dtype)
    other[...] = jnp.where(odd, left, right).astype(other.dtype)


def layer_kernel(*refs):
    *parts, weight, cotangent, message, other, pre_out = refs
    total = tree([wide(part[...]) for part in parts])
    pre, back, term = layer(total, weight[...], cotangent[...])
    pre_out[...] = pre
    store_layer(back, term, message, other)


def in_middle():
    my_col = lax.axis_index("col")
    return (my_col == 1) | (my_col == 2)


def paired_forward_kernel(n, matrix, *refs):
    operands, (own, first, second, third) = refs[:n], refs[n:]
    product = dot(matrix[...], stack(operands)).astype(own.dtype)
    rows = own.shape[0]
    same, other = product[:rows], product[rows:]
    middle = in_middle()
    own[...] = same
    first[...] = jnp.where(middle, same, other)
    second[...] = other
    third[...] = jnp.where(middle, other, same)


def paired_layer_kernel(own, first, second, third, weight, cotangent, beyond, *refs):
    message, other, pre_out = refs
    nodes = cotangent.shape[0]
    middle = in_middle()
    partner = jnp.where(middle, third[...], first[...])
    side = jnp.where(middle, first[...], third[...])
    total = (wide(own[...]) + wide(partner)) + (wide(second[...]) + wide(side))
    high_col = lax.axis_index("col") >= 2
    here, there = cotangent[...], beyond[...]
    both = jnp.concatenate(
        [jnp.where(high_col, there, here), jnp.where(high_col, here, there)], axis=0
    )
    pre, back, term = layer(total, weight[...], both)
    pre_out[...] = jnp.where(high_col, pre[nodes:], pre[:nodes])
    store_layer(back, term, message, other)


def message_kernel(sent, came, message):
    nodes = sent.shape[0] - came.shape[0]
    message[:nodes] = sent[:nodes]
    message[nodes:] = (wide(sent[nodes:]) + wide(came[...])).astype(message.dtype)


def act_kernel(pre, act):
    act[...] = (pre[...] * jax.nn.sigmoid(pre[...])).astype(act.dtype)


def begin_kernel(backs, matrix, message, product):
    product[...] = dot(matrix[:, :backs], message[:backs])


def backward_kernel(n, n_others, matrix, begun, *refs):
    messages, others, refs = refs[:n], refs[n : n + n_others], refs[n + n_others :]
    own, kept, *sends, product = refs
    rows = own.shape[0]
    backs = messages[0].shape[0] - kept.shape[0]
    stacked = jnp.concatenate([message[:backs] for message in messages[1:]], axis=0)
    product[...] = begun[...] + dot(matrix[:, backs:], stacked)
    own[...] = product[:rows]
    term = tree([wide(message[backs:]) for message in messages])
    if others:
        term = term + tree([wide(other[...]) for other in others])
    term = term.astype(kept.dtype)
    kept[...] = term
    here, size = lax.axis_index("row"), lax.axis_size("row")
    for d, send in enumerate(sends, 1):
        start = pl.multiple_of((lax.rem(here + d, size) ^ here) * rows, rows)
        send[:rows] = product[pl.ds(start, rows)].astype(send.dtype)
        send[rows:] = term


def last_kernel(scale, own, kept, *refs):
    *messages, features_out, weight_out = refs
    nodes, half = own.shape[0], kept.shape[1]
    features_out[...] = tree(
        [own[...]] + [wide(message[:nodes]) for message in messages]
    ).astype(features_out.dtype)
    terms = [wide(kept[...])] + [wide(message[nodes:]) for message in messages]
    mine, other = tree(terms[::2]) * scale, tree(terms[1::2]) * scale
    odd = odd_row()
    weight_out[:, :half] = jnp.where(odd, other, mine)
    weight_out[:, half:] = jnp.where(odd, mine, other)


def per_device(features, weight, cotangent, tile_values, tile_rows, tile_cols, tile_count):
    slots, side = tile_values.shape[2:4]
    n_row, n_col = lax.axis_size("row"), lax.axis_size("col")
    nodes, width = features.shape
    hidden = weight.shape[1]
    down, across = n_col * nodes, n_row * nodes
    dense_bytes = 2 * down * across

    paired = n_col == 4
    gathered = [swap(features, "row", d) for d in start_order(n_row)]
    (blank,) = call(zero_kernel, [((down, across), NARROW)], [], need=dense_bytes)()
    (near,) = call(
        functools.partial(dense_kernel, nodes // side, paired),
        [((down, across), NARROW)],
        [VMEM] * 5,
        scratch=[
            pltpu.SMEM(tile_rows.shape, jnp.int32),
            pltpu.SMEM(tile_cols.shape, jnp.int32),
            pltpu.SMEM(tile_count.shape, jnp.int32),
            pltpu.SemaphoreType.DMA((3,)),
        ],
        need=2 * dense_bytes,
    )(blank, tile_values, tile_rows, tile_cols, tile_count)

    forward = dict(flops=2 * down * across * width, need=2 * dense_bytes)
    if paired:
        layers = 2
        own, *sends = call(
            functools.partial(paired_forward_kernel, n_row),
            [((2 * nodes, width), NARROW)] * 4,
            [VMEM] * (1 + n_row),
            **forward,
        )(near, features, *gathered)
        layer_call, cotangents = paired_layer_kernel, [cotangent, swap(cotangent, "col", 2)]
    else:
        layers = 1
        own, *sends = call(
            functools.partial(forward_kernel, n_row),
            [((nodes, width), jnp.float32)] + [((nodes, width), NARROW)] * (n_col - 1),
            [VMEM] * (1 + n_row),
            **forward,
        )(near, features, *gathered)
        layer_call, cotangents = layer_kernel, [cotangent]
    parts = exchange(sends, "col", True)
    (far,) = call(
        functools.partial(turn_kernel, side),
        [((across, down), NARROW)],
        [VMEM],
        need=3 * dense_bytes,
    )(near)

    half = hidden // 2
    square = (width, half)
    message = ((layers * nodes + width, width), NARROW)
    sent, other, pre = call(
        layer_call,
        [message, (square, NARROW), ((nodes, hidden), jnp.float32)],
        [VMEM] * (n_col + 1 + len(cotangents)),
        flops=14 * layers * nodes * width * hidden,
        after=[far],
    )(own, *parts, weight, *cotangents)
    if paired:
        corner = [
            (r * n_col + c, (r ^ 1) * n_col + (c ^ 1)) for r in range(n_row) for c in range(n_col)
        ]
        messages = [sent, swap(sent, "col", 1)]
        others = [swap(other, "row", 1), lax.ppermute(other, ("row", "col"), corner)]
    else:
        (sent,) = call(message_kernel, [message], [VMEM] * 2)(sent, swap(other, "row", 1))
        messages = [sent] + exchange([sent] * (n_col - 1), "col", False)
        others = []
    (act,) = call(act_kernel, [((nodes, hidden), NARROW)], [VMEM])(pre)

    message = ((nodes + width, width), NARROW)
    (begun,) = call(
        functools.partial(begin_kernel, layers * nodes),
        [((across, width), jnp.float32)],
        [VMEM] * 2,
        **forward,
    )(far, sent)
    message = ((nodes + width, width), NARROW)
    own, kept, *sends = call(
        functools.partial(backward_kernel, len(messages), len(others)),
        [((nodes, width), jnp.float32), (square, NARROW)] + [message] * (n_row - 1),
        [VMEM] * (2 + len(messages) + len(others)),
        scratch=[pltpu.VMEM((across, width), jnp.float32)],
        **forward,
    )(far, begun, *messages, *others)
    parts = exchange(sends, "row", True)

    scale = float(nodes * n_row * n_col) ** -0.5
    grad_features, grad_weight = call(
        functools.partial(last_kernel, scale),
        [((nodes, width), NARROW), ((width, hidden), jnp.float32)],
        [VMEM] * (n_row + 1),
    )(own, kept, *parts)
    return act, grad_features, grad_weight


def solution(mesh):
    placed = (
        P(("groups", "row", "col"), None),
        P(),
        P(("groups", "row", "col"), None),
        P(("groups", "row"), "col", None, None, None),
        P(("groups", "row"), "col", None),
        P(("groups", "row"), "col", None),
        P(("groups", "row"), "col"),
    )
    return jax.shard_map(
        per_device,
        mesh=mesh,
        in_specs=placed,
        out_specs=(
            P(("groups", "row", "col"), None),
            P(("groups", "row", "col"), None),
            P("groups", None),
        ),
        check_vma=False,
    )
```
